32 devices in a mesh: dp: 4 (over y, core), ctx: 8 (over z, x).
Axes of the slice: x: 2, y: 2, z: 4, core: 2. Of those that a mesh axis runs over, the one named last changes fastest.
Arguments:
- tokens: bfloat16 [2, 4, 1024, 896], P(None, 'dp', 'ctx'), may hold values from -6 to 6
- doc_lengths: int32 [2, 4, 6], P(None, 'dp'), may hold values from 0 to 1024, as said below
- attn_gain: float32 [896], replicated, may hold values from 0.1 to 1.9
- qkv_weight: bfloat16 [1032192], P(('dp', 'ctx')), may hold values from -0.1875 to 0.1875
- qkv_bias: float32 [1152], replicated, may hold values from -3 to 3
- out_weight: bfloat16 [802816], P(('dp', 'ctx')), may hold values from -1 to 1
- mlp_gain: float32 [896], replicated, may hold values from 0.1 to 1.9
- gate_up_weight: bfloat16 [8716288], P(('dp', 'ctx')), may hold values from -0.1875 to 0.1875
- down_weight: bfloat16 [4358144], P(('dp', 'ctx')), may hold values from -0.078125 to 0.078125
- out_grad: bfloat16 [2, 4, 1024, 896], P(None, 'dp', 'ctx'), may hold values from -6 to 6
Outputs:
- layer_out: bfloat16 [2, 4, 1024, 896], P(None, 'dp', 'ctx')
- input_grad: float32 [2, 4, 1024, 896], P(None, 'dp', 'ctx')
- attn_gain_grad: float32 [896], replicated
- qkv_weight_grad: float32 [1032192], P(('dp', 'ctx'))
- qkv_bias_grad: float32 [1152], replicated
- out_weight_grad: float32 [802816], P(('dp', 'ctx'))
- mlp_gain_grad: float32 [896], replicated
- gate_up_weight_grad: float32 [8716288], P(('dp', 'ctx'))
- down_weight_grad: float32 [4358144], P(('dp', 'ctx'))
The draws below stay inside these ranges and needn't reach their ends.
Inputs may be any that keep to these rules, and one draw needn't show every extreme that they name: `doc_lengths`: each row lists the lengths of the documents packed in order into one sequence; a row sums to 1024, and after its first zero every entry is zero. Every document but the last of its row has 200 to 2000 tokens. For each index of the second dimension, one of the 2 micro-batches holds a single document of 1024 tokens.
All inputs are finite; a program needn't handle non-finite values.
Results may differ from the reference program's by a relative error of at most 0.014.
Values may be sent and summed in bfloat16 or wider, within the bound.
No kernel may reach another device: no remote copies, remote signals or barrier semaphores. Data moves between devices by JAX's collectives and lax.ppermute only.
A program may use at most 256 MiB of HBM per device.

```python
import jax
import jax.numpy as jnp
from jax import lax

D = 896
QUERY_HEADS = 14
KEY_VALUE_HEADS = 2
HEAD_SIZE = 64
FF = 4864
QKV = 1152
MB = 2
SEQUENCE_TOKENS = 1024
SEQ_MB = 4
DOC_LO = 200
DOC_HI = 2000
NDOC = 6


def draw_doc_lengths(key, part):
    key = jax.random.fold_in(key, 17)
    first_key, second_key = jax.random.split(key)
    raw_lengths = jax.random.randint(first_key, (MB, SEQ_MB, NDOC), DOC_LO, DOC_HI + 1, dtype=jnp.int32)
    doc_ends = jnp.cumsum(raw_lengths, axis=-1, dtype=jnp.int32)
    clipped = jnp.minimum(raw_lengths, jnp.maximum(SEQUENCE_TOKENS - (doc_ends - raw_lengths), 0))
    chosen = jax.random.randint(second_key, (SEQ_MB,), 0, MB, dtype=jnp.int32)
    whole_doc = jnp.arange(MB, dtype=jnp.int32)[:, None] == chosen[None, :]
    single_row = jnp.where(jnp.arange(NDOC, dtype=jnp.int32) == 0, SEQUENCE_TOKENS, 0).astype(jnp.int32)
    return jnp.where(whole_doc[:, :, None], single_row[None, None, :], clipped).astype(jnp.int32)


def block_scale(own_key, shape, cuts, smallest, largest):
    loudness, own = 1.0, jax.random.fold_in(own_key, 6)
    for dim, shards_of in cuts:
        heights = jnp.exp(jax.random.uniform(jax.random.fold_in(own, dim), (shards_of,), jnp.float32, smallest / len(cuts), largest / len(cuts)))
        loudness = loudness * jnp.repeat(heights, shape[dim] // shards_of).reshape([-1 if axis == dim else 1 for axis in range(len(shape))])
    return loudness


def noise(own_key, shape, scale, bound, cuts=(), held_as=jnp.bfloat16):
    loudness = block_scale(own_key, shape, cuts, -0.22, 0.18) if cuts else 1.0
    entries = jax.random.normal(own_key, shape, jnp.float32) * scale * loudness
    return jnp.minimum(jnp.maximum(entries, -bound), bound).astype(held_as)


def setup_inputs(seed: int = 0) -> dict:
    keys = jax.random.split(jax.random.key(seed), 11)
    tokens = noise(keys[0], (MB, SEQ_MB, SEQUENCE_TOKENS, D), 1.0, 6.0, ((1, 4), (2, 8)))
    doc_lengths = draw_doc_lengths(jax.random.fold_in(keys[10], 71), 0)
    attn_gain = jnp.clip(1.0 + 0.18 * jax.random.normal(keys[2], (D,), jnp.float32), 0.1, 1.9)
    qkv_weight = noise(keys[3], (D * QKV,), D ** -0.5, 0.1875, ((0, 32),))
    qkv_bias = noise(keys[4], (QKV,), 0.5, 3.0, (), jnp.float32)
    out_weight = noise(keys[5], (QUERY_HEADS * HEAD_SIZE * D,), (QUERY_HEADS * HEAD_SIZE // 32) ** -0.5, 1.0, ((0, 32),))
    mlp_gain = jnp.clip(1.0 + 0.18 * jax.random.normal(keys[6], (D,), jnp.float32), 0.1, 1.9)
    gate_up_weight = noise(keys[7], (2 * D * FF,), D ** -0.5, 0.1875, ((0, 32),))
    down_weight = noise(keys[8], (FF * D,), FF ** -0.5, 0.078125, ((0, 32),))
    out_grad = noise(keys[9], (MB, SEQ_MB, SEQUENCE_TOKENS, D), 1.0, 6.0, ((1, 4), (2, 8)))
    return dict(tokens=tokens, doc_lengths=doc_lengths, attn_gain=attn_gain, qkv_weight=qkv_weight, qkv_bias=qkv_bias, out_weight=out_weight, mlp_gain=mlp_gain, gate_up_weight=gate_up_weight, down_weight=down_weight, out_grad=out_grad)


EPSILON = 1e-06
ROPE_THETA = 1000000.0
NEGATIVE = -1e+30
HIGHEST_PRECISION = lax.Precision.HIGHEST

@jax.custom_vjp
def lower_precision(v):
    return lax.optimization_barrier(v.astype(jnp.bfloat16)).astype(jnp.float32)

@jax.custom_vjp
def low_back(v):
    return v

def low_keep(v):
    return (lower_precision(v), None)

def low_pass(kept, grad):
    return (grad,)

def back_keep(v):
    return (v, None)

def back_low(kept, grad):
    return (lower_precision(grad),)
lower_precision.defvjp(low_keep, low_pass)
low_back.defvjp(back_keep, back_low)

def product(left, right):
    return jnp.dot(left, right, precision=HIGHEST_PRECISION, preferred_element_type=jnp.float32)

def rms_norm(value_rows, gain):
    return value_rows * lax.rsqrt(lax.optimization_barrier(jnp.mean(value_rows * value_rows, axis=-1, keepdims=True)) + EPSILON) * gain

def doc_layout(lengths, first_row, token_count):
    token_index = first_row + jnp.arange(token_count, dtype=jnp.int32)
    doc_ends = jnp.cumsum(lengths, dtype=jnp.int32)
    before = doc_ends[None, :] <= token_index[:, None]
    document_index = lax.optimization_barrier(jnp.sum(before.astype(jnp.int32), axis=1, dtype=jnp.int32))
    doc_start = lax.optimization_barrier(jnp.sum(jnp.where(before, lengths[None, :], 0), axis=1, dtype=jnp.int32))
    return (token_index, document_index, token_index - doc_start)

def rotation(positions, head_dim):
    freqs = ROPE_THETA ** (-(2.0 * jnp.arange(head_dim // 2, dtype=jnp.float32)) / head_dim)
    angles = positions.astype(jnp.float32)[:, None] * freqs[None, :]
    cosine_table = jnp.concatenate([jnp.cos(angles), jnp.cos(angles)], axis=-1)
    sine_table = jnp.concatenate([jnp.sin(angles), jnp.sin(angles)], axis=-1)
    return (cosine_table[:, None, :], sine_table[:, None, :])

def rotary_apply(heads, cosine_table, sine_table):
    half_dim = heads.shape[-1] // 2
    turned = jnp.concatenate([-heads[..., half_dim:], heads[..., :half_dim]], axis=-1)
    return heads * cosine_table + turned * sine_table

def residual_block(params, inputs, document_index, token_index, positions):
    attn_gain, w_qkv, qkv_bias, w_out, mlp_gain, w_gate_up, w_down = params
    query_groups = QUERY_HEADS // KEY_VALUE_HEADS
    query_total_width = QUERY_HEADS * HEAD_SIZE
    key_value_width = KEY_VALUE_HEADS * HEAD_SIZE
    cosine_table, sine_table = rotation(positions, HEAD_SIZE)
    hidden1 = lower_precision(rms_norm(inputs, attn_gain))
    query_key_value = low_back(product(hidden1, w_qkv) + qkv_bias)
    query_matrix = lower_precision(rotary_apply(query_key_value[:, :query_total_width].reshape(SEQUENCE_TOKENS, QUERY_HEADS, HEAD_SIZE), cosine_table, sine_table)).reshape(SEQUENCE_TOKENS, KEY_VALUE_HEADS, query_groups, HEAD_SIZE)
    key_rows = lower_precision(rotary_apply(query_key_value[:, query_total_width:query_total_width + key_value_width].reshape(SEQUENCE_TOKENS, KEY_VALUE_HEADS, HEAD_SIZE), cosine_table, sine_table))
    value_rows = lower_precision(query_key_value[:, query_total_width + key_value_width:].reshape(SEQUENCE_TOKENS, KEY_VALUE_HEADS, HEAD_SIZE))
    query_row_block = min(512, SEQUENCE_TOKENS)
    block_count = SEQUENCE_TOKENS // query_row_block
    score_scale = HEAD_SIZE ** (-0.5)

    def attend_tokens(block_item):
        query_block, seg_block, index_block = block_item
        score = jnp.einsum('qhgd,khd->qhgk', query_block, key_rows, precision=HIGHEST_PRECISION) * score_scale
        score = low_back(score)
        allowed = (document_index[None, :] == seg_block[:, None]) & (token_index[None, :] <= index_block[:, None])
        score = jnp.where(allowed[:, None, None, :], score, NEGATIVE)
        prob_low = lower_precision(jax.nn.softmax(score, axis=-1))
        return jnp.einsum('qhgk,khd->qhgd', prob_low, value_rows, precision=HIGHEST_PRECISION)
    attended_rows = lax.map(jax.checkpoint(attend_tokens), (query_matrix.reshape(block_count, query_row_block, KEY_VALUE_HEADS, query_groups, HEAD_SIZE), document_index.reshape(block_count, query_row_block), token_index.reshape(block_count, query_row_block)))
    att_low = lower_precision(low_back(attended_rows.reshape(SEQUENCE_TOKENS, query_total_width)))
    residual = inputs + low_back(product(att_low, w_out))
    hidden2 = lower_precision(rms_norm(residual, mlp_gain))
    gate_up = low_back(product(hidden2, w_gate_up))
    act_low = lower_precision(jax.nn.silu(gate_up[:, :FF]) * gate_up[:, FF:])
    return residual + product(act_low, w_down)

def reference(tokens, doc_lengths, attn_gain, qkv_weight, qkv_bias, out_weight, mlp_gain, gate_up_weight, down_weight, out_grad):
    params = (attn_gain.astype(jnp.float32), qkv_weight.astype(jnp.float32).reshape(D, QKV), qkv_bias.astype(jnp.float32), out_weight.astype(jnp.float32).reshape(QUERY_HEADS * HEAD_SIZE, D), mlp_gain.astype(jnp.float32), gate_up_weight.astype(jnp.float32).reshape(D, 2 * FF), down_weight.astype(jnp.float32).reshape(FF, D))
    seq_count = MB * SEQ_MB
    sequences = (tokens.reshape(seq_count, SEQUENCE_TOKENS, D), doc_lengths.reshape(seq_count, NDOC), out_grad.reshape(seq_count, SEQUENCE_TOKENS, D))
    zero_grads = jax.tree.map(jnp.zeros_like, params)

    def one_sequence(summed, sequence):
        inputs, lengths, cotangent = sequence
        token_index, document_index, positions = doc_layout(lengths, jnp.int32(0), SEQUENCE_TOKENS)

        def forward(weights_in, values_in):
            return residual_block(weights_in, values_in, document_index, token_index, positions)
        result, pullback = jax.vjp(forward, params, inputs.astype(jnp.float32))
        param_grads, input_grad = pullback(cotangent.astype(jnp.float32))
        return (jax.tree.map(jnp.add, summed, param_grads), (result.astype(jnp.bfloat16), input_grad))
    summed, (layer_out, input_grad) = lax.scan(one_sequence, zero_grads, sequences)
    return (layer_out.reshape(MB, SEQ_MB, SEQUENCE_TOKENS, D), input_grad.reshape(MB, SEQ_MB, SEQUENCE_TOKENS, D), summed[0], summed[1].reshape(-1), summed[2], summed[3].reshape(-1), summed[4], summed[5].reshape(-1), summed[6].reshape(-1))
```

```python
import jax
import jax.numpy as jnp
import numpy as np
from jax import lax
from jax.experimental import pallas as pl
from jax.experimental.pallas import tpu as pltpu
from jax.sharding import PartitionSpec as P

QUERY_HEADS = 14
KEY_VALUE_HEADS = 2
HEAD_SIZE = 64
FF = 4864
WIDTH = 896


EPSILON = 1e-06
ROPE_THETA = 1000000.0
NEGATIVE = -1e30
CONTRACT_ROWS = (((0,), (0,)), ((), ()))
CONTRACT_COLS = (((1,), (1,)), ((), ()))


def doc_layout(lengths, first_row, token_count):
    token_index = first_row + jnp.arange(token_count, dtype=jnp.int32)
    doc_ends = jnp.cumsum(lengths, dtype=jnp.int32)
    before = doc_ends[None, :] <= token_index[:, None]
    document_index = jnp.sum(before.astype(jnp.int32), axis=1, dtype=jnp.int32)
    doc_start = jnp.sum(jnp.where(before, lengths[None, :], 0), axis=1, dtype=jnp.int32)
    return (token_index, document_index, token_index - doc_start)


def rotation(positions, head_dim):
    freqs = ROPE_THETA ** (-(2.0 * jnp.arange(head_dim // 2, dtype=jnp.float32)) / head_dim)
    angles = positions.astype(jnp.float32)[:, None] * freqs[None, :]
    cosine_table = jnp.concatenate([jnp.cos(angles), jnp.cos(angles)], axis=-1)
    sine_table = jnp.concatenate([jnp.sin(angles), jnp.sin(angles)], axis=-1)
    return (cosine_table[:, None, :], sine_table[:, None, :])


def rotary_apply(heads, cosine_table, sine_table):
    half_dim = heads.shape[-1] // 2
    turned = jnp.concatenate([-heads[..., half_dim:], heads[..., :half_dim]], axis=-1)
    return heads * cosine_table + turned * sine_table


def rotary_reverse(grads, cosine_table, sine_table):
    half_dim = grads.shape[-1] // 2
    weighted = grads * sine_table
    turned = jnp.concatenate([weighted[..., half_dim:], -weighted[..., :half_dim]], axis=-1)
    return grads * cosine_table + turned


def rms_forward(value_rows, gain):
    row_scale = lax.rsqrt(jnp.mean(value_rows * value_rows, axis=-1, keepdims=True) + EPSILON)
    normed = value_rows * row_scale
    return (normed, row_scale, normed * gain)


def rms_backward(grads, normed, row_scale, gain):
    grad_normed = grads * gain
    gain_grad = jnp.sum(grads * normed, axis=0)
    back = row_scale * (
        grad_normed - normed * jnp.mean(grad_normed * normed, axis=-1, keepdims=True)
    )
    return (back, gain_grad)


def block_scores(
    query_matrix, key_block, token_index, document_index, seg_block, key_start, score_scale
):
    score = (
        jnp.einsum("qhgd,khd->qhgk", query_matrix, key_block, preferred_element_type=jnp.float32)
        * score_scale
    )
    key_index = key_start + jnp.arange(key_block.shape[0], dtype=jnp.int32)
    allowed = (seg_block[None, :] == document_index[:, None]) & (
        key_index[None, :] <= token_index[:, None]
    )
    return (score, allowed[:, None, None, :])


def split_blocks(keyvals, key_segment, block_rows, kv_heads, head_dim):
    seq_length = keyvals.shape[0]
    block_count = seq_length // block_rows
    kv_blocks = keyvals.reshape(block_count, block_rows, 2, kv_heads, head_dim)
    seg_blocks = key_segment.reshape(block_count, block_rows)
    starts = jnp.arange(block_count, dtype=jnp.int32) * block_rows
    return (kv_blocks, seg_blocks, starts)


def attend_forward(query_matrix, token_index, document_index, keyvals, key_segment, block_rows):
    kv_heads, head_dim = (query_matrix.shape[1], query_matrix.shape[3])
    score_scale = head_dim ** (-0.5)
    kv_blocks, seg_blocks, starts = split_blocks(
        keyvals, key_segment, block_rows, kv_heads, head_dim
    )

    def stats_step(running, block_item):
        kv_block, seg_block, key_start = block_item
        row_max, row_sum = running
        score, allowed = block_scores(
            query_matrix,
            kv_block[:, 0],
            token_index,
            document_index,
            seg_block,
            key_start,
            score_scale,
        )
        new_max = jnp.maximum(row_max, jnp.max(jnp.where(allowed, score, NEGATIVE), axis=-1))
        weights = jnp.where(allowed, jnp.exp(score - new_max[..., None]), 0.0)
        return ((new_max, row_sum * jnp.exp(row_max - new_max) + jnp.sum(weights, axis=-1)), None)

    stats_init = (
        jnp.full(query_matrix.shape[:3], NEGATIVE, jnp.float32),
        jnp.zeros(query_matrix.shape[:3], jnp.float32),
    )
    (row_max, row_sum), unused = lax.scan(stats_step, stats_init, (kv_blocks, seg_blocks, starts))

    def out_step(running, block_item):
        kv_block, seg_block, key_start = block_item
        score, allowed = block_scores(
            query_matrix,
            kv_block[:, 0],
            token_index,
            document_index,
            seg_block,
            key_start,
            score_scale,
        )
        probability = jnp.where(
            allowed, jnp.exp(score - row_max[..., None]) / row_sum[..., None], 0.0
        )
        return (
            running
            + jnp.einsum(
                "qhgk,khd->qhgd",
                probability.astype(jnp.bfloat16),
                kv_block[:, 1],
                preferred_element_type=jnp.float32,
            ),
            None,
        )

    attended_rows, unused = lax.scan(
        out_step, jnp.zeros(query_matrix.shape, jnp.float32), (kv_blocks, seg_blocks, starts)
    )
    return (attended_rows, row_max, row_sum)


def attend_backward(
    query_matrix,
    token_index,
    document_index,
    keyvals,
    key_segment,
    row_max,
    row_sum,
    attention_gradient,
    delta,
    block_rows,
):
    kv_heads, head_dim = (query_matrix.shape[1], query_matrix.shape[3])
    score_scale = head_dim ** (-0.5)
    seq_length = keyvals.shape[0]
    kv_blocks, seg_blocks, starts = split_blocks(
        keyvals, key_segment, block_rows, kv_heads, head_dim
    )

    def grad_step(running, block_item):
        kv_block, seg_block, key_start = block_item
        grad_query = running
        score, allowed = block_scores(
            query_matrix,
            kv_block[:, 0],
            token_index,
            document_index,
            seg_block,
            key_start,
            score_scale,
        )
        probability = jnp.where(
            allowed, jnp.exp(score - row_max[..., None]) / row_sum[..., None], 0.0
        )
        grad_prob = jnp.einsum(
            "qhgd,khd->qhgk", attention_gradient, kv_block[:, 1], preferred_element_type=jnp.float32
        )
        grad_score = (probability * (grad_prob - delta[..., None])).astype(jnp.bfloat16)
        grad_query = (
            grad_query
            + jnp.einsum(
                "qhgk,khd->qhgd", grad_score, kv_block[:, 0], preferred_element_type=jnp.float32
            )
            * score_scale
        )
        key_gradient = (
            jnp.einsum(
                "qhgk,qhgd->khd", grad_score, query_matrix, preferred_element_type=jnp.float32
            )
            * score_scale
        )
        grad_value = jnp.einsum(
            "qhgk,qhgd->khd",
            probability.astype(jnp.bfloat16),
            attention_gradient,
            preferred_element_type=jnp.float32,
        )
        return (
            grad_query,
            jnp.concatenate(
                [key_gradient.reshape(block_rows, -1), grad_value.reshape(block_rows, -1)], axis=1
            ),
        )

    grad_query, grad_kv = lax.scan(
        grad_step, jnp.zeros(query_matrix.shape, jnp.float32), (kv_blocks, seg_blocks, starts)
    )
    return (grad_query, grad_kv.reshape(seq_length, 2 * kv_heads * head_dim))


def body(
    tokens,
    doc_lengths,
    attn_gain,
    qkv_weight,
    qkv_bias,
    out_weight,
    mlp_gain,
    gate_up_weight,
    down_weight,
    out_grad,
):
    model_width = attn_gain.shape[0]
    qkv_width = qkv_bias.shape[0]
    query_total_width = QUERY_HEADS * HEAD_SIZE
    key_value_width = KEY_VALUE_HEADS * HEAD_SIZE
    query_groups = QUERY_HEADS // KEY_VALUE_HEADS
    token_count = tokens.shape[2]
    seq_length = token_count * lax.axis_size("ctx")
    first_row = lax.axis_index("ctx") * token_count
    block_rows = min(512, seq_length)
    device_count = lax.axis_size(("dp", "ctx"))

    def unpack(gathered):
        flat_qkv, flat_out, flat_gate_up, flat_down = gathered
        return (
            flat_qkv.reshape(model_width, qkv_width),
            flat_out.reshape(query_total_width, model_width),
            flat_gate_up.reshape(model_width, 2 * FF),
            flat_down.reshape(FF, model_width),
        )

    grad_qkv = jnp.zeros((model_width, qkv_width), jnp.float32)
    grad_out = jnp.zeros((query_total_width, model_width), jnp.float32)
    grad_gate_up = jnp.zeros((model_width, 2 * FF), jnp.float32)
    grad_down = jnp.zeros((FF, model_width), jnp.float32)
    grad_gain1 = jnp.zeros((model_width,), jnp.float32)
    grad_gain2 = jnp.zeros((model_width,), jnp.float32)
    grad_bias = jnp.zeros((qkv_width,), jnp.float32)
    layer_outs = []
    input_grads = []
    for micro_step in range(tokens.shape[0]):
        w_qkv, w_out, w_gate_up, w_down = unpack(
            (
                lax.all_gather(qkv_weight, ("dp", "ctx"), axis=0, tiled=True),
                lax.all_gather(out_weight, ("dp", "ctx"), axis=0, tiled=True),
                lax.all_gather(gate_up_weight, ("dp", "ctx"), axis=0, tiled=True),
                lax.all_gather(down_weight, ("dp", "ctx"), axis=0, tiled=True),
            )
        )
        inputs = tokens[micro_step, 0].astype(jnp.float32)
        token_index, document_index, positions = doc_layout(
            doc_lengths[micro_step, 0], first_row, token_count
        )
        cosine_table, sine_table = rotation(positions, HEAD_SIZE)
        normed1, scale1, hidden1 = rms_forward(inputs, attn_gain)
        hidden1 = hidden1.astype(jnp.bfloat16)
        query_key_value = jnp.dot(hidden1, w_qkv, preferred_element_type=jnp.float32) + qkv_bias
        query_matrix = rotary_apply(
            query_key_value[:, :query_total_width].reshape(token_count, QUERY_HEADS, HEAD_SIZE),
            cosine_table,
            sine_table,
        )
        query_matrix = query_matrix.astype(jnp.bfloat16).reshape(
            token_count, KEY_VALUE_HEADS, query_groups, HEAD_SIZE
        )
        key_rows = rotary_apply(
            query_key_value[:, query_total_width : query_total_width + key_value_width].reshape(
                token_count, KEY_VALUE_HEADS, HEAD_SIZE
            ),
            cosine_table,
            sine_table,
        ).astype(jnp.bfloat16)
        value_rows = query_key_value[:, query_total_width + key_value_width :].astype(jnp.bfloat16)
        local_kv = jnp.concatenate(
            [key_rows.reshape(token_count, key_value_width), value_rows], axis=1
        )
        all_kv, all_segments = (
            lax.all_gather(local_kv, "ctx", axis=0, tiled=True),
            lax.all_gather(document_index, "ctx", axis=0, tiled=True),
        )
        attended_rows, row_max, row_sum = attend_forward(
            query_matrix, token_index, document_index, all_kv, all_segments, block_rows
        )
        att_low = attended_rows.reshape(token_count, query_total_width).astype(jnp.bfloat16)
        residual = inputs + jnp.dot(att_low, w_out, preferred_element_type=jnp.float32)
        normed2, scale2, hidden2 = rms_forward(residual, mlp_gain)
        hidden2 = hidden2.astype(jnp.bfloat16)
        gate_up = jnp.dot(hidden2, w_gate_up, preferred_element_type=jnp.float32)
        gate_part = gate_up[:, :FF]
        up_part = gate_up[:, FF:]
        sigmoid = jax.nn.sigmoid(gate_part)
        silu_gate = gate_part * sigmoid
        act_low = (silu_gate * up_part).astype(jnp.bfloat16)
        layer_outs.append(
            (residual + jnp.dot(act_low, w_down, preferred_element_type=jnp.float32)).astype(
                jnp.bfloat16
            )
        )
        back_qkv, back_out, back_gate_up, back_down = unpack(
            (
                lax.all_gather(qkv_weight, ("dp", "ctx"), axis=0, tiled=True),
                lax.all_gather(out_weight, ("dp", "ctx"), axis=0, tiled=True),
                lax.all_gather(gate_up_weight, ("dp", "ctx"), axis=0, tiled=True),
                lax.all_gather(down_weight, ("dp", "ctx"), axis=0, tiled=True),
            )
        )
        back_kv, back_segments = (
            lax.all_gather(local_kv, "ctx", axis=0, tiled=True),
            lax.all_gather(document_index, "ctx", axis=0, tiled=True),
        )
        cotangent = out_grad[micro_step, 0]
        grad_down = grad_down + lax.dot_general(
            act_low, cotangent, CONTRACT_ROWS, preferred_element_type=jnp.float32
        )
        grad_act = lax.dot_general(
            cotangent, back_down, CONTRACT_COLS, preferred_element_type=jnp.float32
        )
        grad_gate = grad_act * up_part * sigmoid * (1.0 + gate_part * (1.0 - sigmoid))
        grad_up = grad_act * silu_gate
        grad_gu = jnp.concatenate([grad_gate, grad_up], axis=1).astype(jnp.bfloat16)
        grad_gate_up = grad_gate_up + lax.dot_general(
            hidden2, grad_gu, CONTRACT_ROWS, preferred_element_type=jnp.float32
        )
        grad_hidden2 = lax.dot_general(
            grad_gu, back_gate_up, CONTRACT_COLS, preferred_element_type=jnp.float32
        )
        back_mlp, gain_part2 = rms_backward(grad_hidden2, normed2, scale2, mlp_gain)
        grad_gain2 = grad_gain2 + gain_part2
        grad_mid = cotangent.astype(jnp.float32) + back_mlp
        grad_mid_low = grad_mid.astype(jnp.bfloat16)
        grad_out = grad_out + lax.dot_general(
            att_low, grad_mid_low, CONTRACT_ROWS, preferred_element_type=jnp.float32
        )
        attention_gradient = lax.dot_general(
            grad_mid_low, back_out, CONTRACT_COLS, preferred_element_type=jnp.float32
        )
        attention_gradient = attention_gradient.astype(jnp.bfloat16).reshape(
            token_count, KEY_VALUE_HEADS, query_groups, HEAD_SIZE
        )
        delta = jnp.sum(attention_gradient.astype(jnp.float32) * attended_rows, axis=-1)
        grad_query, grad_kv = attend_backward(
            query_matrix,
            token_index,
            document_index,
            back_kv,
            back_segments,
            row_max,
            row_sum,
            attention_gradient,
            delta,
            block_rows,
        )
        owned_key_value = lax.psum_scatter(
            grad_kv.astype(jnp.bfloat16), "ctx", scatter_dimension=0, tiled=True
        ).astype(jnp.float32)
        key_gradient = rotary_reverse(
            owned_key_value[:, :key_value_width].reshape(token_count, KEY_VALUE_HEADS, HEAD_SIZE),
            cosine_table,
            sine_table,
        )
        grad_query = rotary_reverse(
            grad_query.reshape(token_count, QUERY_HEADS, HEAD_SIZE), cosine_table, sine_table
        )
        grad_qkv_low = jnp.concatenate(
            [
                grad_query.reshape(token_count, query_total_width),
                key_gradient.reshape(token_count, key_value_width),
                owned_key_value[:, key_value_width:],
            ],
            axis=1,
        ).astype(jnp.bfloat16)
        grad_bias = grad_bias + jnp.sum(grad_qkv_low.astype(jnp.float32), axis=0)
        grad_qkv = grad_qkv + lax.dot_general(
            hidden1, grad_qkv_low, CONTRACT_ROWS, preferred_element_type=jnp.float32
        )
        grad_hidden1 = lax.dot_general(
            grad_qkv_low, back_qkv, CONTRACT_COLS, preferred_element_type=jnp.float32
        )
        back_attn, gain_part1 = rms_backward(grad_hidden1, normed1, scale1, attn_gain)
        grad_gain1 = grad_gain1 + gain_part1
        input_grads.append(grad_mid + back_attn)
    grad_list = (grad_qkv, grad_out, grad_gate_up, grad_down)
    widths = [item.size // device_count for item in grad_list]
    stacked = jnp.concatenate([item.reshape(device_count, -1) for item in grad_list], axis=1)
    mine = lax.psum_scatter(stacked, ("dp", "ctx"), scatter_dimension=0, tiled=True).reshape(-1)
    offsets = [0, widths[0], widths[0] + widths[1], widths[0] + widths[1] + widths[2]]
    shares = [mine[offsets[k] : offsets[k] + widths[k]] for k in range(4)]
    small_sums = lax.psum((grad_gain1, grad_bias, grad_gain2), ("dp", "ctx"))
    return (
        jnp.stack(layer_outs)[:, None],
        jnp.stack(input_grads)[:, None],
        small_sums[0],
        shares[0],
        small_sums[1],
        shares[1],
        small_sums[2],
        shares[2],
        shares[3],
    )


def send_perm(total, parts, stride, step):
    pairs = []
    for index in range(total):
        place = (index // stride) % parts
        pairs.append((index, index + ((place + step) % parts - place) * stride))
    return pairs


def swap_perm(total, stride, step):
    return [(index, (((index // stride) ^ step) * stride) + index % stride) for index in range(total)]


class Links:
    def __init__(self):
        self.dp = lax.axis_size("dp")
        self.ctx = lax.axis_size("ctx")
        self.cores = 2
        self.rows = self.dp // 2
        self.wide = self.rows
        self.deep = self.ctx // self.wide
        self.me_dp = lax.axis_index("dp")
        self.me_ctx = lax.axis_index("ctx")
        self.core = self.me_dp % 2
        self.y = self.me_dp // 2
        self.x = self.me_ctx % self.wide
        self.z = self.me_ctx // self.wide

    def core_step(self, item, step=1):
        return lax.ppermute(item, "dp", send_perm(self.dp, 2, 1, step))

    def y_step(self, item, step=1):
        return lax.ppermute(item, "dp", send_perm(self.dp, self.rows, 2, step))

    def dp_step(self, item, step=1):
        return lax.ppermute(item, "dp", send_perm(self.dp, self.dp, 1, step))

    def x_step(self, item, step=1):
        return lax.ppermute(item, "ctx", send_perm(self.ctx, self.wide, 1, step))

    def z_step(self, item, step=1):
        return lax.ppermute(item, "ctx", send_perm(self.ctx, self.deep, self.wide, step))

    def gather_ctx(self, items):
        held = [jnp.zeros((self.ctx, *item.shape), item.dtype) for item in items]
        moving = list(items)
        for back in range(self.deep):
            if back:
                moving = [self.z_step(item) for item in moving]
            from_z = (self.z - back) % self.deep
            for across in range(self.wide):
                from_x = (self.x - across) % self.wide
                place = from_z * self.wide + from_x
                for k, item in enumerate(moving):
                    part = self.x_step(item, across) if across else item
                    held[k] = lax.dynamic_update_index_in_dim(held[k], part, place, 0)
        return held

    def scatter_ctx(self, whole):
        def across_x(to_z):
            first = to_z * self.wide
            total = lax.dynamic_index_in_dim(whole, first + self.x, 0, False).astype(jnp.float32)
            for across in range(1, self.wide):
                to_x = (self.x + across) % self.wide
                part = lax.dynamic_index_in_dim(whole, first + to_x, 0, False)
                total = total + self.x_step(part, across).astype(jnp.float32)
            return total

        moving = None
        for back in range(1, self.deep + 1):
            total = across_x((self.z - back) % self.deep)
            if moving is not None:
                total = total + moving.astype(jnp.float32)
            if back == self.deep:
                return total
            moving = self.z_step(total.astype(whole.dtype))

    def gather_y(self, item):
        held = jnp.zeros((self.rows, *item.shape), item.dtype)
        held = lax.dynamic_update_index_in_dim(held, item, self.y, 0)
        for step in range(1, self.rows):
            held = lax.dynamic_update_index_in_dim(
                held, self.y_step(item, step), (self.y - step) % self.rows, 0
            )
        return held

    def gather_core(self, item):
        other = self.core_step(item)
        first = self.core == 0
        return jnp.stack([jnp.where(first, item, other), jnp.where(first, other, item)])

    def gather_dp(self, item):
        pair = self.gather_core(self.gather_y(item))
        return jnp.swapaxes(pair, 0, 1).reshape(self.dp, *item.shape)

    def scatter_dp(self, whole):
        split = whole.reshape(self.rows, 2, *whole.shape[1:])
        mine = lax.dynamic_index_in_dim(split, self.core, 1, False)
        other = self.core_step(lax.dynamic_index_in_dim(split, 1 - self.core, 1, False))
        pair = mine.astype(jnp.float32) + other.astype(jnp.float32)
        total = lax.dynamic_index_in_dim(pair, self.y, 0, False)
        low = pair.astype(whole.dtype)
        for step in range(1, self.rows):
            part = lax.dynamic_index_in_dim(low, (self.y + step) % self.rows, 0, False)
            total = total + self.y_step(part, step).astype(jnp.float32)
        return total

    def exchange_dp(self, whole):
        held = jnp.zeros_like(whole)
        for step in range(self.dp):
            part = lax.dynamic_index_in_dim(whole, (self.me_dp + step) % self.dp, 0, False)
            part = self.dp_step(part, step) if step else part
            held = lax.dynamic_update_index_in_dim(held, part, (self.me_dp - step) % self.dp, 0)
        return held

    def sum_all(self, item):
        for axis, total, stride, parts in (
            ("dp", self.dp, 1, self.dp),
            ("ctx", self.ctx, 1, self.ctx),
        ):
            step = 1
            while step < parts:
                item = item + lax.ppermute(item, axis, swap_perm(total, stride, step))
                step *= 2
        return item


def allowed_bias(low_ref, first_ref, bias_ref):
    keys = lax.broadcasted_iota(jnp.int32, bias_ref.shape, 0)
    query = first_ref[0] + lax.broadcasted_iota(jnp.int32, bias_ref.shape, 1)
    allowed = (keys >= low_ref[...]) & (keys <= query)
    bias_ref[...] = jnp.where(allowed, 0.0, NEGATIVE)


def head_rows(ref, head):
    return ref[head * HEAD_SIZE : (head + 1) * HEAD_SIZE, :]


def key_columns(kv_ref):
    parts = [kv_ref[j] for j in range(kv_ref.shape[0])]
    return jnp.concatenate(parts, axis=1)


def attention_kernel(first_ref, low_ref, q_ref, kv_ref, att_ref, stat_ref, bias_ref):
    allowed_bias(low_ref, first_ref, bias_ref)
    kv_cols = key_columns(kv_ref)
    groups = QUERY_HEADS // KEY_VALUE_HEADS
    half = KEY_VALUE_HEADS * HEAD_SIZE
    key_rows = kv_cols[:half].T
    for kv_head in range(KEY_VALUE_HEADS):
        key = key_rows[:, kv_head * HEAD_SIZE : (kv_head + 1) * HEAD_SIZE]
        value = kv_cols[half + kv_head * HEAD_SIZE : half + (kv_head + 1) * HEAD_SIZE]
        for head in range(kv_head * groups, (kv_head + 1) * groups):
            score = jnp.dot(key, head_rows(q_ref, head), preferred_element_type=jnp.float32)
            score = score * HEAD_SIZE ** (-0.5) + bias_ref[...]
            top = jnp.max(score, axis=0, keepdims=True)
            weights = jnp.exp(score - top)
            total = jnp.sum(weights, axis=0, keepdims=True)
            out = jnp.dot(value, weights.astype(jnp.bfloat16), preferred_element_type=jnp.float32)
            att_ref[head * HEAD_SIZE : (head + 1) * HEAD_SIZE, :] = out / total
            stat_ref[head : head + 1, :] = top + jnp.log(total)


def attention_back_kernel(
    first_ref,
    low_ref,
    q_ref,
    kv_ref,
    att_ref,
    stat_ref,
    datt_ref,
    dq_ref,
    dkv_ref,
    bias_ref,
    qs_ref,
    das_ref,
    ds_ref,
    p_ref,
):
    allowed_bias(low_ref, first_ref, bias_ref)
    kv_cols = key_columns(kv_ref)
    tokens = q_ref.shape[1]
    groups = QUERY_HEADS // KEY_VALUE_HEADS
    half = KEY_VALUE_HEADS * HEAD_SIZE
    scale = HEAD_SIZE ** (-0.5)
    rows = kv_cols.T
    results = []
    for kv_head in range(KEY_VALUE_HEADS):
        own = slice(kv_head * HEAD_SIZE, (kv_head + 1) * HEAD_SIZE)
        key = rows[:, own]
        value = rows[:, half + kv_head * HEAD_SIZE : half + (kv_head + 1) * HEAD_SIZE]
        key_cols = kv_cols[own]
        for place in range(groups):
            head = kv_head * groups + place
            lanes = slice(place * tokens, (place + 1) * tokens)
            query = head_rows(q_ref, head)
            datt = head_rows(datt_ref, head)
            qs_ref[:, lanes] = query
            das_ref[:, lanes] = datt
            delta = jnp.sum(
                datt.astype(jnp.float32) * head_rows(att_ref, head), axis=0, keepdims=True
            )
            score = jnp.dot(key, query, preferred_element_type=jnp.float32)
            prob = jnp.exp(score * scale + bias_ref[...] - stat_ref[head : head + 1, :])
            dprob = jnp.dot(value, datt, preferred_element_type=jnp.float32)
            dscore = (prob * (dprob - delta)).astype(jnp.bfloat16)
            ds_ref[:, lanes] = dscore
            p_ref[:, lanes] = prob.astype(jnp.bfloat16)
            dq_ref[head * HEAD_SIZE : (head + 1) * HEAD_SIZE, :] = (
                jnp.dot(key_cols, dscore, preferred_element_type=jnp.float32) * scale
            )
        results.append(
            lax.dot_general(
                ds_ref[...], qs_ref[...], CONTRACT_COLS, preferred_element_type=jnp.float32
            )
            * scale
        )
        results.append(
            lax.dot_general(
                p_ref[...], das_ref[...], CONTRACT_COLS, preferred_element_type=jnp.float32
            )
        )
    order = results[0::2] + results[1::2]
    out = jnp.concatenate(order, axis=1).astype(dkv_ref.dtype)
    for j in range(dkv_ref.shape[0]):
        dkv_ref[j] = out[j * tokens : (j + 1) * tokens]


def attention_specs(width, pieces, kv_width, tokens):
    smem = pl.BlockSpec(memory_space=pltpu.SMEM)
    low = pl.BlockSpec((pl.Squeezed(), 1, tokens), lambda mb: (mb, 0, 0))
    cols = pl.BlockSpec((width, tokens), lambda mb: (0, mb))
    kv = pl.BlockSpec((pieces, kv_width, tokens), lambda mb: (0, 0, mb))
    stat = pl.BlockSpec((QUERY_HEADS, tokens), lambda mb: (0, mb))
    return smem, low, cols, kv, stat


def attend(first, low, q_cols, kv_all, batches):
    width, total = q_cols.shape
    tokens = total // batches
    pieces, kv_width, _ = kv_all.shape
    smem, low_spec, cols, kv, stat = attention_specs(width, pieces, kv_width, tokens)
    return pl.pallas_call(
        attention_kernel,
        grid=(batches,),
        in_specs=[smem, low_spec, cols, kv],
        out_specs=[cols, stat],
        out_shape=[
            jax.ShapeDtypeStruct((width, total), jnp.float32),
            jax.ShapeDtypeStruct((QUERY_HEADS, total), jnp.float32),
        ],
        scratch_shapes=[pltpu.VMEM((pieces * tokens, tokens), jnp.float32)],
        compiler_params=pltpu.CompilerParams(vmem_limit_bytes=40 * 2**20),
        cost_estimate=pl.CostEstimate(
            flops=4 * total * pieces * tokens * width,
            bytes_accessed=8 * total * width,
            transcendentals=total * pieces * tokens * QUERY_HEADS,
        ),
        name="attention",
    )(first, low, q_cols, kv_all)


def attend_back(first, low, q_cols, kv_all, att_cols, stats, datt_cols, batches):
    width, total = q_cols.shape
    tokens = total // batches
    pieces, kv_width, _ = kv_all.shape
    groups = QUERY_HEADS // KEY_VALUE_HEADS
    keys = pieces * tokens
    smem, low_spec, cols, kv, stat = attention_specs(width, pieces, kv_width, tokens)
    return pl.pallas_call(
        attention_back_kernel,
        grid=(batches,),
        in_specs=[smem, low_spec, cols, kv, cols, stat, cols],
        out_specs=[
            cols,
            pl.BlockSpec((pieces, pl.Squeezed(), tokens, kv_width), lambda mb: (0, mb, 0, 0)),
        ],
        out_shape=[
            jax.ShapeDtypeStruct((width, total), jnp.float32),
            jax.ShapeDtypeStruct((pieces, batches, tokens, kv_width), jnp.bfloat16),
        ],
        scratch_shapes=[
            pltpu.VMEM((keys, tokens), jnp.float32),
            pltpu.VMEM((HEAD_SIZE, groups * tokens), jnp.bfloat16),
            pltpu.VMEM((HEAD_SIZE, groups * tokens), jnp.bfloat16),
            pltpu.VMEM((keys, groups * tokens), jnp.bfloat16),
            pltpu.VMEM((keys, groups * tokens), jnp.bfloat16),
        ],
        compiler_params=pltpu.CompilerParams(vmem_limit_bytes=48 * 2**20),
        cost_estimate=pl.CostEstimate(
            flops=10 * total * keys * width,
            bytes_accessed=14 * total * width,
            transcendentals=total * keys * QUERY_HEADS,
        ),
        name="attention_back",
    )(first, low, q_cols, kv_all, att_cols, stats, datt_cols)


def one_hot_order(order):
    size = len(order)
    rows = lax.broadcasted_iota(jnp.int32, (size, size), 0)
    return (rows == jnp.asarray(order, jnp.int32)[None, :]).astype(jnp.bfloat16)


def dot32(left, right, dims=(((1,), (0,)), ((), ()))):
    return lax.dot_general(left, right, dims, preferred_element_type=jnp.float32)


def rope_columns(cols, cosine, sine):
    first, second = cols[:, 0], cols[:, 1]
    return jnp.stack([first * cosine - second * sine, second * cosine + first * sine], axis=1)


def rope_columns_back(cols, cosine, sine):
    first, second = cols[:, 0], cols[:, 1]
    return jnp.stack([first * cosine + second * sine, second * cosine - first * sine], axis=1)


def short_body(
    tokens,
    doc_lengths,
    attn_gain,
    qkv_weight,
    qkv_bias,
    out_weight,
    mlp_gain,
    gate_up_weight,
    down_weight,
    out_grad,
):
    links = Links()
    width = attn_gain.shape[0]
    qkv_width = qkv_bias.shape[0]
    query_width = QUERY_HEADS * HEAD_SIZE
    kv_width = KEY_VALUE_HEADS * HEAD_SIZE
    half = HEAD_SIZE // 2
    batches, token_count = tokens.shape[0], tokens.shape[2]
    total = batches * token_count
    devices = links.dp * links.ctx
    piece = width // devices
    own_ff = FF // links.dp
    first_row = links.me_ctx * token_count

    natural = np.arange(width).reshape(links.rows, 2, links.ctx, piece)
    attn_order = natural.transpose(1, 2, 0, 3).reshape(-1)
    mlp_order = natural.reshape(links.dp, links.ctx, piece).transpose(1, 0, 2).reshape(-1)
    attn_pick = one_hot_order(attn_order)
    mlp_pick = one_hot_order(mlp_order)

    def gather_rows(flat, columns):
        pair = links.gather_y(flat.reshape(piece, columns)).reshape(links.rows * piece, columns)
        (part,) = links.gather_ctx([pair])
        return links.gather_core(part.reshape(-1, columns)).reshape(width, columns)

    def scatter_rows(grad):
        columns = grad.shape[1]
        split = grad.reshape(2, width // 2, columns)
        mine = lax.dynamic_index_in_dim(split, links.core, 0, False)
        other = links.core_step(lax.dynamic_index_in_dim(split, 1 - links.core, 0, False))
        pair = (mine.astype(jnp.float32) + other.astype(jnp.float32)).astype(jnp.bfloat16)
        part = links.scatter_ctx(pair.reshape(links.ctx, links.rows * piece, columns))
        part = part.reshape(links.rows, piece, columns)
        sum_y = lax.dynamic_index_in_dim(part, links.y, 0, False)
        low = part.astype(jnp.bfloat16)
        for step in range(1, links.rows):
            there = lax.dynamic_index_in_dim(low, (links.y + step) % links.rows, 0, False)
            sum_y = sum_y + links.y_step(there, step).astype(jnp.float32)
        return sum_y.reshape(-1)

    w_qkv = gather_rows(qkv_weight, qkv_width)
    w_out = gather_rows(out_weight, width)
    gate_up_rows = gate_up_weight.reshape(piece, 2, links.dp, own_ff)
    gate_up_rows = gate_up_rows.transpose(2, 0, 1, 3).reshape(links.dp, piece, 2 * own_ff)
    gate_up_part = links.exchange_dp(gate_up_rows).reshape(links.dp * piece, 2 * own_ff)
    down_part = down_weight.reshape(own_ff // links.ctx, width)
    gate_up_part, down_part, w_qkv = lax.optimization_barrier((gate_up_part, down_part, w_qkv))
    w_gate_up, w_down = links.gather_ctx([gate_up_part, down_part])
    w_gate_up = w_gate_up.reshape(width, 2 * own_ff)
    w_down = w_down.reshape(own_ff, width)

    cotangent = out_grad[:, 0].reshape(total, width)
    all_cotangent = links.gather_dp(cotangent).reshape(links.dp * total, width)

    inputs = tokens[:, 0].reshape(total, width).astype(jnp.float32)
    layouts = [doc_layout(doc_lengths[b, 0], first_row, token_count) for b in range(batches)]
    token_index = layouts[0][0]
    positions = jnp.concatenate([item[2] for item in layouts])
    low = jnp.stack([token_index - item[2] for item in layouts])[:, None, :]
    first = jnp.reshape(first_row, (1,)).astype(jnp.int32)
    freqs = ROPE_THETA ** (-(2.0 * jnp.arange(half, dtype=jnp.float32)) / HEAD_SIZE)
    angles = freqs[:, None] * positions.astype(jnp.float32)[None, :]
    cosine, sine = jnp.cos(angles), jnp.sin(angles)

    normed1, scale1, hidden1 = rms_forward(inputs, attn_gain)
    hidden1 = dot32(hidden1.astype(jnp.bfloat16), attn_pick).astype(jnp.bfloat16)
    qkv_cols = dot32(w_qkv, hidden1, (((0,), (1,)), ((), ()))) + qkv_bias[:, None]
    turned = rope_columns(
        qkv_cols[: query_width + kv_width].reshape(-1, 2, half, total), cosine, sine
    )
    turned = turned.reshape(query_width + kv_width, total).astype(jnp.bfloat16)
    q_cols = turned[:query_width]
    kv_cols = jnp.concatenate(
        [turned[query_width:], qkv_cols[query_width + kv_width :].astype(jnp.bfloat16)]
    )
    (kv_all,) = links.gather_ctx([kv_cols])
    att_cols, stats = attend(first, low, q_cols, kv_all, batches)
    att_low = dot32(
        att_cols.astype(jnp.bfloat16), attn_pick, (((0,), (0,)), ((), ()))
    ).astype(jnp.bfloat16)
    residual = inputs + dot32(att_low, w_out)

    normed2, scale2, hidden2 = rms_forward(residual, mlp_gain)
    hidden2 = dot32(hidden2.astype(jnp.bfloat16), mlp_pick).astype(jnp.bfloat16)
    all_hidden2 = links.gather_dp(hidden2).reshape(links.dp * total, width)
    gate_up = dot32(all_hidden2, w_gate_up)
    gate, up = gate_up[:, :own_ff], gate_up[:, own_ff:]
    sigmoid = jax.nn.sigmoid(gate)
    silu = gate * sigmoid
    act_low = (silu * up).astype(jnp.bfloat16)
    dact = dot32(all_cotangent, w_down, CONTRACT_COLS)
    dgate = dact * up * sigmoid * (1.0 + gate * (1.0 - sigmoid))
    dgu = jnp.concatenate([dgate, dact * silu], axis=1).astype(jnp.bfloat16)
    dhidden2 = dot32(dgu, w_gate_up, CONTRACT_COLS).astype(jnp.bfloat16)
    dhidden2 = dot32(dhidden2, mlp_pick, CONTRACT_COLS).astype(jnp.bfloat16)
    dhidden2 = links.scatter_dp(dhidden2.reshape(links.dp, total, width))
    grad_gate_up = dot32(all_hidden2, dgu, CONTRACT_ROWS).astype(jnp.bfloat16)
    grad_down = dot32(act_low, all_cotangent, CONTRACT_ROWS).astype(jnp.bfloat16)
    out_part = dot32(act_low, w_down).astype(jnp.bfloat16)
    layer_out = residual + links.scatter_dp(out_part.reshape(links.dp, total, width))

    back_mlp, gain2_grad = rms_backward(dhidden2, normed2, scale2, mlp_gain)
    dmid = cotangent.astype(jnp.float32) + back_mlp
    dmid_low = dmid.astype(jnp.bfloat16)
    datt = dot32(dmid_low, w_out, CONTRACT_COLS).astype(jnp.bfloat16)
    datt_cols = dot32(attn_pick, datt, CONTRACT_COLS).astype(jnp.bfloat16)
    grad_out = dot32(att_low, dmid_low, CONTRACT_ROWS).astype(jnp.bfloat16)
    dq_cols, dkv = attend_back(first, low, q_cols, kv_all, att_cols, stats, datt_cols, batches)
    own_dkv = links.scatter_ctx(dkv).reshape(total, 2 * kv_width).T
    dqk = jnp.concatenate([dq_cols, own_dkv[:kv_width]]).reshape(-1, 2, half, total)
    dqk = rope_columns_back(dqk, cosine, sine).reshape(query_width + kv_width, total)
    dqkv = jnp.concatenate([dqk, own_dkv[kv_width:]]).astype(jnp.bfloat16)
    bias_grad = jnp.sum(dqkv.astype(jnp.float32), axis=1)
    grad_qkv = dot32(hidden1, dqkv, (((0,), (1,)), ((), ()))).astype(jnp.bfloat16)
    dhidden1 = dot32(dqkv, w_qkv, (((0,), (1,)), ((), ())))
    top = dhidden1.astype(jnp.bfloat16)
    rest = (dhidden1 - top.astype(jnp.float32)).astype(jnp.bfloat16)
    dhidden1 = dot32(top, attn_pick, CONTRACT_COLS) + dot32(rest, attn_pick, CONTRACT_COLS)
    back_attn, gain1_grad = rms_backward(dhidden1, normed1, scale1, attn_gain)
    input_grad = dmid + back_attn

    parts = links.scatter_ctx(grad_gate_up.reshape(links.ctx, links.dp * piece, 2 * own_ff))
    down_share = links.scatter_ctx(grad_down.reshape(links.ctx, own_ff // links.ctx, width))
    parts = parts.astype(jnp.bfloat16).reshape(links.dp, piece, 2 * own_ff)
    parts = links.exchange_dp(parts).reshape(links.dp, piece, 2, own_ff)
    gate_up_share = parts.transpose(1, 2, 0, 3).astype(jnp.float32).reshape(-1)
    out_share = scatter_rows(grad_out)
    qkv_share = scatter_rows(grad_qkv)
    small = links.sum_all(jnp.concatenate([gain1_grad, bias_grad, gain2_grad]).reshape(-1, 128))
    small = small.reshape(-1)
    return (
        layer_out.astype(jnp.bfloat16).reshape(batches, 1, token_count, width),
        input_grad.reshape(batches, 1, token_count, width),
        small[:width],
        qkv_share,
        small[width : width + qkv_width],
        out_share,
        small[width + qkv_width :],
        gate_up_share,
        down_share.reshape(-1),
    )


def fits(mesh):
    dp, ctx = mesh.shape["dp"], mesh.shape["ctx"]
    return dp % 2 == 0 and ctx % (dp // 2) == 0 and WIDTH % (dp * ctx) == 0 and FF % (dp * ctx) == 0


def solution(mesh):
    return jax.shard_map(
        short_body if fits(mesh) else body,
        mesh=mesh,
        in_specs=(
            P(None, "dp", "ctx", None),
            P(None, "dp", None),
            P(),
            P(("dp", "ctx")),
            P(),
            P(("dp", "ctx")),
            P(),
            P(("dp", "ctx")),
            P(("dp", "ctx")),
            P(None, "dp", "ctx", None),
        ),
        out_specs=(
            P(None, "dp", "ctx", None),
            P(None, "dp", "ctx", None),
            P(),
            P(("dp", "ctx")),
            P(),
            P(("dp", "ctx")),
            P(),
            P(("dp", "ctx")),
            P(("dp", "ctx")),
        ),
        check_vma=False,
    )
```

```python
import jax
import jax.numpy as jnp
from jax import lax
from jax.experimental import pallas as pl
from jax.experimental.pallas import tpu as pltpu
from jax.sharding import Mesh
from jax.sharding import PartitionSpec as P

QUERY_HEADS = 14
KEY_VALUE_HEADS = 2
HEAD_SIZE = 64
FF = 4864
WIDTH = 896


EPSILON = 1e-06
ROPE_THETA = 1000000.0
NEGATIVE = -1e30
CONTRACT_ROWS = (((0,), (0,)), ((), ()))
CONTRACT_COLS = (((1,), (1,)), ((), ()))


def doc_layout(lengths, first_row, token_count):
    token_index = first_row + jnp.arange(token_count, dtype=jnp.int32)
    doc_ends = jnp.cumsum(lengths, dtype=jnp.int32)
    before = doc_ends[None, :] <= token_index[:, None]
    document_index = jnp.sum(before.astype(jnp.int32), axis=1, dtype=jnp.int32)
    doc_start = jnp.sum(jnp.where(before, lengths[None, :], 0), axis=1, dtype=jnp.int32)
    return (token_index, document_index, token_index - doc_start)


def rotation(positions, head_dim):
    freqs = ROPE_THETA ** (-(2.0 * jnp.arange(head_dim // 2, dtype=jnp.float32)) / head_dim)
    angles = positions.astype(jnp.float32)[:, None] * freqs[None, :]
    cosine_table = jnp.concatenate([jnp.cos(angles), jnp.cos(angles)], axis=-1)
    sine_table = jnp.concatenate([jnp.sin(angles), jnp.sin(angles)], axis=-1)
    return (cosine_table[:, None, :], sine_table[:, None, :])


def rotary_apply(heads, cosine_table, sine_table):
    half_dim = heads.shape[-1] // 2
    turned = jnp.concatenate([-heads[..., half_dim:], heads[..., :half_dim]], axis=-1)
    return heads * cosine_table + turned * sine_table


def rotary_reverse(grads, cosine_table, sine_table):
    half_dim = grads.shape[-1] // 2
    weighted = grads * sine_table
    turned = jnp.concatenate([weighted[..., half_dim:], -weighted[..., :half_dim]], axis=-1)
    return grads * cosine_table + turned


def rms_forward(value_rows, gain):
    row_scale = lax.rsqrt(jnp.mean(value_rows * value_rows, axis=-1, keepdims=True) + EPSILON)
    normed = value_rows * row_scale
    return (normed, row_scale, normed * gain)


def rms_backward(grads, normed, row_scale, gain):
    grad_normed = grads * gain
    gain_grad = jnp.sum(grads * normed, axis=0)
    back = row_scale * (
        grad_normed - normed * jnp.mean(grad_normed * normed, axis=-1, keepdims=True)
    )
    return (back, gain_grad)


def block_scores(
    query_matrix, key_block, token_index, document_index, seg_block, key_start, score_scale
):
    score = (
        jnp.einsum("qhgd,khd->qhgk", query_matrix, key_block, preferred_element_type=jnp.float32)
        * score_scale
    )
    key_index = key_start + jnp.arange(key_block.shape[0], dtype=jnp.int32)
    allowed = (seg_block[None, :] == document_index[:, None]) & (
        key_index[None, :] <= token_index[:, None]
    )
    return (score, allowed[:, None, None, :])


def split_blocks(keyvals, key_segment, block_rows, kv_heads, head_dim):
    seq_length = keyvals.shape[0]
    block_count = seq_length // block_rows
    kv_blocks = keyvals.reshape(block_count, block_rows, 2, kv_heads, head_dim)
    seg_blocks = key_segment.reshape(block_count, block_rows)
    starts = jnp.arange(block_count, dtype=jnp.int32) * block_rows
    return (kv_blocks, seg_blocks, starts)


def attend_forward(query_matrix, token_index, document_index, keyvals, key_segment, block_rows):
    kv_heads, head_dim = (query_matrix.shape[1], query_matrix.shape[3])
    score_scale = head_dim ** (-0.5)
    kv_blocks, seg_blocks, starts = split_blocks(
        keyvals, key_segment, block_rows, kv_heads, head_dim
    )

    def stats_step(running, block_item):
        kv_block, seg_block, key_start = block_item
        row_max, row_sum = running
        score, allowed = block_scores(
            query_matrix,
            kv_block[:, 0],
            token_index,
            document_index,
            seg_block,
            key_start,
            score_scale,
        )
        new_max = jnp.maximum(row_max, jnp.max(jnp.where(allowed, score, NEGATIVE), axis=-1))
        weights = jnp.where(allowed, jnp.exp(score - new_max[..., None]), 0.0)
        return ((new_max, row_sum * jnp.exp(row_max - new_max) + jnp.sum(weights, axis=-1)), None)

    stats_init = (
        jnp.full(query_matrix.shape[:3], NEGATIVE, jnp.float32),
        jnp.zeros(query_matrix.shape[:3], jnp.float32),
    )
    (row_max, row_sum), unused = lax.scan(stats_step, stats_init, (kv_blocks, seg_blocks, starts))

    def out_step(running, block_item):
        kv_block, seg_block, key_start = block_item
        score, allowed = block_scores(
            query_matrix,
            kv_block[:, 0],
            token_index,
            document_index,
            seg_block,
            key_start,
            score_scale,
        )
        probability = jnp.where(
            allowed, jnp.exp(score - row_max[..., None]) / row_sum[..., None], 0.0
        )
        return (
            running
            + jnp.einsum(
                "qhgk,khd->qhgd",
                probability.astype(jnp.bfloat16),
                kv_block[:, 1],
                preferred_element_type=jnp.float32,
            ),
            None,
        )

    attended_rows, unused = lax.scan(
        out_step, jnp.zeros(query_matrix.shape, jnp.float32), (kv_blocks, seg_blocks, starts)
    )
    return (attended_rows, row_max, row_sum)


def attend_backward(
    query_matrix,
    token_index,
    document_index,
    keyvals,
    key_segment,
    row_max,
    row_sum,
    attention_gradient,
    delta,
    block_rows,
):
    kv_heads, head_dim = (query_matrix.shape[1], query_matrix.shape[3])
    score_scale = head_dim ** (-0.5)
    seq_length = keyvals.shape[0]
    kv_blocks, seg_blocks, starts = split_blocks(
        keyvals, key_segment, block_rows, kv_heads, head_dim
    )

    def grad_step(running, block_item):
        kv_block, seg_block, key_start = block_item
        grad_query = running
        score, allowed = block_scores(
            query_matrix,
            kv_block[:, 0],
            token_index,
            document_index,
            seg_block,
            key_start,
            score_scale,
        )
        probability = jnp.where(
            allowed, jnp.exp(score - row_max[..., None]) / row_sum[..., None], 0.0
        )
        grad_prob = jnp.einsum(
            "qhgd,khd->qhgk", attention_gradient, kv_block[:, 1], preferred_element_type=jnp.float32
        )
        grad_score = (probability * (grad_prob - delta[..., None])).astype(jnp.bfloat16)
        grad_query = (
            grad_query
            + jnp.einsum(
                "qhgk,khd->qhgd", grad_score, kv_block[:, 0], preferred_element_type=jnp.float32
            )
            * score_scale
        )
        key_gradient = (
            jnp.einsum(
                "qhgk,qhgd->khd", grad_score, query_matrix, preferred_element_type=jnp.float32
            )
            * score_scale
        )
        grad_value = jnp.einsum(
            "qhgk,qhgd->khd",
            probability.astype(jnp.bfloat16),
            attention_gradient,
            preferred_element_type=jnp.float32,
        )
        return (
            grad_query,
            jnp.concatenate(
                [key_gradient.reshape(block_rows, -1), grad_value.reshape(block_rows, -1)], axis=1
            ),
        )

    grad_query, grad_kv = lax.scan(
        grad_step, jnp.zeros(query_matrix.shape, jnp.float32), (kv_blocks, seg_blocks, starts)
    )
    return (grad_query, grad_kv.reshape(seq_length, 2 * kv_heads * head_dim))


def body(
    tokens,
    doc_lengths,
    attn_gain,
    qkv_weight,
    qkv_bias,
    out_weight,
    mlp_gain,
    gate_up_weight,
    down_weight,
    out_grad,
):
    model_width = attn_gain.shape[0]
    qkv_width = qkv_bias.shape[0]
    query_total_width = QUERY_HEADS * HEAD_SIZE
    key_value_width = KEY_VALUE_HEADS * HEAD_SIZE
    query_groups = QUERY_HEADS // KEY_VALUE_HEADS
    token_count = tokens.shape[2]
    seq_length = token_count * lax.axis_size("ctx")
    first_row = lax.axis_index("ctx") * token_count
    block_rows = min(512, seq_length)
    device_count = lax.axis_size(("dp", "ctx"))

    def unpack(gathered):
        flat_qkv, flat_out, flat_gate_up, flat_down = gathered
        return (
            flat_qkv.reshape(model_width, qkv_width),
            flat_out.reshape(query_total_width, model_width),
            flat_gate_up.reshape(model_width, 2 * FF),
            flat_down.reshape(FF, model_width),
        )

    grad_qkv = jnp.zeros((model_width, qkv_width), jnp.float32)
    grad_out = jnp.zeros((query_total_width, model_width), jnp.float32)
    grad_gate_up = jnp.zeros((model_width, 2 * FF), jnp.float32)
    grad_down = jnp.zeros((FF, model_width), jnp.float32)
    grad_gain1 = jnp.zeros((model_width,), jnp.float32)
    grad_gain2 = jnp.zeros((model_width,), jnp.float32)
    grad_bias = jnp.zeros((qkv_width,), jnp.float32)
    layer_outs = []
    input_grads = []
    for micro_step in range(tokens.shape[0]):
        w_qkv, w_out, w_gate_up, w_down = unpack(
            (
                lax.all_gather(qkv_weight, ("dp", "ctx"), axis=0, tiled=True),
                lax.all_gather(out_weight, ("dp", "ctx"), axis=0, tiled=True),
                lax.all_gather(gate_up_weight, ("dp", "ctx"), axis=0, tiled=True),
                lax.all_gather(down_weight, ("dp", "ctx"), axis=0, tiled=True),
            )
        )
        inputs = tokens[micro_step, 0].astype(jnp.float32)
        token_index, document_index, positions = doc_layout(
            doc_lengths[micro_step, 0], first_row, token_count
        )
        cosine_table, sine_table = rotation(positions, HEAD_SIZE)
        normed1, scale1, hidden1 = rms_forward(inputs, attn_gain)
        hidden1 = hidden1.astype(jnp.bfloat16)
        query_key_value = jnp.dot(hidden1, w_qkv, preferred_element_type=jnp.float32) + qkv_bias
        query_matrix = rotary_apply(
            query_key_value[:, :query_total_width].reshape(token_count, QUERY_HEADS, HEAD_SIZE),
            cosine_table,
            sine_table,
        )
        query_matrix = query_matrix.astype(jnp.bfloat16).reshape(
            token_count, KEY_VALUE_HEADS, query_groups, HEAD_SIZE
        )
        key_rows = rotary_apply(
            query_key_value[:, query_total_width : query_total_width + key_value_width].reshape(
                token_count, KEY_VALUE_HEADS, HEAD_SIZE
            ),
            cosine_table,
            sine_table,
        ).astype(jnp.bfloat16)
        value_rows = query_key_value[:, query_total_width + key_value_width :].astype(jnp.bfloat16)
        local_kv = jnp.concatenate(
            [key_rows.reshape(token_count, key_value_width), value_rows], axis=1
        )
        all_kv, all_segments = (
            lax.all_gather(local_kv, "ctx", axis=0, tiled=True),
            lax.all_gather(document_index, "ctx", axis=0, tiled=True),
        )
        attended_rows, row_max, row_sum = attend_forward(
            query_matrix, token_index, document_index, all_kv, all_segments, block_rows
        )
        att_low = attended_rows.reshape(token_count, query_total_width).astype(jnp.bfloat16)
        residual = inputs + jnp.dot(att_low, w_out, preferred_element_type=jnp.float32)
        normed2, scale2, hidden2 = rms_forward(residual, mlp_gain)
        hidden2 = hidden2.astype(jnp.bfloat16)
        gate_up = jnp.dot(hidden2, w_gate_up, preferred_element_type=jnp.float32)
        gate_part = gate_up[:, :FF]
        up_part = gate_up[:, FF:]
        sigmoid = jax.nn.sigmoid(gate_part)
        silu_gate = gate_part * sigmoid
        act_low = (silu_gate * up_part).astype(jnp.bfloat16)
        layer_outs.append(
            (residual + jnp.dot(act_low, w_down, preferred_element_type=jnp.float32)).astype(
                jnp.bfloat16
            )
        )
        back_qkv, back_out, back_gate_up, back_down = unpack(
            (
                lax.all_gather(qkv_weight, ("dp", "ctx"), axis=0, tiled=True),
                lax.all_gather(out_weight, ("dp", "ctx"), axis=0, tiled=True),
                lax.all_gather(gate_up_weight, ("dp", "ctx"), axis=0, tiled=True),
                lax.all_gather(down_weight, ("dp", "ctx"), axis=0, tiled=True),
            )
        )
        back_kv, back_segments = (
            lax.all_gather(local_kv, "ctx", axis=0, tiled=True),
            lax.all_gather(document_index, "ctx", axis=0, tiled=True),
        )
        cotangent = out_grad[micro_step, 0]
        grad_down = grad_down + lax.dot_general(
            act_low, cotangent, CONTRACT_ROWS, preferred_element_type=jnp.float32
        )
        grad_act = lax.dot_general(
            cotangent, back_down, CONTRACT_COLS, preferred_element_type=jnp.float32
        )
        grad_gate = grad_act * up_part * sigmoid * (1.0 + gate_part * (1.0 - sigmoid))
        grad_up = grad_act * silu_gate
        grad_gu = jnp.concatenate([grad_gate, grad_up], axis=1).astype(jnp.bfloat16)
        grad_gate_up = grad_gate_up + lax.dot_general(
            hidden2, grad_gu, CONTRACT_ROWS, preferred_element_type=jnp.float32
        )
        grad_hidden2 = lax.dot_general(
            grad_gu, back_gate_up, CONTRACT_COLS, preferred_element_type=jnp.float32
        )
        back_mlp, gain_part2 = rms_backward(grad_hidden2, normed2, scale2, mlp_gain)
        grad_gain2 = grad_gain2 + gain_part2
        grad_mid = cotangent.astype(jnp.float32) + back_mlp
        grad_mid_low = grad_mid.astype(jnp.bfloat16)
        grad_out = grad_out + lax.dot_general(
            att_low, grad_mid_low, CONTRACT_ROWS, preferred_element_type=jnp.float32
        )
        attention_gradient = lax.dot_general(
            grad_mid_low, back_out, CONTRACT_COLS, preferred_element_type=jnp.float32
        )
        attention_gradient = attention_gradient.astype(jnp.bfloat16).reshape(
            token_count, KEY_VALUE_HEADS, query_groups, HEAD_SIZE
        )
        delta = jnp.sum(attention_gradient.astype(jnp.float32) * attended_rows, axis=-1)
        grad_query, grad_kv = attend_backward(
            query_matrix,
            token_index,
            document_index,
            back_kv,
            back_segments,
            row_max,
            row_sum,
            attention_gradient,
            delta,
            block_rows,
        )
        owned_key_value = lax.psum_scatter(
            grad_kv.astype(jnp.bfloat16), "ctx", scatter_dimension=0, tiled=True
        ).astype(jnp.float32)
        key_gradient = rotary_reverse(
            owned_key_value[:, :key_value_width].reshape(token_count, KEY_VALUE_HEADS, HEAD_SIZE),
            cosine_table,
            sine_table,
        )
        grad_query = rotary_reverse(
            grad_query.reshape(token_count, QUERY_HEADS, HEAD_SIZE), cosine_table, sine_table
        )
        grad_qkv_low = jnp.concatenate(
            [
                grad_query.reshape(token_count, query_total_width),
                key_gradient.reshape(token_count, key_value_width),
                owned_key_value[:, key_value_width:],
            ],
            axis=1,
        ).astype(jnp.bfloat16)
        grad_bias = grad_bias + jnp.sum(grad_qkv_low.astype(jnp.float32), axis=0)
        grad_qkv = grad_qkv + lax.dot_general(
            hidden1, grad_qkv_low, CONTRACT_ROWS, preferred_element_type=jnp.float32
        )
        grad_hidden1 = lax.dot_general(
            grad_qkv_low, back_qkv, CONTRACT_COLS, preferred_element_type=jnp.float32
        )
        back_attn, gain_part1 = rms_backward(grad_hidden1, normed1, scale1, attn_gain)
        grad_gain1 = grad_gain1 + gain_part1
        input_grads.append(grad_mid + back_attn)
    grad_list = (grad_qkv, grad_out, grad_gate_up, grad_down)
    widths = [item.size // device_count for item in grad_list]
    stacked = jnp.concatenate([item.reshape(device_count, -1) for item in grad_list], axis=1)
    mine = lax.psum_scatter(stacked, ("dp", "ctx"), scatter_dimension=0, tiled=True).reshape(-1)
    offsets = [0, widths[0], widths[0] + widths[1], widths[0] + widths[1] + widths[2]]
    shares = [mine[offsets[k] : offsets[k] + widths[k]] for k in range(4)]
    small_sums = lax.psum((grad_gain1, grad_bias, grad_gain2), ("dp", "ctx"))
    return (
        jnp.stack(layer_outs)[:, None],
        jnp.stack(input_grads)[:, None],
        small_sums[0],
        shares[0],
        small_sums[1],
        shares[1],
        small_sums[2],
        shares[2],
        shares[3],
    )


def together(*items):
    return lax.optimization_barrier(items)


class Links:
    def __init__(self):
        self.rows, self.cores = lax.axis_size("y"), lax.axis_size("core")
        self.deep, self.wide = lax.axis_size("z"), lax.axis_size("x")
        self.dp, self.ctx = self.rows * self.cores, self.deep * self.wide
        self.y, self.core = lax.axis_index("y"), lax.axis_index("core")
        self.z, self.x = lax.axis_index("z"), lax.axis_index("x")
        self.me_dp, self.me_ctx = lax.axis_index(("y", "core")), lax.axis_index(("z", "x"))

    def shift(self, item, axis, step=1):
        size = lax.axis_size(axis)
        if step % size == 0:
            return item
        return lax.ppermute(item, axis, [(k, (k + step) % size) for k in range(size)])

    def core_step(self, item):
        return self.shift(item, "core")

    def y_step(self, item, step=1):
        return self.shift(item, "y", step)

    def broadcast(self, item, axes):
        copies = jnp.broadcast_to(item, (lax.axis_size(axes), *item.shape))
        return lax.all_to_all(copies, axes, 0, 0)

    def spread_x(self, part):
        return [self.shift(part, "x", step) for step in range(self.wide)]

    def ring_x(self, held, moving):
        return [old + self.spread_x(item) for old, item in zip(held, moving, strict=True)]

    def ring_z(self, moving):
        return tuple(self.shift(item, "z") for item in moving)

    def near_dp(self):
        return [
            (self.y - far) % self.rows * self.cores + (self.core - core) % self.cores
            for far in range(self.rows)
            for core in range(self.cores)
        ]

    def near_ctx(self):
        return [
            (self.z - back) % self.deep * self.wide + (self.x - across) % self.wide
            for back in range(self.deep)
            for across in range(self.wide)
        ]

    def scatter_near(self, parts):
        return jnp.sum(lax.all_to_all(parts, ("z", "x"), 0, 0).astype(jnp.float32), axis=0)

    def sum_x(self, parts):
        total = parts[0].astype(jnp.float32)
        for across in range(1, self.wide):
            total = total + self.shift(parts[across], "x", -across).astype(jnp.float32)
        return total

    def gather_y(self, item):
        return jnp.stack([item] + [self.y_step(item, step) for step in range(1, self.rows)])

    def gather_core(self, near):
        pair = jnp.stack([near, self.core_step(near)])
        order = [
            ((self.core - dp) % 2) * self.rows + (self.y - dp // 2) % self.rows
            for dp in range(self.dp)
        ]
        pair = pair.reshape(self.dp, *near.shape[1:])
        return jnp.stack([lax.dynamic_index_in_dim(pair, k, 0, False) for k in order])

    def scatter_core(self, whole):
        split = whole.reshape(self.rows, 2, *whole.shape[1:])
        mine = lax.dynamic_index_in_dim(split, self.core, 1, False)
        other = self.core_step(lax.dynamic_index_in_dim(split, 1 - self.core, 1, False))
        return mine.astype(jnp.float32) + other.astype(jnp.float32)

    def scatter_y(self, pair, low):
        total = lax.dynamic_index_in_dim(pair, self.y, 0, False)
        for step in range(1, self.rows):
            part = lax.dynamic_index_in_dim(pair, (self.y + step) % self.rows, 0, False)
            total = total + self.y_step(part.astype(low), step).astype(jnp.float32)
        return total

    def exchange_dp(self, whole):
        came = []
        for far in range(self.rows):
            for core in range(self.cores):
                to_y, to_core = (self.y + far) % self.rows, (self.core + core) % self.cores
                part = lax.dynamic_index_in_dim(whole, to_y * self.cores + to_core, 0, False)
                size = self.dp
                pairs = []
                for k in range(size):
                    there = (k // self.cores + far) % self.rows * self.cores
                    pairs.append((k, there + (k + core) % self.cores))
                came.append(lax.ppermute(part, ("y", "core"), pairs) if far or core else part)
        return came

    def hand_back(self, parts):
        came = []
        for far in range(self.rows):
            for core in range(self.cores):
                pairs = []
                for k in range(self.dp):
                    there = (k // self.cores - far) % self.rows * self.cores
                    pairs.append((k, there + (k - core) % self.cores))
                part = parts[far * self.cores + core]
                came.append(lax.ppermute(part, ("y", "core"), pairs) if far or core else part)
        came = jnp.stack(came)
        order = [
            (dp // self.cores - self.y) % self.rows * self.cores + (dp - self.core) % self.cores
            for dp in range(self.dp)
        ]
        return [lax.dynamic_index_in_dim(came, k, 0, False) for k in order]

    def sum_all(self, item):
        for axis in ("core", "y", "x", "z"):
            step, size = 1, lax.axis_size(axis)
            while step < size:
                pairs = [(k, k ^ step) for k in range(size)]
                item = item + lax.ppermute(item, axis, pairs)
                step *= 2
        return item


def allowed_bias(slot_ref, low_ref, first_ref, bias_ref):
    tokens = bias_ref.shape[1]
    query = first_ref[0] + lax.broadcasted_iota(jnp.int32, (tokens, tokens), 1)
    for slot in range(bias_ref.shape[0] // tokens):
        keys = slot_ref[slot] * tokens + lax.broadcasted_iota(jnp.int32, (tokens, tokens), 0)
        allowed = (keys >= low_ref[...]) & (keys <= query)
        bias_ref[slot * tokens : (slot + 1) * tokens, :] = jnp.where(allowed, 0.0, NEGATIVE)


def head_rows(ref, head):
    return ref[head * HEAD_SIZE : (head + 1) * HEAD_SIZE, :]


def attention_kernel(slot_ref, first_ref, low_ref, q_ref, kv_ref, att_ref, stat_ref, bias_ref):
    allowed_bias(slot_ref, low_ref, first_ref, bias_ref)
    kv_cols = jnp.concatenate([kv_ref[j] for j in range(kv_ref.shape[0])], axis=1)
    groups = QUERY_HEADS // KEY_VALUE_HEADS
    half = KEY_VALUE_HEADS * HEAD_SIZE
    key_rows = kv_cols[:half].T
    for kv_head in range(KEY_VALUE_HEADS):
        key = key_rows[:, kv_head * HEAD_SIZE : (kv_head + 1) * HEAD_SIZE]
        value = kv_cols[half + kv_head * HEAD_SIZE : half + (kv_head + 1) * HEAD_SIZE]
        for head in range(kv_head * groups, (kv_head + 1) * groups):
            score = jnp.dot(key, head_rows(q_ref, head), preferred_element_type=jnp.float32)
            score = score * HEAD_SIZE ** (-0.5) + bias_ref[...]
            top = jnp.max(score, axis=0, keepdims=True)
            weights = jnp.exp(score - top)
            total = jnp.sum(weights, axis=0, keepdims=True)
            out = jnp.dot(value, weights.astype(jnp.bfloat16), preferred_element_type=jnp.float32)
            att_ref[head * HEAD_SIZE : (head + 1) * HEAD_SIZE, :] = out / total
            stat_ref[head : head + 1, :] = top + jnp.log(total)


def attention_back_kernel(
    slot_ref,
    first_ref,
    low_ref,
    q_ref,
    kv_ref,
    att_ref,
    stat_ref,
    datt_ref,
    dq_ref,
    dkv_ref,
    bias_ref,
    qs_ref,
    das_ref,
    ds_ref,
    p_ref,
):
    allowed_bias(slot_ref, low_ref, first_ref, bias_ref)
    kv_cols = jnp.concatenate([kv_ref[j] for j in range(kv_ref.shape[0])], axis=1)
    tokens = q_ref.shape[1]
    groups = QUERY_HEADS // KEY_VALUE_HEADS
    half = KEY_VALUE_HEADS * HEAD_SIZE
    scale = HEAD_SIZE ** (-0.5)
    rows = kv_cols.T
    results = []
    for kv_head in range(KEY_VALUE_HEADS):
        own = slice(kv_head * HEAD_SIZE, (kv_head + 1) * HEAD_SIZE)
        key = rows[:, own]
        value = rows[:, half + kv_head * HEAD_SIZE : half + (kv_head + 1) * HEAD_SIZE]
        key_cols = kv_cols[own]
        for place in range(groups):
            head = kv_head * groups + place
            lanes = slice(place * tokens, (place + 1) * tokens)
            query = head_rows(q_ref, head)
            datt = head_rows(datt_ref, head)
            qs_ref[:, lanes] = query
            das_ref[:, lanes] = datt
            delta = jnp.sum(
                datt.astype(jnp.float32) * head_rows(att_ref, head), axis=0, keepdims=True
            )
            score = jnp.dot(key, query, preferred_element_type=jnp.float32)
            prob = jnp.exp(score * scale + bias_ref[...] - stat_ref[head : head + 1, :])
            dprob = jnp.dot(value, datt, preferred_element_type=jnp.float32)
            dscore = (prob * (dprob - delta)).astype(jnp.bfloat16)
            ds_ref[:, lanes] = dscore
            p_ref[:, lanes] = prob.astype(jnp.bfloat16)
            dq_ref[head * HEAD_SIZE : (head + 1) * HEAD_SIZE, :] = (
                jnp.dot(key_cols, dscore, preferred_element_type=jnp.float32) * scale
            )
        results.append(
            lax.dot_general(
                ds_ref[...], qs_ref[...], CONTRACT_COLS, preferred_element_type=jnp.float32
            )
            * scale
        )
        results.append(
            lax.dot_general(
                p_ref[...], das_ref[...], CONTRACT_COLS, preferred_element_type=jnp.float32
            )
        )
    order = results[0::2] + results[1::2]
    out = jnp.concatenate(order, axis=1).astype(jnp.bfloat16)
    for j in range(dkv_ref.shape[0]):
        dkv_ref[j] = out[j * tokens : (j + 1) * tokens]


def attention_specs(width, pieces, kv_width, tokens):
    smem = pl.BlockSpec(memory_space=pltpu.SMEM)
    low = pl.BlockSpec((pl.Squeezed(), 1, tokens), lambda mb: (mb, 0, 0))
    cols = pl.BlockSpec((width, tokens), lambda mb: (0, mb))
    kv = pl.BlockSpec((pieces, kv_width, tokens), lambda mb: (0, 0, mb))
    stat = pl.BlockSpec((QUERY_HEADS, tokens), lambda mb: (0, mb))
    return smem, low, cols, kv, stat


def attend(slots, first, low, q_cols, kv_all, batches):
    width, total = q_cols.shape
    tokens = total // batches
    pieces, kv_width, _ = kv_all.shape
    smem, low_spec, cols, kv, stat = attention_specs(width, pieces, kv_width, tokens)
    return pl.pallas_call(
        attention_kernel,
        grid=(batches,),
        in_specs=[smem, smem, low_spec, cols, kv],
        out_specs=[cols, stat],
        out_shape=[
            jax.ShapeDtypeStruct((width, total), jnp.float32),
            jax.ShapeDtypeStruct((QUERY_HEADS, total), jnp.float32),
        ],
        scratch_shapes=[pltpu.VMEM((pieces * tokens, tokens), jnp.float32)],
        compiler_params=pltpu.CompilerParams(vmem_limit_bytes=40 * 2**20),
        cost_estimate=pl.CostEstimate(
            flops=4 * total * pieces * tokens * width,
            bytes_accessed=8 * total * width,
            transcendentals=total * pieces * tokens * QUERY_HEADS,
        ),
        name="attention",
    )(slots, first, low, q_cols, kv_all)


def attend_back(slots, first, low, q_cols, kv_all, att_cols, stats, datt_cols, batches):
    width, total = q_cols.shape
    tokens = total // batches
    pieces, kv_width, _ = kv_all.shape
    groups = QUERY_HEADS // KEY_VALUE_HEADS
    keys = pieces * tokens
    smem, low_spec, cols, kv, stat = attention_specs(width, pieces, kv_width, tokens)
    return pl.pallas_call(
        attention_back_kernel,
        grid=(batches,),
        in_specs=[smem, smem, low_spec, cols, kv, cols, stat, cols],
        out_specs=[
            cols,
            pl.BlockSpec((pieces, pl.Squeezed(), tokens, kv_width), lambda mb: (0, mb, 0, 0)),
        ],
        out_shape=[
            jax.ShapeDtypeStruct((width, total), jnp.float32),
            jax.ShapeDtypeStruct((pieces, batches, tokens, kv_width), jnp.bfloat16),
        ],
        scratch_shapes=[
            pltpu.VMEM((keys, tokens), jnp.float32),
            pltpu.VMEM((HEAD_SIZE, groups * tokens), jnp.bfloat16),
            pltpu.VMEM((HEAD_SIZE, groups * tokens), jnp.bfloat16),
            pltpu.VMEM((keys, groups * tokens), jnp.bfloat16),
            pltpu.VMEM((keys, groups * tokens), jnp.bfloat16),
        ],
        compiler_params=pltpu.CompilerParams(vmem_limit_bytes=48 * 2**20),
        cost_estimate=pl.CostEstimate(
            flops=10 * total * keys * width,
            bytes_accessed=14 * total * width,
            transcendentals=total * keys * QUERY_HEADS,
        ),
        name="attention_back",
    )(slots, first, low, q_cols, kv_all, att_cols, stats, datt_cols)


def one_hot_order(order, size):
    rows = lax.broadcasted_iota(jnp.int32, (size, order.shape[0]), 0)
    return (rows == order[None, :]).astype(jnp.bfloat16)


def dot32(left, right, dims=(((1,), (0,)), ((), ()))):
    return lax.dot_general(left, right, dims, preferred_element_type=jnp.float32)


def rope_columns(cols, cosine, sine):
    first, second = cols[:, 0], cols[:, 1]
    return jnp.stack([first * cosine - second * sine, second * cosine + first * sine], axis=1)


def rope_columns_back(cols, cosine, sine):
    first, second = cols[:, 0], cols[:, 1]
    return jnp.stack([first * cosine + second * sine, second * cosine - first * sine], axis=1)


def short_body(
    tokens,
    doc_lengths,
    attn_gain,
    qkv_weight,
    qkv_bias,
    out_weight,
    mlp_gain,
    gate_up_weight,
    down_weight,
    out_grad,
):
    links = Links()
    width = attn_gain.shape[0]
    qkv_width = qkv_bias.shape[0]
    query_width = QUERY_HEADS * HEAD_SIZE
    kv_width = KEY_VALUE_HEADS * HEAD_SIZE
    half = HEAD_SIZE // 2
    batches, token_count = tokens.shape[0], tokens.shape[2]
    total = batches * token_count
    devices = links.dp * links.ctx
    piece = width // devices
    own_ff = FF // links.dp
    first_row = links.me_ctx * token_count

    padded = -(-piece // 16) * 16
    key_slots = jnp.stack(
        [
            z * links.wide + (links.x - across) % links.wide
            for across in range(links.wide)
            for z in range(links.deep)
        ]
    ).astype(jnp.int32)
    row = jnp.arange(padded, dtype=jnp.int32)
    near_dp = jnp.stack(links.near_dp()).astype(jnp.int32)
    near_ctx = jnp.stack(links.near_ctx()).astype(jnp.int32)
    rows_order = near_dp.reshape(links.rows, 2).T.reshape(-1)
    owner = rows_order[:, None] * links.ctx + jnp.arange(links.ctx, dtype=jnp.int32)[None, :]
    attn_order = jnp.where(row < piece, owner[:, :, None] * piece + row, -1).reshape(-1)
    attn_pick = one_hot_order(attn_order, width)
    owner = near_dp[None, :] * links.ctx + near_ctx[:, None]
    mlp_order = (owner[:, :, None] * piece + jnp.arange(piece, dtype=jnp.int32)).reshape(-1)
    mlp_pick = one_hot_order(mlp_order, width)

    def own_rows(flat, columns):
        return jnp.pad(flat.reshape(piece, columns), ((0, padded - piece), (0, 0)))

    def rows_y(near):
        return jnp.concatenate([near] + [links.y_step(near, k) for k in range(1, links.rows)])

    def rows_core(held):
        return jnp.concatenate([held, links.core_step(held)])

    def back_core(grad):
        mine, other = jnp.split(grad, 2)
        return mine.astype(jnp.float32) + links.core_step(other).astype(jnp.float32)

    def back_y(pair):
        parts = jnp.split(pair, links.rows)
        total = parts[0]
        for step in range(1, links.rows):
            there = links.y_step(parts[step].astype(jnp.bfloat16), -step)
            total = total + there.astype(jnp.float32)
        return total.astype(jnp.bfloat16).reshape(links.ctx, padded, -1)

    w_qkv = links.broadcast(own_rows(qkv_weight, qkv_width), ("z", "x")).reshape(-1, qkv_width)
    gate_up_rows = gate_up_weight.reshape(piece, 2, links.dp, own_ff)
    gate_up_rows = gate_up_rows.transpose(2, 0, 1, 3).reshape(links.dp, piece, 2 * own_ff)
    parts = links.exchange_dp(gate_up_rows)
    w_qkv, *parts = together(w_qkv, *parts)

    w_qkv = rows_y(w_qkv)
    moving = (
        jnp.stack(parts).reshape(links.dp * piece, 2 * own_ff),
        down_weight.reshape(-1, width),
    )
    held = links.ring_x([[], []], moving)
    moving = links.ring_z(moving)
    w_out = links.broadcast(own_rows(out_weight, width), ("z", "x")).reshape(-1, width)
    w_qkv, w_out, moving, held = together(w_qkv, w_out, moving, held)

    w_qkv = rows_core(w_qkv)

    cotangent = out_grad[:, 0].reshape(total, width)

    inputs = tokens[:, 0].reshape(total, width).astype(jnp.float32)
    layouts = [doc_layout(doc_lengths[b, 0], first_row, token_count) for b in range(batches)]
    token_index = layouts[0][0]
    positions = jnp.concatenate([item[2] for item in layouts])
    low = jnp.stack([token_index - item[2] for item in layouts])[:, None, :]
    first = jnp.reshape(first_row, (1,)).astype(jnp.int32)
    freqs = ROPE_THETA ** (-(2.0 * jnp.arange(half, dtype=jnp.float32)) / HEAD_SIZE)
    angles = freqs[:, None] * positions.astype(jnp.float32)[None, :]
    cosine, sine = jnp.cos(angles), jnp.sin(angles)

    normed1, scale1, hidden1 = rms_forward(inputs, attn_gain)
    hidden1 = dot32(hidden1.astype(jnp.bfloat16), attn_pick).astype(jnp.bfloat16)
    qkv_cols = dot32(w_qkv, hidden1, (((0,), (1,)), ((), ()))) + qkv_bias[:, None]
    turned = rope_columns(
        qkv_cols[: query_width + kv_width].reshape(-1, 2, half, total), cosine, sine
    )
    turned = turned.reshape(query_width + kv_width, total).astype(jnp.bfloat16)
    q_cols = turned[:query_width]
    kv_cols = jnp.concatenate(
        [turned[query_width:], qkv_cols[query_width + kv_width :].astype(jnp.bfloat16)]
    )
    kv_cols, moving = together(kv_cols, moving)
    kv_all = links.broadcast(kv_cols, "z")
    held = links.ring_x(held, moving)
    kv_all, w_out, moving, held = together(kv_all, w_out, moving, held)

    kv_all = jnp.concatenate(links.spread_x(kv_all))
    w_out = rows_y(w_out)
    for step in range(2, links.deep - 1):
        moving = links.ring_z(moving)
        if step > 2:
            held = links.ring_x(held, moving)
    kv_all, w_out, moving, cotangent = together(kv_all, w_out, moving, cotangent)

    w_out = rows_core(w_out)
    all_cotangent = links.gather_y(cotangent)
    held = links.ring_x(held, moving)
    moving = links.ring_z(moving)
    att_cols, stats = attend(key_slots, first, low, q_cols, kv_all, batches)
    att_cols, w_out, all_cotangent, moving = together(att_cols, w_out, all_cotangent, moving)

    att_low = dot32(
        att_cols.astype(jnp.bfloat16), attn_pick, (((0,), (0,)), ((), ()))
    ).astype(jnp.bfloat16)
    residual = inputs + dot32(att_low, w_out)

    normed2, scale2, hidden2 = rms_forward(residual, mlp_gain)
    all_hidden2 = links.gather_y(hidden2.astype(jnp.bfloat16))
    w_parts, down_parts = links.ring_x(held, moving)
    w_gate_up = jnp.concatenate(w_parts)
    w_down = jnp.zeros((links.ctx, own_ff // links.ctx, width), jnp.bfloat16)
    for k, part in enumerate(down_parts):
        w_down = lax.dynamic_update_index_in_dim(w_down, part, near_ctx[k], 0)
    w_down = w_down.reshape(own_ff, width)
    all_cotangent = links.gather_core(all_cotangent).reshape(links.dp * total, width)
    all_hidden2, w_gate_up, w_down, all_cotangent = together(
        all_hidden2, w_gate_up, w_down, all_cotangent
    )
    all_hidden2 = links.gather_core(all_hidden2).reshape(links.dp * total, width)
    all_hidden2 = dot32(all_hidden2, mlp_pick).astype(jnp.bfloat16)
    gate_up = dot32(all_hidden2, w_gate_up)
    gate, up = gate_up[:, :own_ff], gate_up[:, own_ff:]
    sigmoid = jax.nn.sigmoid(gate)
    silu = gate * sigmoid
    act_low = (silu * up).astype(jnp.bfloat16)
    dact = dot32(all_cotangent, w_down, CONTRACT_COLS)
    dgate = dact * up * sigmoid * (1.0 + gate * (1.0 - sigmoid))
    dgu = jnp.concatenate([dgate, dact * silu], axis=1).astype(jnp.bfloat16)
    dhidden2 = dot32(dgu, w_gate_up, CONTRACT_COLS).astype(jnp.bfloat16)
    dhidden2 = dot32(dhidden2, mlp_pick, CONTRACT_COLS).astype(jnp.bfloat16)
    dhidden2, dgu, act_low = together(dhidden2, dgu, act_low)

    dhidden2 = links.scatter_core(dhidden2.reshape(links.dp, total, width))
    grad_gate_up = dot32(all_hidden2, dgu, CONTRACT_ROWS).astype(jnp.bfloat16)
    grad_down = dot32(act_low, all_cotangent, CONTRACT_ROWS).astype(jnp.bfloat16)
    dhidden2, grad_gate_up, grad_down, act_low = together(
        dhidden2, grad_gate_up, grad_down, act_low
    )

    blocks = grad_gate_up.reshape(links.deep, links.wide, -1, 2 * own_ff)
    down_blocks = grad_down.reshape(links.ctx, own_ff // links.ctx, width)

    def across(blocks, back):
        gate_up_blocks, down_blocks = blocks
        places = [near_ctx[back * links.wide + step] for step in range(links.wide)]
        down = [lax.dynamic_index_in_dim(down_blocks, k, 0, False) for k in places]
        return links.sum_x(gate_up_blocks[back]), links.sum_x(down)

    def lowered(share):
        return [item.astype(jnp.bfloat16) for item in share]

    def plus(share, moved):
        return tuple(a + b.astype(jnp.float32) for a, b in zip(share, moved, strict=True))

    def ring(share, other):
        return plus(other, links.ring_z(lowered(share)))

    blocks = (blocks, down_blocks)
    share = across(blocks, 1)
    dhidden2 = links.scatter_y(dhidden2, jnp.bfloat16)
    out_part = dot32(act_low, w_down).astype(jnp.bfloat16)
    share, blocks, dhidden2, out_part = together(share, blocks, dhidden2, out_part)

    back_mlp, gain2_grad = rms_backward(dhidden2, normed2, scale2, mlp_gain)
    dmid = cotangent.astype(jnp.float32) + back_mlp
    dmid_low = dmid.astype(jnp.bfloat16)
    datt = dot32(dmid_low, w_out, CONTRACT_COLS).astype(jnp.bfloat16)
    datt_cols = dot32(attn_pick, datt, CONTRACT_COLS).astype(jnp.bfloat16)
    grad_out = dot32(att_low, dmid_low, CONTRACT_ROWS).astype(jnp.bfloat16)
    share = ring(share, across(blocks, 2))
    out_part = links.scatter_core(out_part.reshape(links.dp, total, width))
    grad_out = back_core(grad_out)
    dq_cols, dkv = attend_back(
        key_slots, first, low, q_cols, kv_all, att_cols, stats, datt_cols, batches
    )
    dq_cols, dkv, share, blocks, grad_out, out_part = together(
        dq_cols, dkv, share, blocks, grad_out, out_part
    )

    dkv = dkv.reshape(links.wide, links.deep, total, 2 * kv_width)
    dkv = links.sum_x(dkv).astype(jnp.bfloat16)
    for back in range(3, links.deep - 1):
        share = ring(share, across(blocks, back))
    share = links.ring_z(lowered(share))
    dkv, share, blocks = together(dkv, share, blocks)

    own_dkv = jnp.sum(lax.all_to_all(dkv, "z", 0, 0).astype(jnp.float32), axis=0).T
    share = plus(across(blocks, links.deep - 1), share)
    dq = rope_columns_back(dq_cols.reshape(-1, 2, half, total), cosine, sine)
    dq = dq.reshape(query_width, total).astype(jnp.bfloat16)
    grad_q = back_core(dot32(hidden1, dq, (((0,), (1,)), ((), ()))).astype(jnp.bfloat16))
    grad_out = back_y(grad_out)
    own_dkv, grad_q, grad_out, share, blocks = together(
        own_dkv, grad_q, grad_out, share, blocks
    )

    grad_q = back_y(grad_q)
    share = ring(share, across(blocks, 0))
    dk = rope_columns_back(own_dkv[:kv_width].reshape(-1, 2, half, total), cosine, sine)
    dkv = jnp.concatenate([dk.reshape(kv_width, total), own_dkv[kv_width:]]).astype(jnp.bfloat16)
    grad_kv = dot32(hidden1, dkv, (((0,), (1,)), ((), ()))).astype(jnp.bfloat16)
    grad_kv = back_core(grad_kv)
    grad_q, grad_kv, share, out_part, dq, dkv = together(
        grad_q, grad_kv, share, out_part, dq, dkv
    )

    grad_kv = back_y(grad_kv)
    grad_q = links.scatter_near(jnp.concatenate([grad_q, grad_out], axis=2))[:piece]
    layer_out = residual + links.scatter_y(out_part, jnp.bfloat16)
    dqkv = jnp.concatenate([dq, dkv])
    bias_grad = jnp.sum(dqkv.astype(jnp.float32), axis=1)
    dhidden1 = dot32(dqkv, w_qkv, (((0,), (1,)), ((), ())))
    top = dhidden1.astype(jnp.bfloat16)
    rest = (dhidden1 - top.astype(jnp.float32)).astype(jnp.bfloat16)
    dhidden1 = dot32(top, attn_pick, CONTRACT_COLS) + dot32(rest, attn_pick, CONTRACT_COLS)
    back_attn, gain1_grad = rms_backward(dhidden1, normed1, scale1, attn_gain)
    input_grad = dmid + back_attn
    share, down_share = share
    parts = share.astype(jnp.bfloat16).reshape(links.dp, piece, 2 * own_ff)
    parts = jnp.stack(links.hand_back(parts)).reshape(links.dp, piece, 2, own_ff)
    parts, grad_kv, grad_q, gain1_grad = together(parts, grad_kv, grad_q, gain1_grad)

    gate_up_share = parts.transpose(1, 2, 0, 3).astype(jnp.float32).reshape(-1)
    grad_kv = links.scatter_near(grad_kv)[:piece]
    qkv_share = jnp.concatenate([grad_q[:, :query_width], grad_kv], axis=1).reshape(-1)
    out_share = grad_q[:, query_width:].reshape(-1)
    small = links.sum_all(jnp.concatenate([gain1_grad, bias_grad, gain2_grad]).reshape(-1, 128))
    small = small.reshape(-1)
    return (
        layer_out.astype(jnp.bfloat16).reshape(batches, 1, token_count, width),
        input_grad.reshape(batches, 1, token_count, width),
        small[:width],
        qkv_share,
        small[width : width + qkv_width],
        out_share,
        small[width + qkv_width :],
        gate_up_share,
        down_share.reshape(-1),
    )


def fits(mesh):
    dp, ctx = mesh.shape["dp"], mesh.shape["ctx"]
    devices = dp * ctx
    if dp % 2 or ctx % (dp // 2) or ctx // (dp // 2) < 3:
        return False
    return WIDTH % devices == 0 and FF % devices == 0


def solution(mesh):
    run, dp, ctx = body, ("dp",), ("ctx",)
    if fits(mesh):
        rows = mesh.shape["dp"] // 2
        shape = (rows, 2, mesh.shape["ctx"] // rows, rows)
        run, dp, ctx = short_body, ("y", "core"), ("z", "x")
        mesh = Mesh(mesh.devices.reshape(shape), (*dp, *ctx))
    return jax.shard_map(
        run,
        mesh=mesh,
        in_specs=(
            P(None, dp, ctx, None),
            P(None, dp, None),
            P(),
            P((*dp, *ctx)),
            P(),
            P((*dp, *ctx)),
            P(),
            P((*dp, *ctx)),
            P((*dp, *ctx)),
            P(None, dp, ctx, None),
        ),
        out_specs=(
            P(None, dp, ctx, None),
            P(None, dp, ctx, None),
            P(),
            P((*dp, *ctx)),
            P(),
            P((*dp, *ctx)),
            P(),
            P((*dp, *ctx)),
            P((*dp, *ctx)),
        ),
        check_vma=False,
    )
```

```python
import jax
import jax.numpy as jnp
from jax import lax
from jax.experimental import pallas as pl
from jax.experimental.pallas import tpu as pltpu
from jax.sharding import Mesh
from jax.sharding import PartitionSpec as P

QUERY_HEADS = 14
KEY_VALUE_HEADS = 2
HEAD_SIZE = 64
FF = 4864
WIDTH = 896


EPSILON = 1e-06
ROPE_THETA = 1000000.0
NEGATIVE = -1e30
CONTRACT_ROWS = (((0,), (0,)), ((), ()))
CONTRACT_COLS = (((1,), (1,)), ((), ()))


def doc_layout(lengths, first_row, token_count):
    token_index = first_row + jnp.arange(token_count, dtype=jnp.int32)
    doc_ends = jnp.cumsum(lengths, dtype=jnp.int32)
    before = doc_ends[None, :] <= token_index[:, None]
    document_index = jnp.sum(before.astype(jnp.int32), axis=1, dtype=jnp.int32)
    doc_start = jnp.sum(jnp.where(before, lengths[None, :], 0), axis=1, dtype=jnp.int32)
    return (token_index, document_index, token_index - doc_start)


def rotation(positions, head_dim):
    freqs = ROPE_THETA ** (-(2.0 * jnp.arange(head_dim // 2, dtype=jnp.float32)) / head_dim)
    angles = positions.astype(jnp.float32)[:, None] * freqs[None, :]
    cosine_table = jnp.concatenate([jnp.cos(angles), jnp.cos(angles)], axis=-1)
    sine_table = jnp.concatenate([jnp.sin(angles), jnp.sin(angles)], axis=-1)
    return (cosine_table[:, None, :], sine_table[:, None, :])


def rotary_apply(heads, cosine_table, sine_table):
    half_dim = heads.shape[-1] // 2
    turned = jnp.concatenate([-heads[..., half_dim:], heads[..., :half_dim]], axis=-1)
    return heads * cosine_table + turned * sine_table


def rotary_reverse(grads, cosine_table, sine_table):
    half_dim = grads.shape[-1] // 2
    weighted = grads * sine_table
    turned = jnp.concatenate([weighted[..., half_dim:], -weighted[..., :half_dim]], axis=-1)
    return grads * cosine_table + turned


def rms_forward(value_rows, gain):
    row_scale = lax.rsqrt(jnp.mean(value_rows * value_rows, axis=-1, keepdims=True) + EPSILON)
    normed = value_rows * row_scale
    return (normed, row_scale, normed * gain)


def rms_backward(grads, normed, row_scale, gain):
    grad_normed = grads * gain
    gain_grad = jnp.sum(grads * normed, axis=0)
    back = row_scale * (
        grad_normed - normed * jnp.mean(grad_normed * normed, axis=-1, keepdims=True)
    )
    return (back, gain_grad)


def block_scores(
    query_matrix, key_block, token_index, document_index, seg_block, key_start, score_scale
):
    score = (
        jnp.einsum("qhgd,khd->qhgk", query_matrix, key_block, preferred_element_type=jnp.float32)
        * score_scale
    )
    key_index = key_start + jnp.arange(key_block.shape[0], dtype=jnp.int32)
    allowed = (seg_block[None, :] == document_index[:, None]) & (
        key_index[None, :] <= token_index[:, None]
    )
    return (score, allowed[:, None, None, :])


def split_blocks(keyvals, key_segment, block_rows, kv_heads, head_dim):
    seq_length = keyvals.shape[0]
    block_count = seq_length // block_rows
    kv_blocks = keyvals.reshape(block_count, block_rows, 2, kv_heads, head_dim)
    seg_blocks = key_segment.reshape(block_count, block_rows)
    starts = jnp.arange(block_count, dtype=jnp.int32) * block_rows
    return (kv_blocks, seg_blocks, starts)


def attend_forward(query_matrix, token_index, document_index, keyvals, key_segment, block_rows):
    kv_heads, head_dim = (query_matrix.shape[1], query_matrix.shape[3])
    score_scale = head_dim ** (-0.5)
    kv_blocks, seg_blocks, starts = split_blocks(
        keyvals, key_segment, block_rows, kv_heads, head_dim
    )

    def stats_step(running, block_item):
        kv_block, seg_block, key_start = block_item
        row_max, row_sum = running
        score, allowed = block_scores(
            query_matrix,
            kv_block[:, 0],
            token_index,
            document_index,
            seg_block,
            key_start,
            score_scale,
        )
        new_max = jnp.maximum(row_max, jnp.max(jnp.where(allowed, score, NEGATIVE), axis=-1))
        weights = jnp.where(allowed, jnp.exp(score - new_max[..., None]), 0.0)
        return ((new_max, row_sum * jnp.exp(row_max - new_max) + jnp.sum(weights, axis=-1)), None)

    stats_init = (
        jnp.full(query_matrix.shape[:3], NEGATIVE, jnp.float32),
        jnp.zeros(query_matrix.shape[:3], jnp.float32),
    )
    (row_max, row_sum), unused = lax.scan(stats_step, stats_init, (kv_blocks, seg_blocks, starts))

    def out_step(running, block_item):
        kv_block, seg_block, key_start = block_item
        score, allowed = block_scores(
            query_matrix,
            kv_block[:, 0],
            token_index,
            document_index,
            seg_block,
            key_start,
            score_scale,
        )
        probability = jnp.where(
            allowed, jnp.exp(score - row_max[..., None]) / row_sum[..., None], 0.0
        )
        return (
            running
            + jnp.einsum(
                "qhgk,khd->qhgd",
                probability.astype(jnp.bfloat16),
                kv_block[:, 1],
                preferred_element_type=jnp.float32,
            ),
            None,
        )

    attended_rows, unused = lax.scan(
        out_step, jnp.zeros(query_matrix.shape, jnp.float32), (kv_blocks, seg_blocks, starts)
    )
    return (attended_rows, row_max, row_sum)


def attend_backward(
    query_matrix,
    token_index,
    document_index,
    keyvals,
    key_segment,
    row_max,
    row_sum,
    attention_gradient,
    delta,
    block_rows,
):
    kv_heads, head_dim = (query_matrix.shape[1], query_matrix.shape[3])
    score_scale = head_dim ** (-0.5)
    seq_length = keyvals.shape[0]
    kv_blocks, seg_blocks, starts = split_blocks(
        keyvals, key_segment, block_rows, kv_heads, head_dim
    )

    def grad_step(running, block_item):
        kv_block, seg_block, key_start = block_item
        grad_query = running
        score, allowed = block_scores(
            query_matrix,
            kv_block[:, 0],
            token_index,
            document_index,
            seg_block,
            key_start,
            score_scale,
        )
        probability = jnp.where(
            allowed, jnp.exp(score - row_max[..., None]) / row_sum[..., None], 0.0
        )
        grad_prob = jnp.einsum(
            "qhgd,khd->qhgk", attention_gradient, kv_block[:, 1], preferred_element_type=jnp.float32
        )
        grad_score = (probability * (grad_prob - delta[..., None])).astype(jnp.bfloat16)
        grad_query = (
            grad_query
            + jnp.einsum(
                "qhgk,khd->qhgd", grad_score, kv_block[:, 0], preferred_element_type=jnp.float32
            )
            * score_scale
        )
        key_gradient = (
            jnp.einsum(
                "qhgk,qhgd->khd", grad_score, query_matrix, preferred_element_type=jnp.float32
            )
            * score_scale
        )
        grad_value = jnp.einsum(
            "qhgk,qhgd->khd",
            probability.astype(jnp.bfloat16),
            attention_gradient,
            preferred_element_type=jnp.float32,
        )
        return (
            grad_query,
            jnp.concatenate(
                [key_gradient.reshape(block_rows, -1), grad_value.reshape(block_rows, -1)], axis=1
            ),
        )

    grad_query, grad_kv = lax.scan(
        grad_step, jnp.zeros(query_matrix.shape, jnp.float32), (kv_blocks, seg_blocks, starts)
    )
    return (grad_query, grad_kv.reshape(seq_length, 2 * kv_heads * head_dim))


def body(
    tokens,
    doc_lengths,
    attn_gain,
    qkv_weight,
    qkv_bias,
    out_weight,
    mlp_gain,
    gate_up_weight,
    down_weight,
    out_grad,
):
    model_width = attn_gain.shape[0]
    qkv_width = qkv_bias.shape[0]
    query_total_width = QUERY_HEADS * HEAD_SIZE
    key_value_width = KEY_VALUE_HEADS * HEAD_SIZE
    query_groups = QUERY_HEADS // KEY_VALUE_HEADS
    token_count = tokens.shape[2]
    seq_length = token_count * lax.axis_size("ctx")
    first_row = lax.axis_index("ctx") * token_count
    block_rows = min(512, seq_length)
    device_count = lax.axis_size(("dp", "ctx"))

    def unpack(gathered):
        flat_qkv, flat_out, flat_gate_up, flat_down = gathered
        return (
            flat_qkv.reshape(model_width, qkv_width),
            flat_out.reshape(query_total_width, model_width),
            flat_gate_up.reshape(model_width, 2 * FF),
            flat_down.reshape(FF, model_width),
        )

    grad_qkv = jnp.zeros((model_width, qkv_width), jnp.float32)
    grad_out = jnp.zeros((query_total_width, model_width), jnp.float32)
    grad_gate_up = jnp.zeros((model_width, 2 * FF), jnp.float32)
    grad_down = jnp.zeros((FF, model_width), jnp.float32)
    grad_gain1 = jnp.zeros((model_width,), jnp.float32)
    grad_gain2 = jnp.zeros((model_width,), jnp.float32)
    grad_bias = jnp.zeros((qkv_width,), jnp.float32)
    layer_outs = []
    input_grads = []
    for micro_step in range(tokens.shape[0]):
        w_qkv, w_out, w_gate_up, w_down = unpack(
            (
                lax.all_gather(qkv_weight, ("dp", "ctx"), axis=0, tiled=True),
                lax.all_gather(out_weight, ("dp", "ctx"), axis=0, tiled=True),
                lax.all_gather(gate_up_weight, ("dp", "ctx"), axis=0, tiled=True),
                lax.all_gather(down_weight, ("dp", "ctx"), axis=0, tiled=True),
            )
        )
        inputs = tokens[micro_step, 0].astype(jnp.float32)
        token_index, document_index, positions = doc_layout(
            doc_lengths[micro_step, 0], first_row, token_count
        )
        cosine_table, sine_table = rotation(positions, HEAD_SIZE)
        normed1, scale1, hidden1 = rms_forward(inputs, attn_gain)
        hidden1 = hidden1.astype(jnp.bfloat16)
        query_key_value = jnp.dot(hidden1, w_qkv, preferred_element_type=jnp.float32) + qkv_bias
        query_matrix = rotary_apply(
            query_key_value[:, :query_total_width].reshape(token_count, QUERY_HEADS, HEAD_SIZE),
            cosine_table,
            sine_table,
        )
        query_matrix = query_matrix.astype(jnp.bfloat16).reshape(
            token_count, KEY_VALUE_HEADS, query_groups, HEAD_SIZE
        )
        key_rows = rotary_apply(
            query_key_value[:, query_total_width : query_total_width + key_value_width].reshape(
                token_count, KEY_VALUE_HEADS, HEAD_SIZE
            ),
            cosine_table,
            sine_table,
        ).astype(jnp.bfloat16)
        value_rows = query_key_value[:, query_total_width + key_value_width :].astype(jnp.bfloat16)
        local_kv = jnp.concatenate(
            [key_rows.reshape(token_count, key_value_width), value_rows], axis=1
        )
        all_kv, all_segments = (
            lax.all_gather(local_kv, "ctx", axis=0, tiled=True),
            lax.all_gather(document_index, "ctx", axis=0, tiled=True),
        )
        attended_rows, row_max, row_sum = attend_forward(
            query_matrix, token_index, document_index, all_kv, all_segments, block_rows
        )
        att_low = attended_rows.reshape(token_count, query_total_width).astype(jnp.bfloat16)
        residual = inputs + jnp.dot(att_low, w_out, preferred_element_type=jnp.float32)
        normed2, scale2, hidden2 = rms_forward(residual, mlp_gain)
        hidden2 = hidden2.astype(jnp.bfloat16)
        gate_up = jnp.dot(hidden2, w_gate_up, preferred_element_type=jnp.float32)
        gate_part = gate_up[:, :FF]
        up_part = gate_up[:, FF:]
        sigmoid = jax.nn.sigmoid(gate_part)
        silu_gate = gate_part * sigmoid
        act_low = (silu_gate * up_part).astype(jnp.bfloat16)
        layer_outs.append(
            (residual + jnp.dot(act_low, w_down, preferred_element_type=jnp.float32)).astype(
                jnp.bfloat16
            )
        )
        back_qkv, back_out, back_gate_up, back_down = unpack(
            (
                lax.all_gather(qkv_weight, ("dp", "ctx"), axis=0, tiled=True),
                lax.all_gather(out_weight, ("dp", "ctx"), axis=0, tiled=True),
                lax.all_gather(gate_up_weight, ("dp", "ctx"), axis=0, tiled=True),
                lax.all_gather(down_weight, ("dp", "ctx"), axis=0, tiled=True),
            )
        )
        back_kv, back_segments = (
            lax.all_gather(local_kv, "ctx", axis=0, tiled=True),
            lax.all_gather(document_index, "ctx", axis=0, tiled=True),
        )
        cotangent = out_grad[micro_step, 0]
        grad_down = grad_down + lax.dot_general(
            act_low, cotangent, CONTRACT_ROWS, preferred_element_type=jnp.float32
        )
        grad_act = lax.dot_general(
            cotangent, back_down, CONTRACT_COLS, preferred_element_type=jnp.float32
        )
        grad_gate = grad_act * up_part * sigmoid * (1.0 + gate_part * (1.0 - sigmoid))
        grad_up = grad_act * silu_gate
        grad_gu = jnp.concatenate([grad_gate, grad_up], axis=1).astype(jnp.bfloat16)
        grad_gate_up = grad_gate_up + lax.dot_general(
            hidden2, grad_gu, CONTRACT_ROWS, preferred_element_type=jnp.float32
        )
        grad_hidden2 = lax.dot_general(
            grad_gu, back_gate_up, CONTRACT_COLS, preferred_element_type=jnp.float32
        )
        back_mlp, gain_part2 = rms_backward(grad_hidden2, normed2, scale2, mlp_gain)
        grad_gain2 = grad_gain2 + gain_part2
        grad_mid = cotangent.astype(jnp.float32) + back_mlp
        grad_mid_low = grad_mid.astype(jnp.bfloat16)
        grad_out = grad_out + lax.dot_general(
            att_low, grad_mid_low, CONTRACT_ROWS, preferred_element_type=jnp.float32
        )
        attention_gradient = lax.dot_general(
            grad_mid_low, back_out, CONTRACT_COLS, preferred_element_type=jnp.float32
        )
        attention_gradient = attention_gradient.astype(jnp.bfloat16).reshape(
            token_count, KEY_VALUE_HEADS, query_groups, HEAD_SIZE
        )
        delta = jnp.sum(attention_gradient.astype(jnp.float32) * attended_rows, axis=-1)
        grad_query, grad_kv = attend_backward(
            query_matrix,
            token_index,
            document_index,
            back_kv,
            back_segments,
            row_max,
            row_sum,
            attention_gradient,
            delta,
            block_rows,
        )
        owned_key_value = lax.psum_scatter(
            grad_kv.astype(jnp.bfloat16), "ctx", scatter_dimension=0, tiled=True
        ).astype(jnp.float32)
        key_gradient = rotary_reverse(
            owned_key_value[:, :key_value_width].reshape(token_count, KEY_VALUE_HEADS, HEAD_SIZE),
            cosine_table,
            sine_table,
        )
        grad_query = rotary_reverse(
            grad_query.reshape(token_count, QUERY_HEADS, HEAD_SIZE), cosine_table, sine_table
        )
        grad_qkv_low = jnp.concatenate(
            [
                grad_query.reshape(token_count, query_total_width),
                key_gradient.reshape(token_count, key_value_width),
                owned_key_value[:, key_value_width:],
            ],
            axis=1,
        ).astype(jnp.bfloat16)
        grad_bias = grad_bias + jnp.sum(grad_qkv_low.astype(jnp.float32), axis=0)
        grad_qkv = grad_qkv + lax.dot_general(
            hidden1, grad_qkv_low, CONTRACT_ROWS, preferred_element_type=jnp.float32
        )
        grad_hidden1 = lax.dot_general(
            grad_qkv_low, back_qkv, CONTRACT_COLS, preferred_element_type=jnp.float32
        )
        back_attn, gain_part1 = rms_backward(grad_hidden1, normed1, scale1, attn_gain)
        grad_gain1 = grad_gain1 + gain_part1
        input_grads.append(grad_mid + back_attn)
    grad_list = (grad_qkv, grad_out, grad_gate_up, grad_down)
    widths = [item.size // device_count for item in grad_list]
    stacked = jnp.concatenate([item.reshape(device_count, -1) for item in grad_list], axis=1)
    mine = lax.psum_scatter(stacked, ("dp", "ctx"), scatter_dimension=0, tiled=True).reshape(-1)
    offsets = [0, widths[0], widths[0] + widths[1], widths[0] + widths[1] + widths[2]]
    shares = [mine[offsets[k] : offsets[k] + widths[k]] for k in range(4)]
    small_sums = lax.psum((grad_gain1, grad_bias, grad_gain2), ("dp", "ctx"))
    return (
        jnp.stack(layer_outs)[:, None],
        jnp.stack(input_grads)[:, None],
        small_sums[0],
        shares[0],
        small_sums[1],
        shares[1],
        small_sums[2],
        shares[2],
        shares[3],
    )


def together(*items):
    return lax.optimization_barrier(items)


class Links:
    def __init__(self):
        self.rows, self.cores = lax.axis_size("y"), lax.axis_size("core")
        self.deep, self.wide = lax.axis_size("z"), lax.axis_size("x")
        self.dp, self.ctx = self.rows * self.cores, self.deep * self.wide
        self.y, self.core = lax.axis_index("y"), lax.axis_index("core")
        self.z, self.x = lax.axis_index("z"), lax.axis_index("x")
        self.me_dp, self.me_ctx = lax.axis_index(("y", "core")), lax.axis_index(("z", "x"))

    def shift(self, item, axis, step=1):
        size = lax.axis_size(axis)
        if step % size == 0:
            return item
        return lax.ppermute(item, axis, [(k, (k + step) % size) for k in range(size)])

    def core_step(self, item):
        return self.shift(item, "core")

    def y_step(self, item, step=1):
        return self.shift(item, "y", step)

    def broadcast(self, item, axes):
        copies = jnp.broadcast_to(item, (lax.axis_size(axes), *item.shape))
        return lax.all_to_all(copies, axes, 0, 0)

    def spread_x(self, part):
        return [self.shift(part, "x", step) for step in range(self.wide)]

    def ring_x(self, held, moving):
        return [old + self.spread_x(item) for old, item in zip(held, moving, strict=True)]

    def ring_z(self, moving):
        return tuple(self.shift(item, "z") for item in moving)

    def near_dp(self):
        return [
            (self.y - far) % self.rows * self.cores + (self.core - core) % self.cores
            for far in range(self.rows)
            for core in range(self.cores)
        ]

    def near_ctx(self):
        return [
            (self.z - back) % self.deep * self.wide + (self.x - across) % self.wide
            for back in range(self.deep)
            for across in range(self.wide)
        ]

    def scatter_near(self, parts):
        return jnp.sum(lax.all_to_all(parts, ("z", "x"), 0, 0).astype(jnp.float32), axis=0)

    def sum_x(self, parts):
        total = parts[0].astype(jnp.float32)
        for across in range(1, self.wide):
            total = total + self.shift(parts[across], "x", -across).astype(jnp.float32)
        return total

    def gather_y(self, item):
        return jnp.stack([item] + [self.y_step(item, step) for step in range(1, self.rows)])

    def scatter_core(self, whole):
        return whole[0].astype(jnp.float32) + self.core_step(whole[1]).astype(jnp.float32)

    def scatter_y(self, pair, low):
        total = pair[0]
        for step in range(1, self.rows):
            total = total + self.y_step(pair[step].astype(low), -step).astype(jnp.float32)
        return total

    def exchange_dp(self, whole):
        came = []
        for far in range(self.rows):
            for core in range(self.cores):
                to_y, to_core = (self.y + far) % self.rows, (self.core + core) % self.cores
                part = lax.dynamic_index_in_dim(whole, to_y * self.cores + to_core, 0, False)
                size = self.dp
                pairs = []
                for k in range(size):
                    there = (k // self.cores + far) % self.rows * self.cores
                    pairs.append((k, there + (k + core) % self.cores))
                came.append(lax.ppermute(part, ("y", "core"), pairs) if far or core else part)
        return came

    def hand_back(self, parts):
        came = []
        for far in range(self.rows):
            for core in range(self.cores):
                pairs = []
                for k in range(self.dp):
                    there = (k // self.cores - far) % self.rows * self.cores
                    pairs.append((k, there + (k - core) % self.cores))
                part = parts[far * self.cores + core]
                came.append(lax.ppermute(part, ("y", "core"), pairs) if far or core else part)
        came = jnp.stack(came)
        order = [
            (dp // self.cores - self.y) % self.rows * self.cores + (dp - self.core) % self.cores
            for dp in range(self.dp)
        ]
        return [lax.dynamic_index_in_dim(came, k, 0, False) for k in order]

    def sum_dp(self, item):
        for axis in ("core", "y"):
            step, size = 1, lax.axis_size(axis)
            while step < size:
                pairs = [(k, k ^ step) for k in range(size)]
                item = item + lax.ppermute(item, axis, pairs)
                step *= 2
        return item


def allowed_bias(slot_ref, low_ref, first_ref, bias_ref):
    tokens = bias_ref.shape[1]
    query = first_ref[0] + lax.broadcasted_iota(jnp.int32, (tokens, tokens), 1)
    for slot in range(bias_ref.shape[0] // tokens):
        keys = slot_ref[slot] * tokens + lax.broadcasted_iota(jnp.int32, (tokens, tokens), 0)
        allowed = (keys >= low_ref[...]) & (keys <= query)
        bias_ref[slot * tokens : (slot + 1) * tokens, :] = jnp.where(allowed, 0.0, NEGATIVE)


def head_rows(ref, head):
    return ref[head * HEAD_SIZE : (head + 1) * HEAD_SIZE, :]


def attention_kernel(slot_ref, first_ref, low_ref, q_ref, kv_ref, att_ref, stat_ref, bias_ref):
    allowed_bias(slot_ref, low_ref, first_ref, bias_ref)
    kv_cols = jnp.concatenate([kv_ref[j] for j in range(kv_ref.shape[0])], axis=1)
    groups = QUERY_HEADS // KEY_VALUE_HEADS
    half = KEY_VALUE_HEADS * HEAD_SIZE
    key_rows = kv_cols[:half].T
    for kv_head in range(KEY_VALUE_HEADS):
        key = key_rows[:, kv_head * HEAD_SIZE : (kv_head + 1) * HEAD_SIZE]
        value = kv_cols[half + kv_head * HEAD_SIZE : half + (kv_head + 1) * HEAD_SIZE]
        for head in range(kv_head * groups, (kv_head + 1) * groups):
            score = jnp.dot(key, head_rows(q_ref, head), preferred_element_type=jnp.float32)
            score = score * HEAD_SIZE ** (-0.5) + bias_ref[...]
            top = jnp.max(score, axis=0, keepdims=True)
            weights = jnp.exp(score - top)
            total = jnp.sum(weights, axis=0, keepdims=True)
            out = jnp.dot(value, weights.astype(jnp.bfloat16), preferred_element_type=jnp.float32)
            att_ref[head * HEAD_SIZE : (head + 1) * HEAD_SIZE, :] = out / total
            stat_ref[head : head + 1, :] = top + jnp.log(total)


def attention_back_kernel(
    slot_ref,
    first_ref,
    low_ref,
    q_ref,
    kv_ref,
    att_ref,
    stat_ref,
    datt_ref,
    dq_ref,
    dkv_ref,
    bias_ref,
    qs_ref,
    das_ref,
    ds_ref,
    p_ref,
):
    allowed_bias(slot_ref, low_ref, first_ref, bias_ref)
    kv_cols = jnp.concatenate([kv_ref[j] for j in range(kv_ref.shape[0])], axis=1)
    tokens = q_ref.shape[1]
    groups = QUERY_HEADS // KEY_VALUE_HEADS
    half = KEY_VALUE_HEADS * HEAD_SIZE
    scale = HEAD_SIZE ** (-0.5)
    rows = kv_cols.T
    results = []
    for kv_head in range(KEY_VALUE_HEADS):
        own = slice(kv_head * HEAD_SIZE, (kv_head + 1) * HEAD_SIZE)
        key = rows[:, own]
        value = rows[:, half + kv_head * HEAD_SIZE : half + (kv_head + 1) * HEAD_SIZE]
        key_cols = kv_cols[own]
        for place in range(groups):
            head = kv_head * groups + place
            lanes = slice(place * tokens, (place + 1) * tokens)
            query = head_rows(q_ref, head)
            datt = head_rows(datt_ref, head)
            qs_ref[:, lanes] = query
            das_ref[:, lanes] = datt
            delta = jnp.sum(
                datt.astype(jnp.float32) * head_rows(att_ref, head), axis=0, keepdims=True
            )
            score = jnp.dot(key, query, preferred_element_type=jnp.float32)
            prob = jnp.exp(score * scale + bias_ref[...] - stat_ref[head : head + 1, :])
            dprob = jnp.dot(value, datt, preferred_element_type=jnp.float32)
            dscore = (prob * (dprob - delta)).astype(jnp.bfloat16)
            ds_ref[:, lanes] = dscore
            p_ref[:, lanes] = prob.astype(jnp.bfloat16)
            dq_ref[head * HEAD_SIZE : (head + 1) * HEAD_SIZE, :] = (
                jnp.dot(key_cols, dscore, preferred_element_type=jnp.float32) * scale
            )
        results.append(
            lax.dot_general(
                ds_ref[...], qs_ref[...], CONTRACT_COLS, preferred_element_type=jnp.float32
            )
            * scale
        )
        results.append(
            lax.dot_general(
                p_ref[...], das_ref[...], CONTRACT_COLS, preferred_element_type=jnp.float32
            )
        )
    order = results[0::2] + results[1::2]
    out = jnp.concatenate(order, axis=1).astype(jnp.bfloat16)
    for j in range(dkv_ref.shape[0]):
        dkv_ref[j] = out[j * tokens : (j + 1) * tokens]


def attention_specs(width, pieces, kv_width, tokens):
    smem = pl.BlockSpec(memory_space=pltpu.SMEM)
    low = pl.BlockSpec((pl.Squeezed(), 1, tokens), lambda mb: (mb, 0, 0))
    cols = pl.BlockSpec((width, tokens), lambda mb: (0, mb))
    kv = pl.BlockSpec((pieces, kv_width, tokens), lambda mb: (0, 0, mb))
    stat = pl.BlockSpec((QUERY_HEADS, tokens), lambda mb: (0, mb))
    return smem, low, cols, kv, stat


def attend(slots, first, low, q_cols, kv_all, batches):
    width, total = q_cols.shape
    tokens = total // batches
    pieces, kv_width, _ = kv_all.shape
    smem, low_spec, cols, kv, stat = attention_specs(width, pieces, kv_width, tokens)
    return pl.pallas_call(
        attention_kernel,
        grid=(batches,),
        in_specs=[smem, smem, low_spec, cols, kv],
        out_specs=[cols, stat],
        out_shape=[
            jax.ShapeDtypeStruct((width, total), jnp.float32),
            jax.ShapeDtypeStruct((QUERY_HEADS, total), jnp.float32),
        ],
        scratch_shapes=[pltpu.VMEM((pieces * tokens, tokens), jnp.float32)],
        compiler_params=pltpu.CompilerParams(vmem_limit_bytes=40 * 2**20),
        cost_estimate=pl.CostEstimate(
            flops=4 * total * pieces * tokens * width,
            bytes_accessed=8 * total * width,
            transcendentals=total * pieces * tokens * QUERY_HEADS,
        ),
        name="attention",
    )(slots, first, low, q_cols, kv_all)


def attend_back(slots, first, low, q_cols, kv_all, att_cols, stats, datt_cols, batches):
    width, total = q_cols.shape
    tokens = total // batches
    pieces, kv_width, _ = kv_all.shape
    groups = QUERY_HEADS // KEY_VALUE_HEADS
    keys = pieces * tokens
    smem, low_spec, cols, kv, stat = attention_specs(width, pieces, kv_width, tokens)
    return pl.pallas_call(
        attention_back_kernel,
        grid=(batches,),
        in_specs=[smem, smem, low_spec, cols, kv, cols, stat, cols],
        out_specs=[
            cols,
            pl.BlockSpec((pieces, pl.Squeezed(), tokens, kv_width), lambda mb: (0, mb, 0, 0)),
        ],
        out_shape=[
            jax.ShapeDtypeStruct((width, total), jnp.float32),
            jax.ShapeDtypeStruct((pieces, batches, tokens, kv_width), jnp.bfloat16),
        ],
        scratch_shapes=[
            pltpu.VMEM((keys, tokens), jnp.float32),
            pltpu.VMEM((HEAD_SIZE, groups * tokens), jnp.bfloat16),
            pltpu.VMEM((HEAD_SIZE, groups * tokens), jnp.bfloat16),
            pltpu.VMEM((keys, groups * tokens), jnp.bfloat16),
            pltpu.VMEM((keys, groups * tokens), jnp.bfloat16),
        ],
        compiler_params=pltpu.CompilerParams(vmem_limit_bytes=48 * 2**20),
        cost_estimate=pl.CostEstimate(
            flops=10 * total * keys * width,
            bytes_accessed=14 * total * width,
            transcendentals=total * keys * QUERY_HEADS,
        ),
        name="attention_back",
    )(slots, first, low, q_cols, kv_all, att_cols, stats, datt_cols)


def forward_kernel(
    near_ref,
    far_ref,
    near_dy_ref,
    far_dy_ref,
    gate_up_ref,
    down_ref,
    pick_ref,
    hidden_ref,
    act_ref,
    dgu_ref,
    dhidden_ref,
):
    first = pl.program_id(0) < pl.num_programs(0) // 2
    hidden = jnp.where(first, near_ref[...], far_ref[...])
    dy = jnp.where(first, near_dy_ref[...], far_dy_ref[...])
    hidden = dot32(hidden, pick_ref[...]).astype(jnp.bfloat16)
    hidden_ref[...] = hidden
    own_ff = down_ref.shape[0]
    gate_up = dot32(hidden, gate_up_ref[...])
    gate, up = gate_up[:, :own_ff], gate_up[:, own_ff:]
    sigmoid = jax.nn.sigmoid(gate)
    silu = gate * sigmoid
    act_ref[...] = (silu * up).astype(jnp.bfloat16)
    dact = dot32(dy, down_ref[...], CONTRACT_COLS)
    dgate = dact * up * sigmoid * (1.0 + gate * (1.0 - sigmoid))
    dgu = jnp.concatenate([dgate, dact * silu], axis=1).astype(jnp.bfloat16)
    dgu_ref[...] = dgu
    dhidden = dot32(dgu, gate_up_ref[...], CONTRACT_COLS).astype(jnp.bfloat16)
    dhidden_ref[...] = dot32(dhidden, pick_ref[...], CONTRACT_COLS).astype(jnp.bfloat16)


def feed_forward(hidden, dy, w_gate_up, w_down, pick, tile):
    half, width = hidden[0].shape
    own_ff = w_down.shape[0]
    steps = half // tile
    near = pl.BlockSpec((tile, width), lambda i: (jnp.minimum(i, steps - 1), 0))
    far = pl.BlockSpec((tile, width), lambda i: (jnp.maximum(i - steps, 0), 0))

    def whole(item):
        return pl.BlockSpec(item.shape, lambda i: (0, 0), pipeline_mode=pl.Buffered(1))

    def rows(columns):
        return pl.BlockSpec((tile, columns), lambda i: (i, 0))

    widths = (width, own_ff, 2 * own_ff, width)
    return pl.pallas_call(
        forward_kernel,
        grid=(2 * steps,),
        in_specs=[near, far, near, far, whole(w_gate_up), whole(w_down), whole(pick)],
        out_specs=[rows(columns) for columns in widths],
        out_shape=[jax.ShapeDtypeStruct((2 * half, columns), jnp.bfloat16) for columns in widths],
        compiler_params=pltpu.CompilerParams(vmem_limit_bytes=48 * 2**20),
        cost_estimate=pl.CostEstimate(
            flops=4 * half * width * (5 * own_ff + 2 * width),
            bytes_accessed=8 * half * (2 * width + 2 * own_ff) + 6 * width * own_ff,
            transcendentals=2 * half * own_ff,
        ),
        name="feed_forward",
    )(*hidden, *dy, w_gate_up, w_down, pick)


def one_hot_order(order, size):
    rows = lax.broadcasted_iota(jnp.int32, (size, order.shape[0]), 0)
    return (rows == order[None, :]).astype(jnp.bfloat16)


def dot32(left, right, dims=(((1,), (0,)), ((), ()))):
    return lax.dot_general(left, right, dims, preferred_element_type=jnp.float32)


def rope_columns(cols, cosine, sine):
    first, second = cols[:, 0], cols[:, 1]
    return jnp.stack([first * cosine - second * sine, second * cosine + first * sine], axis=1)


def rope_columns_back(cols, cosine, sine):
    first, second = cols[:, 0], cols[:, 1]
    return jnp.stack([first * cosine + second * sine, second * cosine - first * sine], axis=1)


def short_body(
    tokens,
    doc_lengths,
    attn_gain,
    qkv_weight,
    qkv_bias,
    out_weight,
    mlp_gain,
    gate_up_weight,
    down_weight,
    out_grad,
):
    links = Links()
    width = attn_gain.shape[0]
    qkv_width = qkv_bias.shape[0]
    query_width = QUERY_HEADS * HEAD_SIZE
    kv_width = KEY_VALUE_HEADS * HEAD_SIZE
    half = HEAD_SIZE // 2
    batches, token_count = tokens.shape[0], tokens.shape[2]
    total = batches * token_count
    devices = links.dp * links.ctx
    piece = width // devices
    own_ff = FF // links.dp
    first_row = links.me_ctx * token_count

    padded = -(-piece // 16) * 16
    key_slots = jnp.stack(
        [
            z * links.wide + (links.x - across) % links.wide
            for across in range(links.wide)
            for z in range(links.deep)
        ]
    ).astype(jnp.int32)
    row = jnp.arange(padded, dtype=jnp.int32)
    near_dp = jnp.stack(links.near_dp()).astype(jnp.int32)
    near_ctx = jnp.stack(links.near_ctx()).astype(jnp.int32)
    rows_order = near_dp.reshape(links.rows, 2).T.reshape(-1)
    owner = rows_order[:, None] * links.ctx + jnp.arange(links.ctx, dtype=jnp.int32)[None, :]
    attn_order = jnp.where(row < piece, owner[:, :, None] * piece + row, -1).reshape(-1)
    attn_pick = one_hot_order(attn_order, width)
    owner = near_dp[None, :] * links.ctx + near_ctx[:, None]
    mlp_order = (owner[:, :, None] * piece + jnp.arange(piece, dtype=jnp.int32)).reshape(-1)
    mlp_pick = one_hot_order(mlp_order, width)

    def own_rows(flat, columns):
        return jnp.pad(flat.reshape(piece, columns), ((0, padded - piece), (0, 0)))

    def rows_y(near):
        return jnp.concatenate([near] + [links.y_step(near, k) for k in range(1, links.rows)])

    def rows_core(held):
        return jnp.concatenate([held, links.core_step(held)])

    def back_core(grad):
        mine, other = jnp.split(grad, 2)
        return mine.astype(jnp.float32) + links.core_step(other).astype(jnp.float32)

    def back_y(pair):
        parts = jnp.split(pair, links.rows)
        total = parts[0]
        for step in range(1, links.rows):
            there = links.y_step(parts[step].astype(jnp.bfloat16), -step)
            total = total + there.astype(jnp.float32)
        return total.astype(jnp.bfloat16).reshape(links.ctx, padded, -1)

    w_qkv = links.broadcast(own_rows(qkv_weight, qkv_width), ("z", "x")).reshape(-1, qkv_width)
    gate_up_rows = gate_up_weight.reshape(piece, 2, links.dp, own_ff)
    gate_up_rows = gate_up_rows.transpose(2, 0, 1, 3).reshape(links.dp, piece, 2 * own_ff)
    parts = links.exchange_dp(gate_up_rows)
    all_cotangent = links.gather_y(out_grad[:, 0].reshape(total, width))
    w_qkv, all_cotangent, down_part, *parts = together(
        w_qkv, all_cotangent, down_weight.reshape(-1, width), *parts
    )

    w_qkv = rows_y(w_qkv)
    moving = (
        jnp.stack(parts).reshape(links.dp * piece, 2 * own_ff),
        down_part,
    )
    held = links.ring_x([[], []], moving)
    moving = links.ring_z(moving)
    w_out = links.broadcast(own_rows(out_weight, width), ("z", "x")).reshape(-1, width)
    w_qkv, w_out, moving, held = together(w_qkv, w_out, moving, held)

    w_qkv = rows_core(w_qkv)

    cotangent = out_grad[:, 0].reshape(total, width)

    inputs = tokens[:, 0].reshape(total, width).astype(jnp.float32)
    layouts = [doc_layout(doc_lengths[b, 0], first_row, token_count) for b in range(batches)]
    token_index = layouts[0][0]
    positions = jnp.concatenate([item[2] for item in layouts])
    low = jnp.stack([token_index - item[2] for item in layouts])[:, None, :]
    first = jnp.reshape(first_row, (1,)).astype(jnp.int32)
    freqs = ROPE_THETA ** (-(2.0 * jnp.arange(half, dtype=jnp.float32)) / HEAD_SIZE)
    angles = freqs[:, None] * positions.astype(jnp.float32)[None, :]
    cosine, sine = jnp.cos(angles), jnp.sin(angles)

    normed1, scale1, hidden1 = rms_forward(inputs, attn_gain)
    hidden1 = dot32(hidden1.astype(jnp.bfloat16), attn_pick).astype(jnp.bfloat16)
    qkv_cols = dot32(w_qkv, hidden1, (((0,), (1,)), ((), ()))) + qkv_bias[:, None]
    turned = rope_columns(
        qkv_cols[: query_width + kv_width].reshape(-1, 2, half, total), cosine, sine
    )
    turned = turned.reshape(query_width + kv_width, total).astype(jnp.bfloat16)
    q_cols = turned[:query_width]
    kv_cols = jnp.concatenate(
        [turned[query_width:], qkv_cols[query_width + kv_width :].astype(jnp.bfloat16)]
    )
    kv_cols, moving = together(kv_cols, moving)
    kv_all = links.broadcast(kv_cols, "z")
    held = links.ring_x(held, moving)
    kv_all, w_out, moving, held = together(kv_all, w_out, moving, held)

    kv_all = jnp.concatenate(links.spread_x(kv_all))
    w_out = rows_y(w_out)
    for step in range(2, links.deep - 1):
        moving = links.ring_z(moving)
        if step > 2:
            held = links.ring_x(held, moving)
    kv_all, w_out, moving, cotangent = together(kv_all, w_out, moving, cotangent)

    w_out = rows_core(w_out)
    held = links.ring_x(held, moving)
    moving = links.ring_z(moving)
    att_cols, stats = attend(key_slots, first, low, q_cols, kv_all, batches)
    att_cols, w_out, all_cotangent = together(att_cols, w_out, all_cotangent)

    att_low = dot32(
        att_cols.astype(jnp.bfloat16), attn_pick, (((0,), (0,)), ((), ()))
    ).astype(jnp.bfloat16)
    residual = inputs + dot32(att_low, w_out)

    normed2, scale2, hidden2 = rms_forward(residual, mlp_gain)
    hidden2 = hidden2.astype(jnp.bfloat16)
    near_hidden2 = links.gather_y(hidden2).reshape(-1, width)
    moving, _ = together(moving, hidden2)
    w_parts, down_parts = links.ring_x(held, moving)
    w_gate_up = jnp.concatenate(w_parts)
    w_down = jnp.zeros((links.ctx, own_ff // links.ctx, width), jnp.bfloat16)
    for k, part in enumerate(down_parts):
        w_down = lax.dynamic_update_index_in_dim(w_down, part, near_ctx[k], 0)
    w_down = w_down.reshape(own_ff, width)
    near_dy = all_cotangent.reshape(-1, width)
    far_dy = links.core_step(near_dy)
    near_hidden2, far_dy, w_gate_up, w_down = together(near_hidden2, far_dy, w_gate_up, w_down)
    far_hidden2 = links.core_step(near_hidden2)
    all_hidden2, act_low, dgu, dhidden2 = feed_forward(
        (near_hidden2, far_hidden2), (near_dy, far_dy), w_gate_up, w_down, mlp_pick, total
    )
    all_cotangent = jnp.concatenate([near_dy, far_dy])
    dhidden2, dgu, act_low = together(dhidden2, dgu, act_low)

    dhidden2 = links.scatter_core(dhidden2.reshape(2, links.rows, total, width))
    grad_gate_up = dot32(all_hidden2, dgu, CONTRACT_ROWS).astype(jnp.bfloat16)
    grad_down = dot32(act_low, all_cotangent, CONTRACT_ROWS).astype(jnp.bfloat16)
    dhidden2, grad_gate_up, grad_down, act_low = together(
        dhidden2, grad_gate_up, grad_down, act_low
    )

    blocks = grad_gate_up.reshape(links.deep, links.wide, -1, 2 * own_ff)
    down_blocks = grad_down.reshape(links.ctx, own_ff // links.ctx, width)

    def across(blocks, back):
        gate_up_blocks, down_blocks = blocks
        places = [near_ctx[back * links.wide + step] for step in range(links.wide)]
        down = [lax.dynamic_index_in_dim(down_blocks, k, 0, False) for k in places]
        return links.sum_x(gate_up_blocks[back]), links.sum_x(down)

    def lowered(share):
        return [item.astype(jnp.bfloat16) for item in share]

    def plus(share, moved):
        return tuple(a + b.astype(jnp.float32) for a, b in zip(share, moved, strict=True))

    def ring(share, other):
        return plus(other, links.ring_z(lowered(share)))

    blocks = (blocks, down_blocks)
    share = across(blocks, 1)
    dhidden2 = links.scatter_y(dhidden2, jnp.bfloat16)
    out_part = dot32(act_low, w_down).astype(jnp.bfloat16)

    back_mlp, gain2_grad = rms_backward(dhidden2, normed2, scale2, mlp_gain)
    dmid = cotangent.astype(jnp.float32) + back_mlp
    dmid_low = dmid.astype(jnp.bfloat16)
    datt = dot32(dmid_low, w_out, CONTRACT_COLS).astype(jnp.bfloat16)
    datt_cols = dot32(attn_pick, datt, CONTRACT_COLS).astype(jnp.bfloat16)
    grad_out = dot32(att_low, dmid_low, CONTRACT_ROWS).astype(jnp.bfloat16)
    share, blocks, datt_cols, out_part = together(share, blocks, datt_cols, out_part)
    share = ring(share, across(blocks, 2))
    out_part = links.scatter_core(out_part.reshape(2, links.rows, total, width))
    grad_out = back_core(grad_out)
    dq_cols, dkv = attend_back(
        key_slots, first, low, q_cols, kv_all, att_cols, stats, datt_cols, batches
    )
    dq_cols, dkv, share, blocks, grad_out, out_part = together(
        dq_cols, dkv, share, blocks, grad_out, out_part
    )

    dkv = dkv.reshape(links.wide, links.deep, total, 2 * kv_width)
    dkv = links.sum_x(dkv).astype(jnp.bfloat16)
    for back in range(3, links.deep - 1):
        share = ring(share, across(blocks, back))
    share = links.ring_z(lowered(share))
    dkv, blocks, out_part = together(dkv, blocks, out_part)

    layer_out = residual + links.scatter_y(out_part, jnp.bfloat16)
    own_dkv = jnp.sum(lax.all_to_all(dkv, "z", 0, 0).astype(jnp.float32), axis=0).T
    share = plus(across(blocks, links.deep - 1), share)
    dq = rope_columns_back(dq_cols.reshape(-1, 2, half, total), cosine, sine)
    dq = dq.reshape(query_width, total).astype(jnp.bfloat16)
    grad_q = back_core(dot32(hidden1, dq, (((0,), (1,)), ((), ()))).astype(jnp.bfloat16))
    grad_out = back_y(grad_out)
    own_dkv, grad_q, grad_out, layer_out, blocks = together(
        own_dkv, grad_q, grad_out, layer_out, blocks
    )

    grad_q = jnp.concatenate([back_y(grad_q), grad_out], axis=2)
    share = ring(share, across(blocks, 0))
    dk = rope_columns_back(own_dkv[:kv_width].reshape(-1, 2, half, total), cosine, sine)
    dkv = jnp.concatenate([dk.reshape(kv_width, total), own_dkv[kv_width:]]).astype(jnp.bfloat16)
    grad_kv = dot32(hidden1, dkv, (((0,), (1,)), ((), ()))).astype(jnp.bfloat16)
    grad_kv = back_y(back_core(grad_kv))
    grad_q = links.scatter_near(grad_q)[:piece]
    dqkv = jnp.concatenate([dq, dkv])
    bias_grad = jnp.sum(dqkv.astype(jnp.float32), axis=1)
    dhidden1 = dot32(dqkv, w_qkv, (((0,), (1,)), ((), ())))
    (top,) = together(dhidden1.astype(jnp.bfloat16))
    rest = (dhidden1 - top.astype(jnp.float32)).astype(jnp.bfloat16)
    dhidden1 = dot32(top, attn_pick, CONTRACT_COLS) + dot32(rest, attn_pick, CONTRACT_COLS)
    back_attn, gain1_grad = rms_backward(dhidden1, normed1, scale1, attn_gain)
    input_grad = dmid + back_attn
    small = links.sum_dp(jnp.concatenate([gain1_grad, bias_grad, gain2_grad]).reshape(-1, 128))
    (high,) = together(small.astype(jnp.bfloat16))
    rest = small - high.astype(jnp.float32)
    (mid_part,) = together(rest.astype(jnp.bfloat16))
    last = (rest - mid_part.astype(jnp.float32)).astype(jnp.bfloat16)
    grad_q, grad_kv, share, high, mid_part, last = together(
        grad_q, grad_kv, share, high, mid_part, last
    )

    share, down_share = share
    parts = share.astype(jnp.bfloat16).reshape(links.dp, piece, 2 * own_ff)
    parts = jnp.stack(links.hand_back(parts)).reshape(links.dp, piece, 2, own_ff)
    gate_up_share = parts.transpose(1, 2, 0, 3).astype(jnp.float32).reshape(-1)
    sums = jnp.concatenate([high, mid_part, last]).reshape(-1)
    columns = grad_kv.shape[2]
    extra = -(-sums.size // (16 * columns)) * 16
    sums = jnp.pad(sums, (0, extra * columns - sums.size)).reshape(extra, columns)
    sums = jnp.broadcast_to(sums, (links.ctx, extra, columns))
    grad_kv = links.scatter_near(jnp.concatenate([grad_kv, sums], axis=1))
    small = grad_kv[padded:].reshape(-1)[: 3 * small.size].reshape(3, -1).sum(axis=0)
    grad_kv = grad_kv[:piece]
    qkv_share = jnp.concatenate([grad_q[:, :query_width], grad_kv], axis=1).reshape(-1)
    out_share = grad_q[:, query_width:].reshape(-1)
    return (
        layer_out.astype(jnp.bfloat16).reshape(batches, 1, token_count, width),
        input_grad.reshape(batches, 1, token_count, width),
        small[:width],
        qkv_share,
        small[width : width + qkv_width],
        out_share,
        small[width + qkv_width :],
        gate_up_share,
        down_share.reshape(-1),
    )


def fits(mesh):
    dp, ctx = mesh.shape["dp"], mesh.shape["ctx"]
    devices = dp * ctx
    if dp % 2 or ctx % (dp // 2) or ctx // (dp // 2) < 3:
        return False
    return WIDTH % devices == 0 and FF % devices == 0


def solution(mesh):
    run, dp, ctx = body, ("dp",), ("ctx",)
    if fits(mesh):
        rows = mesh.shape["dp"] // 2
        shape = (rows, 2, mesh.shape["ctx"] // rows, rows)
        run, dp, ctx = short_body, ("y", "core"), ("z", "x")
        mesh = Mesh(mesh.devices.reshape(shape), (*dp, *ctx))
    return jax.shard_map(
        run,
        mesh=mesh,
        in_specs=(
            P(None, dp, ctx, None),
            P(None, dp, None),
            P(),
            P((*dp, *ctx)),
            P(),
            P((*dp, *ctx)),
            P(),
            P((*dp, *ctx)),
            P((*dp, *ctx)),
            P(None, dp, ctx, None),
        ),
        out_specs=(
            P(None, dp, ctx, None),
            P(None, dp, ctx, None),
            P(),
            P((*dp, *ctx)),
            P(),
            P((*dp, *ctx)),
            P(),
            P((*dp, *ctx)),
            P((*dp, *ctx)),
        ),
        check_vma=False,
    )
```

```python
import jax
import jax.numpy as jnp
from jax import lax
from jax.experimental import pallas as pl
from jax.experimental.pallas import tpu as pltpu
from jax.sharding import Mesh
from jax.sharding import PartitionSpec as P

QUERY_HEADS = 14
KEY_VALUE_HEADS = 2
HEAD_SIZE = 64
FF = 4864
WIDTH = 896


EPSILON = 1e-06
ROPE_THETA = 1000000.0
NEGATIVE = -1e30
CONTRACT_ROWS = (((0,), (0,)), ((), ()))
CONTRACT_COLS = (((1,), (1,)), ((), ()))


def doc_layout(lengths, first_row, token_count):
    token_index = first_row + jnp.arange(token_count, dtype=jnp.int32)
    doc_ends = jnp.cumsum(lengths, dtype=jnp.int32)
    before = doc_ends[None, :] <= token_index[:, None]
    document_index = jnp.sum(before.astype(jnp.int32), axis=1, dtype=jnp.int32)
    doc_start = jnp.sum(jnp.where(before, lengths[None, :], 0), axis=1, dtype=jnp.int32)
    return (token_index, document_index, token_index - doc_start)


def rotation(positions, head_dim):
    freqs = ROPE_THETA ** (-(2.0 * jnp.arange(head_dim // 2, dtype=jnp.float32)) / head_dim)
    angles = positions.astype(jnp.float32)[:, None] * freqs[None, :]
    cosine_table = jnp.concatenate([jnp.cos(angles), jnp.cos(angles)], axis=-1)
    sine_table = jnp.concatenate([jnp.sin(angles), jnp.sin(angles)], axis=-1)
    return (cosine_table[:, None, :], sine_table[:, None, :])


def rotary_apply(heads, cosine_table, sine_table):
    half_dim = heads.shape[-1] // 2
    turned = jnp.concatenate([-heads[..., half_dim:], heads[..., :half_dim]], axis=-1)
    return heads * cosine_table + turned * sine_table


def rotary_reverse(grads, cosine_table, sine_table):
    half_dim = grads.shape[-1] // 2
    weighted = grads * sine_table
    turned = jnp.concatenate([weighted[..., half_dim:], -weighted[..., :half_dim]], axis=-1)
    return grads * cosine_table + turned


def rms_forward(value_rows, gain):
    row_scale = lax.rsqrt(jnp.mean(value_rows * value_rows, axis=-1, keepdims=True) + EPSILON)
    normed = value_rows * row_scale
    return (normed, row_scale, normed * gain)


def rms_backward(grads, normed, row_scale, gain):
    grad_normed = grads * gain
    gain_grad = jnp.sum(grads * normed, axis=0)
    back = row_scale * (
        grad_normed - normed * jnp.mean(grad_normed * normed, axis=-1, keepdims=True)
    )
    return (back, gain_grad)


def block_scores(
    query_matrix, key_block, token_index, document_index, seg_block, key_start, score_scale
):
    score = (
        jnp.einsum("qhgd,khd->qhgk", query_matrix, key_block, preferred_element_type=jnp.float32)
        * score_scale
    )
    key_index = key_start + jnp.arange(key_block.shape[0], dtype=jnp.int32)
    allowed = (seg_block[None, :] == document_index[:, None]) & (
        key_index[None, :] <= token_index[:, None]
    )
    return (score, allowed[:, None, None, :])


def split_blocks(keyvals, key_segment, block_rows, kv_heads, head_dim):
    seq_length = keyvals.shape[0]
    block_count = seq_length // block_rows
    kv_blocks = keyvals.reshape(block_count, block_rows, 2, kv_heads, head_dim)
    seg_blocks = key_segment.reshape(block_count, block_rows)
    starts = jnp.arange(block_count, dtype=jnp.int32) * block_rows
    return (kv_blocks, seg_blocks, starts)


def attend_forward(query_matrix, token_index, document_index, keyvals, key_segment, block_rows):
    kv_heads, head_dim = (query_matrix.shape[1], query_matrix.shape[3])
    score_scale = head_dim ** (-0.5)
    kv_blocks, seg_blocks, starts = split_blocks(
        keyvals, key_segment, block_rows, kv_heads, head_dim
    )

    def stats_step(running, block_item):
        kv_block, seg_block, key_start = block_item
        row_max, row_sum = running
        score, allowed = block_scores(
            query_matrix,
            kv_block[:, 0],
            token_index,
            document_index,
            seg_block,
            key_start,
            score_scale,
        )
        new_max = jnp.maximum(row_max, jnp.max(jnp.where(allowed, score, NEGATIVE), axis=-1))
        weights = jnp.where(allowed, jnp.exp(score - new_max[..., None]), 0.0)
        return ((new_max, row_sum * jnp.exp(row_max - new_max) + jnp.sum(weights, axis=-1)), None)

    stats_init = (
        jnp.full(query_matrix.shape[:3], NEGATIVE, jnp.float32),
        jnp.zeros(query_matrix.shape[:3], jnp.float32),
    )
    (row_max, row_sum), unused = lax.scan(stats_step, stats_init, (kv_blocks, seg_blocks, starts))

    def out_step(running, block_item):
        kv_block, seg_block, key_start = block_item
        score, allowed = block_scores(
            query_matrix,
            kv_block[:, 0],
            token_index,
            document_index,
            seg_block,
            key_start,
            score_scale,
        )
        probability = jnp.where(
            allowed, jnp.exp(score - row_max[..., None]) / row_sum[..., None], 0.0
        )
        return (
            running
            + jnp.einsum(
                "qhgk,khd->qhgd",
                probability.astype(jnp.bfloat16),
                kv_block[:, 1],
                preferred_element_type=jnp.float32,
            ),
            None,
        )

    attended_rows, unused = lax.scan(
        out_step, jnp.zeros(query_matrix.shape, jnp.float32), (kv_blocks, seg_blocks, starts)
    )
    return (attended_rows, row_max, row_sum)


def attend_backward(
    query_matrix,
    token_index,
    document_index,
    keyvals,
    key_segment,
    row_max,
    row_sum,
    attention_gradient,
    delta,
    block_rows,
):
    kv_heads, head_dim = (query_matrix.shape[1], query_matrix.shape[3])
    score_scale = head_dim ** (-0.5)
    seq_length = keyvals.shape[0]
    kv_blocks, seg_blocks, starts = split_blocks(
        keyvals, key_segment, block_rows, kv_heads, head_dim
    )

    def grad_step(running, block_item):
        kv_block, seg_block, key_start = block_item
        grad_query = running
        score, allowed = block_scores(
            query_matrix,
            kv_block[:, 0],
            token_index,
            document_index,
            seg_block,
            key_start,
            score_scale,
        )
        probability = jnp.where(
            allowed, jnp.exp(score - row_max[..., None]) / row_sum[..., None], 0.0
        )
        grad_prob = jnp.einsum(
            "qhgd,khd->qhgk", attention_gradient, kv_block[:, 1], preferred_element_type=jnp.float32
        )
        grad_score = (probability * (grad_prob - delta[..., None])).astype(jnp.bfloat16)
        grad_query = (
            grad_query
            + jnp.einsum(
                "qhgk,khd->qhgd", grad_score, kv_block[:, 0], preferred_element_type=jnp.float32
            )
            * score_scale
        )
        key_gradient = (
            jnp.einsum(
                "qhgk,qhgd->khd", grad_score, query_matrix, preferred_element_type=jnp.float32
            )
            * score_scale
        )
        grad_value = jnp.einsum(
            "qhgk,qhgd->khd",
            probability.astype(jnp.bfloat16),
            attention_gradient,
            preferred_element_type=jnp.float32,
        )
        return (
            grad_query,
            jnp.concatenate(
                [key_gradient.reshape(block_rows, -1), grad_value.reshape(block_rows, -1)], axis=1
            ),
        )

    grad_query, grad_kv = lax.scan(
        grad_step, jnp.zeros(query_matrix.shape, jnp.float32), (kv_blocks, seg_blocks, starts)
    )
    return (grad_query, grad_kv.reshape(seq_length, 2 * kv_heads * head_dim))


def body(
    tokens,
    doc_lengths,
    attn_gain,
    qkv_weight,
    qkv_bias,
    out_weight,
    mlp_gain,
    gate_up_weight,
    down_weight,
    out_grad,
):
    model_width = attn_gain.shape[0]
    qkv_width = qkv_bias.shape[0]
    query_total_width = QUERY_HEADS * HEAD_SIZE
    key_value_width = KEY_VALUE_HEADS * HEAD_SIZE
    query_groups = QUERY_HEADS // KEY_VALUE_HEADS
    token_count = tokens.shape[2]
    seq_length = token_count * lax.axis_size("ctx")
    first_row = lax.axis_index("ctx") * token_count
    block_rows = min(512, seq_length)
    device_count = lax.axis_size(("dp", "ctx"))

    def unpack(gathered):
        flat_qkv, flat_out, flat_gate_up, flat_down = gathered
        return (
            flat_qkv.reshape(model_width, qkv_width),
            flat_out.reshape(query_total_width, model_width),
            flat_gate_up.reshape(model_width, 2 * FF),
            flat_down.reshape(FF, model_width),
        )

    grad_qkv = jnp.zeros((model_width, qkv_width), jnp.float32)
    grad_out = jnp.zeros((query_total_width, model_width), jnp.float32)
    grad_gate_up = jnp.zeros((model_width, 2 * FF), jnp.float32)
    grad_down = jnp.zeros((FF, model_width), jnp.float32)
    grad_gain1 = jnp.zeros((model_width,), jnp.float32)
    grad_gain2 = jnp.zeros((model_width,), jnp.float32)
    grad_bias = jnp.zeros((qkv_width,), jnp.float32)
    layer_outs = []
    input_grads = []
    for micro_step in range(tokens.shape[0]):
        w_qkv, w_out, w_gate_up, w_down = unpack(
            (
                lax.all_gather(qkv_weight, ("dp", "ctx"), axis=0, tiled=True),
                lax.all_gather(out_weight, ("dp", "ctx"), axis=0, tiled=True),
                lax.all_gather(gate_up_weight, ("dp", "ctx"), axis=0, tiled=True),
                lax.all_gather(down_weight, ("dp", "ctx"), axis=0, tiled=True),
            )
        )
        inputs = tokens[micro_step, 0].astype(jnp.float32)
        token_index, document_index, positions = doc_layout(
            doc_lengths[micro_step, 0], first_row, token_count
        )
        cosine_table, sine_table = rotation(positions, HEAD_SIZE)
        normed1, scale1, hidden1 = rms_forward(inputs, attn_gain)
        hidden1 = hidden1.astype(jnp.bfloat16)
        query_key_value = jnp.dot(hidden1, w_qkv, preferred_element_type=jnp.float32) + qkv_bias
        query_matrix = rotary_apply(
            query_key_value[:, :query_total_width].reshape(token_count, QUERY_HEADS, HEAD_SIZE),
            cosine_table,
            sine_table,
        )
        query_matrix = query_matrix.astype(jnp.bfloat16).reshape(
            token_count, KEY_VALUE_HEADS, query_groups, HEAD_SIZE
        )
        key_rows = rotary_apply(
            query_key_value[:, query_total_width : query_total_width + key_value_width].reshape(
                token_count, KEY_VALUE_HEADS, HEAD_SIZE
            ),
            cosine_table,
            sine_table,
        ).astype(jnp.bfloat16)
        value_rows = query_key_value[:, query_total_width + key_value_width :].astype(jnp.bfloat16)
        local_kv = jnp.concatenate(
            [key_rows.reshape(token_count, key_value_width), value_rows], axis=1
        )
        all_kv, all_segments = (
            lax.all_gather(local_kv, "ctx", axis=0, tiled=True),
            lax.all_gather(document_index, "ctx", axis=0, tiled=True),
        )
        attended_rows, row_max, row_sum = attend_forward(
            query_matrix, token_index, document_index, all_kv, all_segments, block_rows
        )
        att_low = attended_rows.reshape(token_count, query_total_width).astype(jnp.bfloat16)
        residual = inputs + jnp.dot(att_low, w_out, preferred_element_type=jnp.float32)
        normed2, scale2, hidden2 = rms_forward(residual, mlp_gain)
        hidden2 = hidden2.astype(jnp.bfloat16)
        gate_up = jnp.dot(hidden2, w_gate_up, preferred_element_type=jnp.float32)
        gate_part = gate_up[:, :FF]
        up_part = gate_up[:, FF:]
        sigmoid = jax.nn.sigmoid(gate_part)
        silu_gate = gate_part * sigmoid
        act_low = (silu_gate * up_part).astype(jnp.bfloat16)
        layer_outs.append(
            (residual + jnp.dot(act_low, w_down, preferred_element_type=jnp.float32)).astype(
                jnp.bfloat16
            )
        )
        back_qkv, back_out, back_gate_up, back_down = unpack(
            (
                lax.all_gather(qkv_weight, ("dp", "ctx"), axis=0, tiled=True),
                lax.all_gather(out_weight, ("dp", "ctx"), axis=0, tiled=True),
                lax.all_gather(gate_up_weight, ("dp", "ctx"), axis=0, tiled=True),
                lax.all_gather(down_weight, ("dp", "ctx"), axis=0, tiled=True),
            )
        )
        back_kv, back_segments = (
            lax.all_gather(local_kv, "ctx", axis=0, tiled=True),
            lax.all_gather(document_index, "ctx", axis=0, tiled=True),
        )
        cotangent = out_grad[micro_step, 0]
        grad_down = grad_down + lax.dot_general(
            act_low, cotangent, CONTRACT_ROWS, preferred_element_type=jnp.float32
        )
        grad_act = lax.dot_general(
            cotangent, back_down, CONTRACT_COLS, preferred_element_type=jnp.float32
        )
        grad_gate = grad_act * up_part * sigmoid * (1.0 + gate_part * (1.0 - sigmoid))
        grad_up = grad_act * silu_gate
        grad_gu = jnp.concatenate([grad_gate, grad_up], axis=1).astype(jnp.bfloat16)
        grad_gate_up = grad_gate_up + lax.dot_general(
            hidden2, grad_gu, CONTRACT_ROWS, preferred_element_type=jnp.float32
        )
        grad_hidden2 = lax.dot_general(
            grad_gu, back_gate_up, CONTRACT_COLS, preferred_element_type=jnp.float32
        )
        back_mlp, gain_part2 = rms_backward(grad_hidden2, normed2, scale2, mlp_gain)
        grad_gain2 = grad_gain2 + gain_part2
        grad_mid = cotangent.astype(jnp.float32) + back_mlp
        grad_mid_low = grad_mid.astype(jnp.bfloat16)
        grad_out = grad_out + lax.dot_general(
            att_low, grad_mid_low, CONTRACT_ROWS, preferred_element_type=jnp.float32
        )
        attention_gradient = lax.dot_general(
            grad_mid_low, back_out, CONTRACT_COLS, preferred_element_type=jnp.float32
        )
        attention_gradient = attention_gradient.astype(jnp.bfloat16).reshape(
            token_count, KEY_VALUE_HEADS, query_groups, HEAD_SIZE
        )
        delta = jnp.sum(attention_gradient.astype(jnp.float32) * attended_rows, axis=-1)
        grad_query, grad_kv = attend_backward(
            query_matrix,
            token_index,
            document_index,
            back_kv,
            back_segments,
            row_max,
            row_sum,
            attention_gradient,
            delta,
            block_rows,
        )
        owned_key_value = lax.psum_scatter(
            grad_kv.astype(jnp.bfloat16), "ctx", scatter_dimension=0, tiled=True
        ).astype(jnp.float32)
        key_gradient = rotary_reverse(
            owned_key_value[:, :key_value_width].reshape(token_count, KEY_VALUE_HEADS, HEAD_SIZE),
            cosine_table,
            sine_table,
        )
        grad_query = rotary_reverse(
            grad_query.reshape(token_count, QUERY_HEADS, HEAD_SIZE), cosine_table, sine_table
        )
        grad_qkv_low = jnp.concatenate(
            [
                grad_query.reshape(token_count, query_total_width),
                key_gradient.reshape(token_count, key_value_width),
                owned_key_value[:, key_value_width:],
            ],
            axis=1,
        ).astype(jnp.bfloat16)
        grad_bias = grad_bias + jnp.sum(grad_qkv_low.astype(jnp.float32), axis=0)
        grad_qkv = grad_qkv + lax.dot_general(
            hidden1, grad_qkv_low, CONTRACT_ROWS, preferred_element_type=jnp.float32
        )
        grad_hidden1 = lax.dot_general(
            grad_qkv_low, back_qkv, CONTRACT_COLS, preferred_element_type=jnp.float32
        )
        back_attn, gain_part1 = rms_backward(grad_hidden1, normed1, scale1, attn_gain)
        grad_gain1 = grad_gain1 + gain_part1
        input_grads.append(grad_mid + back_attn)
    grad_list = (grad_qkv, grad_out, grad_gate_up, grad_down)
    widths = [item.size // device_count for item in grad_list]
    stacked = jnp.concatenate([item.reshape(device_count, -1) for item in grad_list], axis=1)
    mine = lax.psum_scatter(stacked, ("dp", "ctx"), scatter_dimension=0, tiled=True).reshape(-1)
    offsets = [0, widths[0], widths[0] + widths[1], widths[0] + widths[1] + widths[2]]
    shares = [mine[offsets[k] : offsets[k] + widths[k]] for k in range(4)]
    small_sums = lax.psum((grad_gain1, grad_bias, grad_gain2), ("dp", "ctx"))
    return (
        jnp.stack(layer_outs)[:, None],
        jnp.stack(input_grads)[:, None],
        small_sums[0],
        shares[0],
        small_sums[1],
        shares[1],
        small_sums[2],
        shares[2],
        shares[3],
    )


def together(*items):
    return lax.optimization_barrier(items)


class Links:
    def __init__(self):
        self.rows, self.cores = lax.axis_size("y"), lax.axis_size("core")
        self.deep, self.wide = lax.axis_size("z"), lax.axis_size("x")
        self.dp, self.ctx = self.rows * self.cores, self.deep * self.wide
        self.y, self.core = lax.axis_index("y"), lax.axis_index("core")
        self.z, self.x = lax.axis_index("z"), lax.axis_index("x")
        self.me_dp, self.me_ctx = lax.axis_index(("y", "core")), lax.axis_index(("z", "x"))

    def shift(self, item, axis, step=1):
        size = lax.axis_size(axis)
        if step % size == 0:
            return item
        return lax.ppermute(item, axis, [(k, (k + step) % size) for k in range(size)])

    def core_step(self, item):
        return self.shift(item, "core")

    def y_step(self, item, step=1):
        return self.shift(item, "y", step)

    def broadcast(self, item, axes):
        copies = jnp.broadcast_to(item, (lax.axis_size(axes), *item.shape))
        return lax.all_to_all(copies, axes, 0, 0)

    def spread_x(self, part):
        return [self.shift(part, "x", step) for step in range(self.wide)]

    def ring_x(self, held, moving):
        return [old + self.spread_x(item) for old, item in zip(held, moving, strict=True)]

    def ring_z(self, moving):
        return tuple(self.shift(item, "z") for item in moving)

    def near_dp(self):
        return [
            (self.y - far) % self.rows * self.cores + (self.core - core) % self.cores
            for far in range(self.rows)
            for core in range(self.cores)
        ]

    def near_ctx(self):
        return [
            (self.z - back) % self.deep * self.wide + (self.x - across) % self.wide
            for back in range(self.deep)
            for across in range(self.wide)
        ]

    def scatter_near(self, parts):
        return jnp.sum(lax.all_to_all(parts, ("z", "x"), 0, 0).astype(jnp.float32), axis=0)

    def sum_x(self, parts):
        total = parts[0].astype(jnp.float32)
        for across in range(1, self.wide):
            total = total + self.shift(parts[across], "x", -across).astype(jnp.float32)
        return total

    def gather_y(self, item):
        return jnp.stack([item] + [self.y_step(item, step) for step in range(1, self.rows)])

    def scatter_core(self, whole):
        return whole[0].astype(jnp.float32) + self.core_step(whole[1]).astype(jnp.float32)

    def scatter_y(self, pair, low):
        total = pair[0]
        for step in range(1, self.rows):
            total = total + self.y_step(pair[step].astype(low), -step).astype(jnp.float32)
        return total

    def exchange_dp(self, whole):
        came = []
        for far in range(self.rows):
            for core in range(self.cores):
                to_y, to_core = (self.y + far) % self.rows, (self.core + core) % self.cores
                part = lax.dynamic_index_in_dim(whole, to_y * self.cores + to_core, 0, False)
                size = self.dp
                pairs = []
                for k in range(size):
                    there = (k // self.cores + far) % self.rows * self.cores
                    pairs.append((k, there + (k + core) % self.cores))
                came.append(lax.ppermute(part, ("y", "core"), pairs) if far or core else part)
        return came

    def hand_back(self, parts):
        came = []
        for far in range(self.rows):
            for core in range(self.cores):
                pairs = []
                for k in range(self.dp):
                    there = (k // self.cores - far) % self.rows * self.cores
                    pairs.append((k, there + (k - core) % self.cores))
                part = parts[far * self.cores + core]
                came.append(lax.ppermute(part, ("y", "core"), pairs) if far or core else part)
        came = jnp.stack(came)
        order = [
            (dp // self.cores - self.y) % self.rows * self.cores + (dp - self.core) % self.cores
            for dp in range(self.dp)
        ]
        return [lax.dynamic_index_in_dim(came, k, 0, False) for k in order]

    def sum_dp(self, item):
        for axis in ("core", "y"):
            step, size = 1, lax.axis_size(axis)
            while step < size:
                pairs = [(k, k ^ step) for k in range(size)]
                item = item + lax.ppermute(item, axis, pairs)
                step *= 2
        return item


def allowed_bias(slot_ref, low_ref, first_ref, bias_ref):
    tokens = bias_ref.shape[1]
    query = first_ref[0] + lax.broadcasted_iota(jnp.int32, (tokens, tokens), 1)
    for slot in range(bias_ref.shape[0] // tokens):
        keys = slot_ref[slot] * tokens + lax.broadcasted_iota(jnp.int32, (tokens, tokens), 0)
        allowed = (keys >= low_ref[...]) & (keys <= query)
        bias_ref[slot * tokens : (slot + 1) * tokens, :] = jnp.where(allowed, 0.0, NEGATIVE)


def head_rows(ref, head):
    return ref[head * HEAD_SIZE : (head + 1) * HEAD_SIZE, :]


def attention_kernel(slot_ref, first_ref, low_ref, q_ref, kv_ref, att_ref, stat_ref, bias_ref):
    allowed_bias(slot_ref, low_ref, first_ref, bias_ref)
    kv_cols = jnp.concatenate([kv_ref[j] for j in range(kv_ref.shape[0])], axis=1)
    groups = QUERY_HEADS // KEY_VALUE_HEADS
    half = KEY_VALUE_HEADS * HEAD_SIZE
    key_rows = kv_cols[:half].T
    for kv_head in range(KEY_VALUE_HEADS):
        key = key_rows[:, kv_head * HEAD_SIZE : (kv_head + 1) * HEAD_SIZE]
        value = kv_cols[half + kv_head * HEAD_SIZE : half + (kv_head + 1) * HEAD_SIZE]
        for head in range(kv_head * groups, (kv_head + 1) * groups):
            score = jnp.dot(key, head_rows(q_ref, head), preferred_element_type=jnp.float32)
            score = score * HEAD_SIZE ** (-0.5) + bias_ref[...]
            top = jnp.max(score, axis=0, keepdims=True)
            weights = jnp.exp(score - top)
            total = jnp.sum(weights, axis=0, keepdims=True)
            out = jnp.dot(value, weights.astype(jnp.bfloat16), preferred_element_type=jnp.float32)
            att_ref[head * HEAD_SIZE : (head + 1) * HEAD_SIZE, :] = out / total
            stat_ref[head : head + 1, :] = top + jnp.log(total)


def attention_back_kernel(
    slot_ref,
    first_ref,
    low_ref,
    q_ref,
    kv_ref,
    att_ref,
    stat_ref,
    datt_ref,
    dq_ref,
    dkv_ref,
    bias_ref,
    qs_ref,
    das_ref,
    ds_ref,
    p_ref,
):
    allowed_bias(slot_ref, low_ref, first_ref, bias_ref)
    kv_cols = jnp.concatenate([kv_ref[j] for j in range(kv_ref.shape[0])], axis=1)
    tokens = q_ref.shape[1]
    groups = QUERY_HEADS // KEY_VALUE_HEADS
    half = KEY_VALUE_HEADS * HEAD_SIZE
    scale = HEAD_SIZE ** (-0.5)
    rows = kv_cols.T
    results = []
    for kv_head in range(KEY_VALUE_HEADS):
        own = slice(kv_head * HEAD_SIZE, (kv_head + 1) * HEAD_SIZE)
        key = rows[:, own]
        value = rows[:, half + kv_head * HEAD_SIZE : half + (kv_head + 1) * HEAD_SIZE]
        key_cols = kv_cols[own]
        for place in range(groups):
            head = kv_head * groups + place
            lanes = slice(place * tokens, (place + 1) * tokens)
            query = head_rows(q_ref, head)
            datt = head_rows(datt_ref, head)
            qs_ref[:, lanes] = query
            das_ref[:, lanes] = datt
            delta = jnp.sum(
                datt.astype(jnp.float32) * head_rows(att_ref, head), axis=0, keepdims=True
            )
            score = jnp.dot(key, query, preferred_element_type=jnp.float32)
            prob = jnp.exp(score * scale + bias_ref[...] - stat_ref[head : head + 1, :])
            dprob = jnp.dot(value, datt, preferred_element_type=jnp.float32)
            dscore = (prob * (dprob - delta)).astype(jnp.bfloat16)
            ds_ref[:, lanes] = dscore
            p_ref[:, lanes] = prob.astype(jnp.bfloat16)
            dq_ref[head * HEAD_SIZE : (head + 1) * HEAD_SIZE, :] = (
                jnp.dot(key_cols, dscore, preferred_element_type=jnp.float32) * scale
            )
        results.append(
            lax.dot_general(
                ds_ref[...], qs_ref[...], CONTRACT_COLS, preferred_element_type=jnp.float32
            )
            * scale
        )
        results.append(
            lax.dot_general(
                p_ref[...], das_ref[...], CONTRACT_COLS, preferred_element_type=jnp.float32
            )
        )
    order = results[0::2] + results[1::2]
    out = jnp.concatenate(order, axis=1).astype(jnp.bfloat16)
    for j in range(dkv_ref.shape[0]):
        dkv_ref[j] = out[j * tokens : (j + 1) * tokens]


def attention_specs(width, pieces, kv_width, tokens):
    smem = pl.BlockSpec(memory_space=pltpu.SMEM)
    low = pl.BlockSpec((pl.Squeezed(), 1, tokens), lambda mb: (mb, 0, 0))
    cols = pl.BlockSpec((width, tokens), lambda mb: (0, mb))
    kv = pl.BlockSpec((pieces, kv_width, tokens), lambda mb: (0, 0, mb))
    stat = pl.BlockSpec((QUERY_HEADS, tokens), lambda mb: (0, mb))
    return smem, low, cols, kv, stat


def attend(slots, first, low, q_cols, kv_all, batches):
    width, total = q_cols.shape
    tokens = total // batches
    pieces, kv_width, _ = kv_all.shape
    smem, low_spec, cols, kv, stat = attention_specs(width, pieces, kv_width, tokens)
    return pl.pallas_call(
        attention_kernel,
        grid=(batches,),
        in_specs=[smem, smem, low_spec, cols, kv],
        out_specs=[cols, stat],
        out_shape=[
            jax.ShapeDtypeStruct((width, total), jnp.float32),
            jax.ShapeDtypeStruct((QUERY_HEADS, total), jnp.float32),
        ],
        scratch_shapes=[pltpu.VMEM((pieces * tokens, tokens), jnp.float32)],
        compiler_params=pltpu.CompilerParams(vmem_limit_bytes=40 * 2**20),
        cost_estimate=pl.CostEstimate(
            flops=4 * total * pieces * tokens * width,
            bytes_accessed=8 * total * width,
            transcendentals=total * pieces * tokens * QUERY_HEADS,
        ),
        name="attention",
    )(slots, first, low, q_cols, kv_all)


def attend_back(slots, first, low, q_cols, kv_all, att_cols, stats, datt_cols, batches):
    width, total = q_cols.shape
    tokens = total // batches
    pieces, kv_width, _ = kv_all.shape
    groups = QUERY_HEADS // KEY_VALUE_HEADS
    keys = pieces * tokens
    smem, low_spec, cols, kv, stat = attention_specs(width, pieces, kv_width, tokens)
    return pl.pallas_call(
        attention_back_kernel,
        grid=(batches,),
        in_specs=[smem, smem, low_spec, cols, kv, cols, stat, cols],
        out_specs=[
            cols,
            pl.BlockSpec((pieces, pl.Squeezed(), tokens, kv_width), lambda mb: (0, mb, 0, 0)),
        ],
        out_shape=[
            jax.ShapeDtypeStruct((width, total), jnp.float32),
            jax.ShapeDtypeStruct((pieces, batches, tokens, kv_width), jnp.bfloat16),
        ],
        scratch_shapes=[
            pltpu.VMEM((keys, tokens), jnp.float32),
            pltpu.VMEM((HEAD_SIZE, groups * tokens), jnp.bfloat16),
            pltpu.VMEM((HEAD_SIZE, groups * tokens), jnp.bfloat16),
            pltpu.VMEM((keys, groups * tokens), jnp.bfloat16),
            pltpu.VMEM((keys, groups * tokens), jnp.bfloat16),
        ],
        compiler_params=pltpu.CompilerParams(vmem_limit_bytes=48 * 2**20),
        cost_estimate=pl.CostEstimate(
            flops=10 * total * keys * width,
            bytes_accessed=14 * total * width,
            transcendentals=total * keys * QUERY_HEADS,
        ),
        name="attention_back",
    )(slots, first, low, q_cols, kv_all, att_cols, stats, datt_cols)


def forward_kernel(
    near_ref,
    far_ref,
    near_dy_ref,
    far_dy_ref,
    gate_up_ref,
    down_ref,
    pick_ref,
    hidden_ref,
    act_ref,
    dgu_ref,
    dhidden_ref,
):
    first = pl.program_id(0) < pl.num_programs(0) // 2
    hidden = jnp.where(first, near_ref[...], far_ref[...])
    dy = jnp.where(first, near_dy_ref[...], far_dy_ref[...])
    hidden = dot32(hidden, pick_ref[...]).astype(jnp.bfloat16)
    hidden_ref[...] = hidden
    own_ff = down_ref.shape[0]
    gate_up = dot32(hidden, gate_up_ref[...])
    gate, up = gate_up[:, :own_ff], gate_up[:, own_ff:]
    sigmoid = jax.nn.sigmoid(gate)
    silu = gate * sigmoid
    act_ref[...] = (silu * up).astype(jnp.bfloat16)
    dact = dot32(dy, down_ref[...], CONTRACT_COLS)
    dgate = dact * up * sigmoid * (1.0 + gate * (1.0 - sigmoid))
    dgu = jnp.concatenate([dgate, dact * silu], axis=1).astype(jnp.bfloat16)
    dgu_ref[...] = dgu
    dhidden = dot32(dgu, gate_up_ref[...], CONTRACT_COLS).astype(jnp.bfloat16)
    dhidden_ref[...] = dot32(dhidden, pick_ref[...], CONTRACT_COLS).astype(jnp.bfloat16)


def feed_forward(hidden, dy, w_gate_up, w_down, pick, tile):
    half, width = hidden[0].shape
    own_ff = w_down.shape[0]
    steps = half // tile
    near = pl.BlockSpec((tile, width), lambda i: (jnp.minimum(i, steps - 1), 0))
    far = pl.BlockSpec((tile, width), lambda i: (jnp.maximum(i - steps, 0), 0))

    def whole(item):
        return pl.BlockSpec(item.shape, lambda i: (0, 0), pipeline_mode=pl.Buffered(1))

    def rows(columns):
        return pl.BlockSpec((tile, columns), lambda i: (i, 0))

    widths = (width, own_ff, 2 * own_ff, width)
    return pl.pallas_call(
        forward_kernel,
        grid=(2 * steps,),
        in_specs=[near, far, near, far, whole(w_gate_up), whole(w_down), whole(pick)],
        out_specs=[rows(columns) for columns in widths],
        out_shape=[jax.ShapeDtypeStruct((2 * half, columns), jnp.bfloat16) for columns in widths],
        compiler_params=pltpu.CompilerParams(vmem_limit_bytes=48 * 2**20),
        cost_estimate=pl.CostEstimate(
            flops=4 * half * width * (5 * own_ff + 2 * width),
            bytes_accessed=8 * half * (2 * width + 2 * own_ff) + 6 * width * own_ff,
            transcendentals=2 * half * own_ff,
        ),
        name="feed_forward",
    )(*hidden, *dy, w_gate_up, w_down, pick)


def one_hot_order(order, size):
    rows = lax.broadcasted_iota(jnp.int32, (size, order.shape[0]), 0)
    return (rows == order[None, :]).astype(jnp.bfloat16)


def dot32(left, right, dims=(((1,), (0,)), ((), ()))):
    return lax.dot_general(left, right, dims, preferred_element_type=jnp.float32)


def rope_columns(cols, cosine, sine):
    first, second = cols[:, 0], cols[:, 1]
    return jnp.stack([first * cosine - second * sine, second * cosine + first * sine], axis=1)


def rope_columns_back(cols, cosine, sine):
    first, second = cols[:, 0], cols[:, 1]
    return jnp.stack([first * cosine + second * sine, second * cosine - first * sine], axis=1)


def short_body(
    tokens,
    doc_lengths,
    attn_gain,
    qkv_weight,
    qkv_bias,
    out_weight,
    mlp_gain,
    gate_up_weight,
    down_weight,
    out_grad,
):
    links = Links()
    width = attn_gain.shape[0]
    qkv_width = qkv_bias.shape[0]
    query_width = QUERY_HEADS * HEAD_SIZE
    kv_width = KEY_VALUE_HEADS * HEAD_SIZE
    half = HEAD_SIZE // 2
    batches, token_count = tokens.shape[0], tokens.shape[2]
    total = batches * token_count
    devices = links.dp * links.ctx
    piece = width // devices
    own_ff = FF // links.dp
    first_row = links.me_ctx * token_count

    padded = -(-piece // 16) * 16
    key_slots = jnp.stack(
        [
            z * links.wide + (links.x - across) % links.wide
            for across in range(links.wide)
            for z in range(links.deep)
        ]
    ).astype(jnp.int32)
    row = jnp.arange(padded, dtype=jnp.int32)
    near_dp = jnp.stack(links.near_dp()).astype(jnp.int32)
    near_ctx = jnp.stack(links.near_ctx()).astype(jnp.int32)
    rows_order = near_dp.reshape(links.rows, 2).T.reshape(-1)
    owner = rows_order[:, None] * links.ctx + jnp.arange(links.ctx, dtype=jnp.int32)[None, :]
    attn_order = jnp.where(row < piece, owner[:, :, None] * piece + row, -1).reshape(-1)
    attn_pick = one_hot_order(attn_order, width)
    owner = near_dp[None, :] * links.ctx + near_ctx[:, None]
    mlp_order = (owner[:, :, None] * piece + jnp.arange(piece, dtype=jnp.int32)).reshape(-1)
    mlp_pick = one_hot_order(mlp_order, width)

    def own_rows(flat, columns):
        return jnp.pad(flat.reshape(piece, columns), ((0, padded - piece), (0, 0)))

    def rows_y(near):
        return jnp.concatenate([near] + [links.y_step(near, k) for k in range(1, links.rows)])

    def rows_core(held):
        return jnp.concatenate([held, links.core_step(held)])

    def back_core(grad):
        mine, other = jnp.split(grad, 2)
        return mine.astype(jnp.float32) + links.core_step(other).astype(jnp.float32)

    def back_y(pair):
        parts = jnp.split(pair, links.rows)
        total = parts[0]
        for step in range(1, links.rows):
            there = links.y_step(parts[step].astype(jnp.bfloat16), -step)
            total = total + there.astype(jnp.float32)
        return total.astype(jnp.bfloat16).reshape(links.ctx, padded, -1)

    w_qkv = links.broadcast(own_rows(qkv_weight, qkv_width), ("z", "x")).reshape(-1, qkv_width)
    gate_up_rows = gate_up_weight.reshape(piece, 2, links.dp, own_ff)
    gate_up_rows = gate_up_rows.transpose(2, 0, 1, 3).reshape(links.dp, piece, 2 * own_ff)
    parts = links.exchange_dp(gate_up_rows)
    all_cotangent = links.gather_y(out_grad[:, 0].reshape(total, width))
    w_qkv, all_cotangent, down_part, *parts = together(
        w_qkv, all_cotangent, down_weight.reshape(-1, width), *parts
    )

    w_qkv = rows_y(w_qkv)
    moving = (
        jnp.stack(parts).reshape(links.dp * piece, 2 * own_ff),
        down_part,
    )
    held = links.ring_x([[], []], moving)
    moving = links.ring_z(moving)
    w_out = links.broadcast(own_rows(out_weight, width), ("z", "x")).reshape(-1, width)
    w_qkv = rows_core(w_qkv)

    cotangent = out_grad[:, 0].reshape(total, width)

    inputs = tokens[:, 0].reshape(total, width).astype(jnp.float32)
    layouts = [doc_layout(doc_lengths[b, 0], first_row, token_count) for b in range(batches)]
    token_index = layouts[0][0]
    positions = jnp.concatenate([item[2] for item in layouts])
    low = jnp.stack([token_index - item[2] for item in layouts])[:, None, :]
    first = jnp.reshape(first_row, (1,)).astype(jnp.int32)
    freqs = ROPE_THETA ** (-(2.0 * jnp.arange(half, dtype=jnp.float32)) / HEAD_SIZE)
    angles = freqs[:, None] * positions.astype(jnp.float32)[None, :]
    cosine, sine = jnp.cos(angles), jnp.sin(angles)

    normed1, scale1, hidden1 = rms_forward(inputs, attn_gain)
    hidden1 = dot32(hidden1.astype(jnp.bfloat16), attn_pick).astype(jnp.bfloat16)
    qkv_cols = dot32(w_qkv, hidden1, (((0,), (1,)), ((), ()))) + qkv_bias[:, None]
    turned = rope_columns(
        qkv_cols[: query_width + kv_width].reshape(-1, 2, half, total), cosine, sine
    )
    turned = turned.reshape(query_width + kv_width, total).astype(jnp.bfloat16)
    q_cols = turned[:query_width]
    kv_cols = jnp.concatenate(
        [turned[query_width:], qkv_cols[query_width + kv_width :].astype(jnp.bfloat16)]
    )
    kv_all = links.broadcast(kv_cols, "z")
    moving, _ = together(moving, kv_cols)
    held = links.ring_x(held, moving)
    kv_all, w_out, moving = together(kv_all, w_out, moving)

    kv_all = jnp.concatenate(links.spread_x(kv_all))
    w_out = rows_y(w_out)
    for step in range(2, links.deep - 1):
        moving = links.ring_z(moving)
        if step > 2:
            held = links.ring_x(held, moving)
    moving, _ = together(moving, kv_all)
    kv_all, w_out, cotangent = together(kv_all, w_out, cotangent)

    w_out = rows_core(w_out)
    held = links.ring_x(held, moving)
    moving = links.ring_z(moving)
    att_cols, stats = attend(key_slots, first, low, q_cols, kv_all, batches)
    att_cols, w_out, all_cotangent = together(att_cols, w_out, all_cotangent)

    att_low = dot32(
        att_cols.astype(jnp.bfloat16), attn_pick, (((0,), (0,)), ((), ()))
    ).astype(jnp.bfloat16)
    residual = inputs + dot32(att_low, w_out)

    normed2, scale2, hidden2 = rms_forward(residual, mlp_gain)
    hidden2 = hidden2.astype(jnp.bfloat16)
    near_hidden2 = links.gather_y(hidden2).reshape(-1, width)
    moving, _ = together(moving, hidden2)
    w_parts, down_parts = links.ring_x(held, moving)
    w_gate_up = jnp.concatenate(w_parts)
    w_down = jnp.zeros((links.ctx, own_ff // links.ctx, width), jnp.bfloat16)
    for k, part in enumerate(down_parts):
        w_down = lax.dynamic_update_index_in_dim(w_down, part, near_ctx[k], 0)
    w_down = w_down.reshape(own_ff, width)
    near_dy = all_cotangent.reshape(-1, width)
    far_dy = links.core_step(near_dy)
    near_hidden2, far_dy, w_gate_up, w_down = together(near_hidden2, far_dy, w_gate_up, w_down)
    far_hidden2 = links.core_step(near_hidden2)
    all_hidden2, act_low, dgu, dhidden2 = feed_forward(
        (near_hidden2, far_hidden2), (near_dy, far_dy), w_gate_up, w_down, mlp_pick, total
    )
    all_cotangent = jnp.concatenate([near_dy, far_dy])
    dhidden2, dgu, act_low = together(dhidden2, dgu, act_low)

    dhidden2 = links.scatter_core(dhidden2.reshape(2, links.rows, total, width))
    grad_gate_up = dot32(all_hidden2, dgu, CONTRACT_ROWS).astype(jnp.bfloat16)
    grad_down = dot32(act_low, all_cotangent, CONTRACT_ROWS).astype(jnp.bfloat16)
    dhidden2, grad_gate_up, grad_down, act_low = together(
        dhidden2, grad_gate_up, grad_down, act_low
    )

    blocks = grad_gate_up.reshape(links.deep, links.wide, -1, 2 * own_ff)
    down_blocks = grad_down.reshape(links.ctx, own_ff // links.ctx, width)

    def across(blocks, back):
        gate_up_blocks, down_blocks = blocks
        places = [near_ctx[back * links.wide + step] for step in range(links.wide)]
        down = [lax.dynamic_index_in_dim(down_blocks, k, 0, False) for k in places]
        return links.sum_x(gate_up_blocks[back]), links.sum_x(down)

    def lowered(share):
        return [item.astype(jnp.bfloat16) for item in share]

    def plus(share, moved):
        return tuple(a + b.astype(jnp.float32) for a, b in zip(share, moved, strict=True))

    def ring(share, other):
        return plus(other, links.ring_z(lowered(share)))

    blocks = (blocks, down_blocks)
    share = across(blocks, 1)
    dhidden2 = links.scatter_y(dhidden2, jnp.bfloat16)
    out_part = dot32(act_low, w_down).astype(jnp.bfloat16)

    back_mlp, gain2_grad = rms_backward(dhidden2, normed2, scale2, mlp_gain)
    dmid = cotangent.astype(jnp.float32) + back_mlp
    dmid_low = dmid.astype(jnp.bfloat16)
    datt = dot32(dmid_low, w_out, CONTRACT_COLS).astype(jnp.bfloat16)
    datt_cols = dot32(attn_pick, datt, CONTRACT_COLS).astype(jnp.bfloat16)
    grad_out = dot32(att_low, dmid_low, CONTRACT_ROWS).astype(jnp.bfloat16)
    share, blocks, datt_cols, out_part = together(share, blocks, datt_cols, out_part)
    share = ring(share, across(blocks, 2))
    out_part = links.scatter_core(out_part.reshape(2, links.rows, total, width))
    grad_out = back_core(grad_out)
    dq_cols, dkv = attend_back(
        key_slots, first, low, q_cols, kv_all, att_cols, stats, datt_cols, batches
    )
    dq_cols, dkv, share, blocks, grad_out, out_part = together(
        dq_cols, dkv, share, blocks, grad_out, out_part
    )

    dkv = dkv.reshape(links.wide, links.deep, total, 2 * kv_width)
    dkv = links.sum_x(dkv).astype(jnp.bfloat16)
    for back in range(3, links.deep - 1):
        share = ring(share, across(blocks, back))
    share = links.ring_z(lowered(share))
    dkv, blocks, out_part = together(dkv, blocks, out_part)

    layer_out = residual + links.scatter_y(out_part, jnp.bfloat16)
    own_dkv = lax.all_to_all(dkv, "z", 0, 0)
    own_dkv, share = together(own_dkv, share)
    own_dkv = jnp.sum(own_dkv.astype(jnp.float32), axis=0).T
    share = plus(across(blocks, links.deep - 1), share)
    dq = rope_columns_back(dq_cols.reshape(-1, 2, half, total), cosine, sine)
    dq = dq.reshape(query_width, total).astype(jnp.bfloat16)
    grad_q = back_core(dot32(hidden1, dq, (((0,), (1,)), ((), ()))).astype(jnp.bfloat16))
    grad_out = back_y(grad_out)
    grad_q, grad_out = together(grad_q, grad_out)

    grad_q = jnp.concatenate([back_y(grad_q), grad_out], axis=2)
    share, blocks, grad_q = together(share, blocks, grad_q)
    share = ring(share, across(blocks, 0))
    dk = rope_columns_back(own_dkv[:kv_width].reshape(-1, 2, half, total), cosine, sine)
    dkv = jnp.concatenate([dk.reshape(kv_width, total), own_dkv[kv_width:]]).astype(jnp.bfloat16)
    grad_kv = dot32(hidden1, dkv, (((0,), (1,)), ((), ()))).astype(jnp.bfloat16)
    grad_kv = back_y(back_core(grad_kv))
    dqkv = jnp.concatenate([dq, dkv])
    bias_grad = jnp.sum(dqkv.astype(jnp.float32), axis=1)
    dhidden1 = dot32(dqkv, w_qkv, (((0,), (1,)), ((), ())))
    (top,) = together(dhidden1.astype(jnp.bfloat16))
    rest = (dhidden1 - top.astype(jnp.float32)).astype(jnp.bfloat16)
    dhidden1 = dot32(top, attn_pick, CONTRACT_COLS) + dot32(rest, attn_pick, CONTRACT_COLS)
    back_attn, gain1_grad = rms_backward(dhidden1, normed1, scale1, attn_gain)
    input_grad = dmid + back_attn
    small = links.sum_dp(jnp.concatenate([gain1_grad, bias_grad, gain2_grad]).reshape(-1, 128))
    (high,) = together(small.astype(jnp.bfloat16))
    rest = (small - high.astype(jnp.float32)).astype(jnp.bfloat16)
    sums = jnp.concatenate([high, rest]).reshape(-1)
    grads = jnp.concatenate([grad_q, grad_kv], axis=2)
    columns = grads.shape[2]
    sums = jnp.pad(sums, (0, (padded - piece) * columns - sums.size)).reshape(-1, columns)
    grads = links.scatter_near(grads + jnp.pad(sums, ((piece, 0), (0, 0))))
    share, down_share = share
    parts = share.astype(jnp.bfloat16).reshape(links.dp, piece, 2 * own_ff)
    parts = jnp.stack(links.hand_back(parts)).reshape(links.dp, piece, 2, own_ff)

    gate_up_share = parts.transpose(1, 2, 0, 3).astype(jnp.float32).reshape(-1)
    small = grads[piece:].reshape(-1)[: 2 * small.size].reshape(2, -1).sum(axis=0)
    grad_q, grad_out, grad_kv = jnp.split(grads[:piece], (query_width, query_width + width), axis=1)
    qkv_share = jnp.concatenate([grad_q, grad_kv], axis=1).reshape(-1)
    out_share = grad_out.reshape(-1)
    return (
        layer_out.astype(jnp.bfloat16).reshape(batches, 1, token_count, width),
        input_grad.reshape(batches, 1, token_count, width),
        small[:width],
        qkv_share,
        small[width : width + qkv_width],
        out_share,
        small[width + qkv_width :],
        gate_up_share,
        down_share.reshape(-1),
    )


def fits(mesh):
    dp, ctx = mesh.shape["dp"], mesh.shape["ctx"]
    devices = dp * ctx
    if dp % 2 or ctx % (dp // 2) or ctx // (dp // 2) < 3:
        return False
    piece = WIDTH // devices
    spare = (-piece % 16) * 2 * (WIDTH + KEY_VALUE_HEADS * HEAD_SIZE)
    sums = 2 * (3 * WIDTH + 2 * KEY_VALUE_HEADS * HEAD_SIZE)
    return WIDTH % devices == 0 and FF % devices == 0 and sums <= spare


def solution(mesh):
    run, dp, ctx = body, ("dp",), ("ctx",)
    if fits(mesh):
        rows = mesh.shape["dp"] // 2
        shape = (rows, 2, mesh.shape["ctx"] // rows, rows)
        run, dp, ctx = short_body, ("y", "core"), ("z", "x")
        mesh = Mesh(mesh.devices.reshape(shape), (*dp, *ctx))
    return jax.shard_map(
        run,
        mesh=mesh,
        in_specs=(
            P(None, dp, ctx, None),
            P(None, dp, None),
            P(),
            P((*dp, *ctx)),
            P(),
            P((*dp, *ctx)),
            P(),
            P((*dp, *ctx)),
            P((*dp, *ctx)),
            P(None, dp, ctx, None),
        ),
        out_specs=(
            P(None, dp, ctx, None),
            P(None, dp, ctx, None),
            P(),
            P((*dp, *ctx)),
            P(),
            P((*dp, *ctx)),
            P(),
            P((*dp, *ctx)),
            P((*dp, *ctx)),
        ),
        check_vma=False,
    )
```

```python
import jax
import jax.numpy as jnp
from jax import lax
from jax.experimental import pallas as pl
from jax.experimental.pallas import tpu as pltpu
from jax.sharding import Mesh
from jax.sharding import PartitionSpec as P

QUERY_HEADS = 14
KEY_VALUE_HEADS = 2
HEAD_SIZE = 64
FF = 4864
WIDTH = 896


EPSILON = 1e-06
ROPE_THETA = 1000000.0
NEGATIVE = -1e30
CONTRACT_ROWS = (((0,), (0,)), ((), ()))
CONTRACT_COLS = (((1,), (1,)), ((), ()))


def doc_layout(lengths, first_row, token_count):
    token_index = first_row + jnp.arange(token_count, dtype=jnp.int32)
    doc_ends = jnp.cumsum(lengths, dtype=jnp.int32)
    before = doc_ends[None, :] <= token_index[:, None]
    document_index = jnp.sum(before.astype(jnp.int32), axis=1, dtype=jnp.int32)
    doc_start = jnp.sum(jnp.where(before, lengths[None, :], 0), axis=1, dtype=jnp.int32)
    return (token_index, document_index, token_index - doc_start)


def rotation(positions, head_dim):
    freqs = ROPE_THETA ** (-(2.0 * jnp.arange(head_dim // 2, dtype=jnp.float32)) / head_dim)
    angles = positions.astype(jnp.float32)[:, None] * freqs[None, :]
    cosine_table = jnp.concatenate([jnp.cos(angles), jnp.cos(angles)], axis=-1)
    sine_table = jnp.concatenate([jnp.sin(angles), jnp.sin(angles)], axis=-1)
    return (cosine_table[:, None, :], sine_table[:, None, :])


def rotary_apply(heads, cosine_table, sine_table):
    half_dim = heads.shape[-1] // 2
    turned = jnp.concatenate([-heads[..., half_dim:], heads[..., :half_dim]], axis=-1)
    return heads * cosine_table + turned * sine_table


def rotary_reverse(grads, cosine_table, sine_table):
    half_dim = grads.shape[-1] // 2
    weighted = grads * sine_table
    turned = jnp.concatenate([weighted[..., half_dim:], -weighted[..., :half_dim]], axis=-1)
    return grads * cosine_table + turned


def rms_forward(value_rows, gain):
    row_scale = lax.rsqrt(jnp.mean(value_rows * value_rows, axis=-1, keepdims=True) + EPSILON)
    normed = value_rows * row_scale
    return (normed, row_scale, normed * gain)


def rms_backward(grads, normed, row_scale, gain):
    grad_normed = grads * gain
    gain_grad = jnp.sum(grads * normed, axis=0)
    back = row_scale * (
        grad_normed - normed * jnp.mean(grad_normed * normed, axis=-1, keepdims=True)
    )
    return (back, gain_grad)


def block_scores(
    query_matrix, key_block, token_index, document_index, seg_block, key_start, score_scale
):
    score = (
        jnp.einsum("qhgd,khd->qhgk", query_matrix, key_block, preferred_element_type=jnp.float32)
        * score_scale
    )
    key_index = key_start + jnp.arange(key_block.shape[0], dtype=jnp.int32)
    allowed = (seg_block[None, :] == document_index[:, None]) & (
        key_index[None, :] <= token_index[:, None]
    )
    return (score, allowed[:, None, None, :])


def split_blocks(keyvals, key_segment, block_rows, kv_heads, head_dim):
    seq_length = keyvals.shape[0]
    block_count = seq_length // block_rows
    kv_blocks = keyvals.reshape(block_count, block_rows, 2, kv_heads, head_dim)
    seg_blocks = key_segment.reshape(block_count, block_rows)
    starts = jnp.arange(block_count, dtype=jnp.int32) * block_rows
    return (kv_blocks, seg_blocks, starts)


def attend_forward(query_matrix, token_index, document_index, keyvals, key_segment, block_rows):
    kv_heads, head_dim = (query_matrix.shape[1], query_matrix.shape[3])
    score_scale = head_dim ** (-0.5)
    kv_blocks, seg_blocks, starts = split_blocks(
        keyvals, key_segment, block_rows, kv_heads, head_dim
    )

    def stats_step(running, block_item):
        kv_block, seg_block, key_start = block_item
        row_max, row_sum = running
        score, allowed = block_scores(
            query_matrix,
            kv_block[:, 0],
            token_index,
            document_index,
            seg_block,
            key_start,
            score_scale,
        )
        new_max = jnp.maximum(row_max, jnp.max(jnp.where(allowed, score, NEGATIVE), axis=-1))
        weights = jnp.where(allowed, jnp.exp(score - new_max[..., None]), 0.0)
        return ((new_max, row_sum * jnp.exp(row_max - new_max) + jnp.sum(weights, axis=-1)), None)

    stats_init = (
        jnp.full(query_matrix.shape[:3], NEGATIVE, jnp.float32),
        jnp.zeros(query_matrix.shape[:3], jnp.float32),
    )
    (row_max, row_sum), unused = lax.scan(stats_step, stats_init, (kv_blocks, seg_blocks, starts))

    def out_step(running, block_item):
        kv_block, seg_block, key_start = block_item
        score, allowed = block_scores(
            query_matrix,
            kv_block[:, 0],
            token_index,
            document_index,
            seg_block,
            key_start,
            score_scale,
        )
        probability = jnp.where(
            allowed, jnp.exp(score - row_max[..., None]) / row_sum[..., None], 0.0
        )
        return (
            running
            + jnp.einsum(
                "qhgk,khd->qhgd",
                probability.astype(jnp.bfloat16),
                kv_block[:, 1],
                preferred_element_type=jnp.float32,
            ),
            None,
        )

    attended_rows, unused = lax.scan(
        out_step, jnp.zeros(query_matrix.shape, jnp.float32), (kv_blocks, seg_blocks, starts)
    )
    return (attended_rows, row_max, row_sum)


def attend_backward(
    query_matrix,
    token_index,
    document_index,
    keyvals,
    key_segment,
    row_max,
    row_sum,
    attention_gradient,
    delta,
    block_rows,
):
    kv_heads, head_dim = (query_matrix.shape[1], query_matrix.shape[3])
    score_scale = head_dim ** (-0.5)
    seq_length = keyvals.shape[0]
    kv_blocks, seg_blocks, starts = split_blocks(
        keyvals, key_segment, block_rows, kv_heads, head_dim
    )

    def grad_step(running, block_item):
        kv_block, seg_block, key_start = block_item
        grad_query = running
        score, allowed = block_scores(
            query_matrix,
            kv_block[:, 0],
            token_index,
            document_index,
            seg_block,
            key_start,
            score_scale,
        )
        probability = jnp.where(
            allowed, jnp.exp(score - row_max[..., None]) / row_sum[..., None], 0.0
        )
        grad_prob = jnp.einsum(
            "qhgd,khd->qhgk", attention_gradient, kv_block[:, 1], preferred_element_type=jnp.float32
        )
        grad_score = (probability * (grad_prob - delta[..., None])).astype(jnp.bfloat16)
        grad_query = (
            grad_query
            + jnp.einsum(
                "qhgk,khd->qhgd", grad_score, kv_block[:, 0], preferred_element_type=jnp.float32
            )
            * score_scale
        )
        key_gradient = (
            jnp.einsum(
                "qhgk,qhgd->khd", grad_score, query_matrix, preferred_element_type=jnp.float32
            )
            * score_scale
        )
        grad_value = jnp.einsum(
            "qhgk,qhgd->khd",
            probability.astype(jnp.bfloat16),
            attention_gradient,
            preferred_element_type=jnp.float32,
        )
        return (
            grad_query,
            jnp.concatenate(
                [key_gradient.reshape(block_rows, -1), grad_value.reshape(block_rows, -1)], axis=1
            ),
        )

    grad_query, grad_kv = lax.scan(
        grad_step, jnp.zeros(query_matrix.shape, jnp.float32), (kv_blocks, seg_blocks, starts)
    )
    return (grad_query, grad_kv.reshape(seq_length, 2 * kv_heads * head_dim))


def body(
    tokens,
    doc_lengths,
    attn_gain,
    qkv_weight,
    qkv_bias,
    out_weight,
    mlp_gain,
    gate_up_weight,
    down_weight,
    out_grad,
):
    model_width = attn_gain.shape[0]
    qkv_width = qkv_bias.shape[0]
    query_total_width = QUERY_HEADS * HEAD_SIZE
    key_value_width = KEY_VALUE_HEADS * HEAD_SIZE
    query_groups = QUERY_HEADS // KEY_VALUE_HEADS
    token_count = tokens.shape[2]
    seq_length = token_count * lax.axis_size("ctx")
    first_row = lax.axis_index("ctx") * token_count
    block_rows = min(512, seq_length)
    device_count = lax.axis_size(("dp", "ctx"))

    def unpack(gathered):
        flat_qkv, flat_out, flat_gate_up, flat_down = gathered
        return (
            flat_qkv.reshape(model_width, qkv_width),
            flat_out.reshape(query_total_width, model_width),
            flat_gate_up.reshape(model_width, 2 * FF),
            flat_down.reshape(FF, model_width),
        )

    grad_qkv = jnp.zeros((model_width, qkv_width), jnp.float32)
    grad_out = jnp.zeros((query_total_width, model_width), jnp.float32)
    grad_gate_up = jnp.zeros((model_width, 2 * FF), jnp.float32)
    grad_down = jnp.zeros((FF, model_width), jnp.float32)
    grad_gain1 = jnp.zeros((model_width,), jnp.float32)
    grad_gain2 = jnp.zeros((model_width,), jnp.float32)
    grad_bias = jnp.zeros((qkv_width,), jnp.float32)
    layer_outs = []
    input_grads = []
    for micro_step in range(tokens.shape[0]):
        w_qkv, w_out, w_gate_up, w_down = unpack(
            (
                lax.all_gather(qkv_weight, ("dp", "ctx"), axis=0, tiled=True),
                lax.all_gather(out_weight, ("dp", "ctx"), axis=0, tiled=True),
                lax.all_gather(gate_up_weight, ("dp", "ctx"), axis=0, tiled=True),
                lax.all_gather(down_weight, ("dp", "ctx"), axis=0, tiled=True),
            )
        )
        inputs = tokens[micro_step, 0].astype(jnp.float32)
        token_index, document_index, positions = doc_layout(
            doc_lengths[micro_step, 0], first_row, token_count
        )
        cosine_table, sine_table = rotation(positions, HEAD_SIZE)
        normed1, scale1, hidden1 = rms_forward(inputs, attn_gain)
        hidden1 = hidden1.astype(jnp.bfloat16)
        query_key_value = jnp.dot(hidden1, w_qkv, preferred_element_type=jnp.float32) + qkv_bias
        query_matrix = rotary_apply(
            query_key_value[:, :query_total_width].reshape(token_count, QUERY_HEADS, HEAD_SIZE),
            cosine_table,
            sine_table,
        )
        query_matrix = query_matrix.astype(jnp.bfloat16).reshape(
            token_count, KEY_VALUE_HEADS, query_groups, HEAD_SIZE
        )
        key_rows = rotary_apply(
            query_key_value[:, query_total_width : query_total_width + key_value_width].reshape(
                token_count, KEY_VALUE_HEADS, HEAD_SIZE
            ),
            cosine_table,
            sine_table,
        ).astype(jnp.bfloat16)
        value_rows = query_key_value[:, query_total_width + key_value_width :].astype(jnp.bfloat16)
        local_kv = jnp.concatenate(
            [key_rows.reshape(token_count, key_value_width), value_rows], axis=1
        )
        all_kv, all_segments = (
            lax.all_gather(local_kv, "ctx", axis=0, tiled=True),
            lax.all_gather(document_index, "ctx", axis=0, tiled=True),
        )
        attended_rows, row_max, row_sum = attend_forward(
            query_matrix, token_index, document_index, all_kv, all_segments, block_rows
        )
        att_low = attended_rows.reshape(token_count, query_total_width).astype(jnp.bfloat16)
        residual = inputs + jnp.dot(att_low, w_out, preferred_element_type=jnp.float32)
        normed2, scale2, hidden2 = rms_forward(residual, mlp_gain)
        hidden2 = hidden2.astype(jnp.bfloat16)
        gate_up = jnp.dot(hidden2, w_gate_up, preferred_element_type=jnp.float32)
        gate_part = gate_up[:, :FF]
        up_part = gate_up[:, FF:]
        sigmoid = jax.nn.sigmoid(gate_part)
        silu_gate = gate_part * sigmoid
        act_low = (silu_gate * up_part).astype(jnp.bfloat16)
        layer_outs.append(
            (residual + jnp.dot(act_low, w_down, preferred_element_type=jnp.float32)).astype(
                jnp.bfloat16
            )
        )
        back_qkv, back_out, back_gate_up, back_down = unpack(
            (
                lax.all_gather(qkv_weight, ("dp", "ctx"), axis=0, tiled=True),
                lax.all_gather(out_weight, ("dp", "ctx"), axis=0, tiled=True),
                lax.all_gather(gate_up_weight, ("dp", "ctx"), axis=0, tiled=True),
                lax.all_gather(down_weight, ("dp", "ctx"), axis=0, tiled=True),
            )
        )
        back_kv, back_segments = (
            lax.all_gather(local_kv, "ctx", axis=0, tiled=True),
            lax.all_gather(document_index, "ctx", axis=0, tiled=True),
        )
        cotangent = out_grad[micro_step, 0]
        grad_down = grad_down + lax.dot_general(
            act_low, cotangent, CONTRACT_ROWS, preferred_element_type=jnp.float32
        )
        grad_act = lax.dot_general(
            cotangent, back_down, CONTRACT_COLS, preferred_element_type=jnp.float32
        )
        grad_gate = grad_act * up_part * sigmoid * (1.0 + gate_part * (1.0 - sigmoid))
        grad_up = grad_act * silu_gate
        grad_gu = jnp.concatenate([grad_gate, grad_up], axis=1).astype(jnp.bfloat16)
        grad_gate_up = grad_gate_up + lax.dot_general(
            hidden2, grad_gu, CONTRACT_ROWS, preferred_element_type=jnp.float32
        )
        grad_hidden2 = lax.dot_general(
            grad_gu, back_gate_up, CONTRACT_COLS, preferred_element_type=jnp.float32
        )
        back_mlp, gain_part2 = rms_backward(grad_hidden2, normed2, scale2, mlp_gain)
        grad_gain2 = grad_gain2 + gain_part2
        grad_mid = cotangent.astype(jnp.float32) + back_mlp
        grad_mid_low = grad_mid.astype(jnp.bfloat16)
        grad_out = grad_out + lax.dot_general(
            att_low, grad_mid_low, CONTRACT_ROWS, preferred_element_type=jnp.float32
        )
        attention_gradient = lax.dot_general(
            grad_mid_low, back_out, CONTRACT_COLS, preferred_element_type=jnp.float32
        )
        attention_gradient = attention_gradient.astype(jnp.bfloat16).reshape(
            token_count, KEY_VALUE_HEADS, query_groups, HEAD_SIZE
        )
        delta = jnp.sum(attention_gradient.astype(jnp.float32) * attended_rows, axis=-1)
        grad_query, grad_kv = attend_backward(
            query_matrix,
            token_index,
            document_index,
            back_kv,
            back_segments,
            row_max,
            row_sum,
            attention_gradient,
            delta,
            block_rows,
        )
        owned_key_value = lax.psum_scatter(
            grad_kv.astype(jnp.bfloat16), "ctx", scatter_dimension=0, tiled=True
        ).astype(jnp.float32)
        key_gradient = rotary_reverse(
            owned_key_value[:, :key_value_width].reshape(token_count, KEY_VALUE_HEADS, HEAD_SIZE),
            cosine_table,
            sine_table,
        )
        grad_query = rotary_reverse(
            grad_query.reshape(token_count, QUERY_HEADS, HEAD_SIZE), cosine_table, sine_table
        )
        grad_qkv_low = jnp.concatenate(
            [
                grad_query.reshape(token_count, query_total_width),
                key_gradient.reshape(token_count, key_value_width),
                owned_key_value[:, key_value_width:],
            ],
            axis=1,
        ).astype(jnp.bfloat16)
        grad_bias = grad_bias + jnp.sum(grad_qkv_low.astype(jnp.float32), axis=0)
        grad_qkv = grad_qkv + lax.dot_general(
            hidden1, grad_qkv_low, CONTRACT_ROWS, preferred_element_type=jnp.float32
        )
        grad_hidden1 = lax.dot_general(
            grad_qkv_low, back_qkv, CONTRACT_COLS, preferred_element_type=jnp.float32
        )
        back_attn, gain_part1 = rms_backward(grad_hidden1, normed1, scale1, attn_gain)
        grad_gain1 = grad_gain1 + gain_part1
        input_grads.append(grad_mid + back_attn)
    grad_list = (grad_qkv, grad_out, grad_gate_up, grad_down)
    widths = [item.size // device_count for item in grad_list]
    stacked = jnp.concatenate([item.reshape(device_count, -1) for item in grad_list], axis=1)
    mine = lax.psum_scatter(stacked, ("dp", "ctx"), scatter_dimension=0, tiled=True).reshape(-1)
    offsets = [0, widths[0], widths[0] + widths[1], widths[0] + widths[1] + widths[2]]
    shares = [mine[offsets[k] : offsets[k] + widths[k]] for k in range(4)]
    small_sums = lax.psum((grad_gain1, grad_bias, grad_gain2), ("dp", "ctx"))
    return (
        jnp.stack(layer_outs)[:, None],
        jnp.stack(input_grads)[:, None],
        small_sums[0],
        shares[0],
        small_sums[1],
        shares[1],
        small_sums[2],
        shares[2],
        shares[3],
    )


def together(*items):
    return lax.optimization_barrier(items)


class Links:
    def __init__(self):
        self.rows, self.cores = lax.axis_size("y"), lax.axis_size("core")
        self.deep, self.wide = lax.axis_size("z"), lax.axis_size("x")
        self.dp, self.ctx = self.rows * self.cores, self.deep * self.wide
        self.y, self.core = lax.axis_index("y"), lax.axis_index("core")
        self.z, self.x = lax.axis_index("z"), lax.axis_index("x")
        self.me_dp, self.me_ctx = lax.axis_index(("y", "core")), lax.axis_index(("z", "x"))

    def shift(self, item, axis, step=1):
        size = lax.axis_size(axis)
        if step % size == 0:
            return item
        return lax.ppermute(item, axis, [(k, (k + step) % size) for k in range(size)])

    def core_step(self, item):
        return self.shift(item, "core")

    def y_step(self, item, step=1):
        return self.shift(item, "y", step)

    def broadcast(self, item, axes):
        copies = jnp.broadcast_to(item, (lax.axis_size(axes), *item.shape))
        return lax.all_to_all(copies, axes, 0, 0)

    def spread_x(self, part):
        return [self.shift(part, "x", step) for step in range(self.wide)]

    def ring_x(self, held, moving):
        return [old + self.spread_x(item) for old, item in zip(held, moving, strict=True)]

    def ring_z(self, moving):
        return tuple(self.shift(item, "z") for item in moving)

    def near_dp(self):
        return [
            (self.y - far) % self.rows * self.cores + (self.core - core) % self.cores
            for far in range(self.rows)
            for core in range(self.cores)
        ]

    def near_ctx(self):
        return [
            (self.z - back) % self.deep * self.wide + (self.x - across) % self.wide
            for back in range(self.deep)
            for across in range(self.wide)
        ]

    def scatter_near(self, parts):
        return jnp.sum(lax.all_to_all(parts, ("z", "x"), 0, 0).astype(jnp.float32), axis=0)

    def sum_x(self, parts):
        total = parts[0].astype(jnp.float32)
        for across in range(1, self.wide):
            total = total + self.shift(parts[across], "x", -across).astype(jnp.float32)
        return total

    def gather_y(self, item):
        return jnp.stack([item] + [self.y_step(item, step) for step in range(1, self.rows)])

    def scatter_core(self, whole):
        return whole[0].astype(jnp.float32) + self.core_step(whole[1]).astype(jnp.float32)

    def scatter_y(self, pair, low):
        total = pair[0]
        for step in range(1, self.rows):
            total = total + self.y_step(pair[step].astype(low), -step).astype(jnp.float32)
        return total

    def exchange_dp(self, whole):
        came = []
        for far in range(self.rows):
            for core in range(self.cores):
                to_y, to_core = (self.y + far) % self.rows, (self.core + core) % self.cores
                part = lax.dynamic_index_in_dim(whole, to_y * self.cores + to_core, 0, False)
                size = self.dp
                pairs = []
                for k in range(size):
                    there = (k // self.cores + far) % self.rows * self.cores
                    pairs.append((k, there + (k + core) % self.cores))
                came.append(lax.ppermute(part, ("y", "core"), pairs) if far or core else part)
        return came

    def hand_back(self, parts):
        came = []
        for far in range(self.rows):
            for core in range(self.cores):
                pairs = []
                for k in range(self.dp):
                    there = (k // self.cores - far) % self.rows * self.cores
                    pairs.append((k, there + (k - core) % self.cores))
                part = parts[far * self.cores + core]
                came.append(lax.ppermute(part, ("y", "core"), pairs) if far or core else part)
        came = jnp.stack(came)
        order = [
            (dp // self.cores - self.y) % self.rows * self.cores + (dp - self.core) % self.cores
            for dp in range(self.dp)
        ]
        return [lax.dynamic_index_in_dim(came, k, 0, False) for k in order]

    def sum_dp(self, item):
        for axis in ("core", "y"):
            step, size = 1, lax.axis_size(axis)
            while step < size:
                pairs = [(k, k ^ step) for k in range(size)]
                item = item + lax.ppermute(item, axis, pairs)
                step *= 2
        return item


def allowed_bias(slot_ref, low_ref, first_ref, bias_ref):
    tokens = bias_ref.shape[1]
    query = first_ref[0] + lax.broadcasted_iota(jnp.int32, (tokens, tokens), 1)
    for slot in range(bias_ref.shape[0] // tokens):
        keys = slot_ref[slot] * tokens + lax.broadcasted_iota(jnp.int32, (tokens, tokens), 0)
        allowed = (keys >= low_ref[...]) & (keys <= query)
        bias_ref[slot * tokens : (slot + 1) * tokens, :] = jnp.where(allowed, 0.0, NEGATIVE)


def head_rows(ref, head):
    return ref[head * HEAD_SIZE : (head + 1) * HEAD_SIZE, :]


def attention_kernel(slot_ref, first_ref, low_ref, q_ref, kv_ref, att_ref, stat_ref, bias_ref):
    allowed_bias(slot_ref, low_ref, first_ref, bias_ref)
    kv_cols = jnp.concatenate([kv_ref[j] for j in range(kv_ref.shape[0])], axis=1)
    groups = QUERY_HEADS // KEY_VALUE_HEADS
    half = KEY_VALUE_HEADS * HEAD_SIZE
    key_rows = kv_cols[:half].T
    for kv_head in range(KEY_VALUE_HEADS):
        key = key_rows[:, kv_head * HEAD_SIZE : (kv_head + 1) * HEAD_SIZE]
        value = kv_cols[half + kv_head * HEAD_SIZE : half + (kv_head + 1) * HEAD_SIZE]
        for head in range(kv_head * groups, (kv_head + 1) * groups):
            score = jnp.dot(key, head_rows(q_ref, head), preferred_element_type=jnp.float32)
            score = score * HEAD_SIZE ** (-0.5) + bias_ref[...]
            top = jnp.max(score, axis=0, keepdims=True)
            weights = jnp.exp(score - top)
            total = jnp.sum(weights, axis=0, keepdims=True)
            out = jnp.dot(value, weights.astype(jnp.bfloat16), preferred_element_type=jnp.float32)
            att_ref[head * HEAD_SIZE : (head + 1) * HEAD_SIZE, :] = out / total
            stat_ref[head : head + 1, :] = top + jnp.log(total)


def attention_back_kernel(
    slot_ref,
    first_ref,
    low_ref,
    q_ref,
    kv_ref,
    att_ref,
    stat_ref,
    datt_ref,
    dq_ref,
    dkv_ref,
    bias_ref,
    qs_ref,
    das_ref,
    ds_ref,
    p_ref,
):
    allowed_bias(slot_ref, low_ref, first_ref, bias_ref)
    kv_cols = jnp.concatenate([kv_ref[j] for j in range(kv_ref.shape[0])], axis=1)
    tokens = q_ref.shape[1]
    groups = QUERY_HEADS // KEY_VALUE_HEADS
    half = KEY_VALUE_HEADS * HEAD_SIZE
    scale = HEAD_SIZE ** (-0.5)
    rows = kv_cols.T
    results = []
    for kv_head in range(KEY_VALUE_HEADS):
        own = slice(kv_head * HEAD_SIZE, (kv_head + 1) * HEAD_SIZE)
        key = rows[:, own]
        value = rows[:, half + kv_head * HEAD_SIZE : half + (kv_head + 1) * HEAD_SIZE]
        key_cols = kv_cols[own]
        for place in range(groups):
            head = kv_head * groups + place
            lanes = slice(place * tokens, (place + 1) * tokens)
            query = head_rows(q_ref, head)
            datt = head_rows(datt_ref, head)
            qs_ref[:, lanes] = query
            das_ref[:, lanes] = datt
            delta = jnp.sum(
                datt.astype(jnp.float32) * head_rows(att_ref, head), axis=0, keepdims=True
            )
            score = jnp.dot(key, query, preferred_element_type=jnp.float32)
            prob = jnp.exp(score * scale + bias_ref[...] - stat_ref[head : head + 1, :])
            dprob = jnp.dot(value, datt, preferred_element_type=jnp.float32)
            dscore = (prob * (dprob - delta)).astype(jnp.bfloat16)
            ds_ref[:, lanes] = dscore
            p_ref[:, lanes] = prob.astype(jnp.bfloat16)
            dq_ref[head * HEAD_SIZE : (head + 1) * HEAD_SIZE, :] = (
                jnp.dot(key_cols, dscore, preferred_element_type=jnp.float32) * scale
            )
        results.append(
            lax.dot_general(
                ds_ref[...], qs_ref[...], CONTRACT_COLS, preferred_element_type=jnp.float32
            )
            * scale
        )
        results.append(
            lax.dot_general(
                p_ref[...], das_ref[...], CONTRACT_COLS, preferred_element_type=jnp.float32
            )
        )
    order = results[0::2] + results[1::2]
    out = jnp.concatenate(order, axis=1).astype(jnp.bfloat16)
    for j in range(dkv_ref.shape[0]):
        dkv_ref[j] = out[j * tokens : (j + 1) * tokens]


def attention_specs(width, pieces, kv_width, tokens):
    smem = pl.BlockSpec(memory_space=pltpu.SMEM)
    low = pl.BlockSpec((pl.Squeezed(), 1, tokens), lambda mb: (mb, 0, 0))
    cols = pl.BlockSpec((width, tokens), lambda mb: (0, mb))
    kv = pl.BlockSpec((pieces, kv_width, tokens), lambda mb: (0, 0, mb))
    stat = pl.BlockSpec((QUERY_HEADS, tokens), lambda mb: (0, mb))
    return smem, low, cols, kv, stat


def attend(slots, first, low, q_cols, kv_all, batches):
    width, total = q_cols.shape
    tokens = total // batches
    pieces, kv_width, _ = kv_all.shape
    smem, low_spec, cols, kv, stat = attention_specs(width, pieces, kv_width, tokens)
    return pl.pallas_call(
        attention_kernel,
        grid=(batches,),
        in_specs=[smem, smem, low_spec, cols, kv],
        out_specs=[cols, stat],
        out_shape=[
            jax.ShapeDtypeStruct((width, total), jnp.float32),
            jax.ShapeDtypeStruct((QUERY_HEADS, total), jnp.float32),
        ],
        scratch_shapes=[pltpu.VMEM((pieces * tokens, tokens), jnp.float32)],
        compiler_params=pltpu.CompilerParams(vmem_limit_bytes=40 * 2**20),
        cost_estimate=pl.CostEstimate(
            flops=4 * total * pieces * tokens * width,
            bytes_accessed=8 * total * width,
            transcendentals=total * pieces * tokens * QUERY_HEADS,
        ),
        name="attention",
    )(slots, first, low, q_cols, kv_all)


def attend_back(slots, first, low, q_cols, kv_all, att_cols, stats, datt_cols, batches):
    width, total = q_cols.shape
    tokens = total // batches
    pieces, kv_width, _ = kv_all.shape
    groups = QUERY_HEADS // KEY_VALUE_HEADS
    keys = pieces * tokens
    smem, low_spec, cols, kv, stat = attention_specs(width, pieces, kv_width, tokens)
    return pl.pallas_call(
        attention_back_kernel,
        grid=(batches,),
        in_specs=[smem, smem, low_spec, cols, kv, cols, stat, cols],
        out_specs=[
            cols,
            pl.BlockSpec((pieces, pl.Squeezed(), tokens, kv_width), lambda mb: (0, mb, 0, 0)),
        ],
        out_shape=[
            jax.ShapeDtypeStruct((width, total), jnp.float32),
            jax.ShapeDtypeStruct((pieces, batches, tokens, kv_width), jnp.bfloat16),
        ],
        scratch_shapes=[
            pltpu.VMEM((keys, tokens), jnp.float32),
            pltpu.VMEM((HEAD_SIZE, groups * tokens), jnp.bfloat16),
            pltpu.VMEM((HEAD_SIZE, groups * tokens), jnp.bfloat16),
            pltpu.VMEM((keys, groups * tokens), jnp.bfloat16),
            pltpu.VMEM((keys, groups * tokens), jnp.bfloat16),
        ],
        compiler_params=pltpu.CompilerParams(vmem_limit_bytes=48 * 2**20),
        cost_estimate=pl.CostEstimate(
            flops=10 * total * keys * width,
            bytes_accessed=14 * total * width,
            transcendentals=total * keys * QUERY_HEADS,
        ),
        name="attention_back",
    )(slots, first, low, q_cols, kv_all, att_cols, stats, datt_cols)


def forward_kernel(
    near_ref,
    far_ref,
    near_dy_ref,
    far_dy_ref,
    gate_up_ref,
    down_ref,
    pick_ref,
    hidden_ref,
    act_ref,
    dgu_ref,
    dhidden_ref,
):
    first = pl.program_id(0) < pl.num_programs(0) // 2
    hidden = jnp.where(first, near_ref[...], far_ref[...])
    dy = jnp.where(first, near_dy_ref[...], far_dy_ref[...])
    hidden = dot32(hidden, pick_ref[...]).astype(jnp.bfloat16)
    hidden_ref[...] = hidden
    own_ff = down_ref.shape[0]
    gate_up = dot32(hidden, gate_up_ref[...])
    gate, up = gate_up[:, :own_ff], gate_up[:, own_ff:]
    sigmoid = jax.nn.sigmoid(gate)
    silu = gate * sigmoid
    act_ref[...] = (silu * up).astype(jnp.bfloat16)
    dact = dot32(dy, down_ref[...], CONTRACT_COLS)
    dgate = dact * up * sigmoid * (1.0 + gate * (1.0 - sigmoid))
    dgu = jnp.concatenate([dgate, dact * silu], axis=1).astype(jnp.bfloat16)
    dgu_ref[...] = dgu
    dhidden = dot32(dgu, gate_up_ref[...], CONTRACT_COLS).astype(jnp.bfloat16)
    dhidden_ref[...] = dot32(dhidden, pick_ref[...], CONTRACT_COLS).astype(jnp.bfloat16)


def feed_forward(hidden, dy, w_gate_up, w_down, pick, tile):
    half, width = hidden[0].shape
    own_ff = w_down.shape[0]
    steps = half // tile
    near = pl.BlockSpec((tile, width), lambda i: (jnp.minimum(i, steps - 1), 0))
    far = pl.BlockSpec((tile, width), lambda i: (jnp.maximum(i - steps, 0), 0))

    def whole(item):
        return pl.BlockSpec(item.shape, lambda i: (0, 0), pipeline_mode=pl.Buffered(1))

    def rows(columns):
        return pl.BlockSpec((tile, columns), lambda i: (i, 0))

    widths = (width, own_ff, 2 * own_ff, width)
    return pl.pallas_call(
        forward_kernel,
        grid=(2 * steps,),
        in_specs=[near, far, near, far, whole(w_gate_up), whole(w_down), whole(pick)],
        out_specs=[rows(columns) for columns in widths],
        out_shape=[jax.ShapeDtypeStruct((2 * half, columns), jnp.bfloat16) for columns in widths],
        compiler_params=pltpu.CompilerParams(vmem_limit_bytes=48 * 2**20),
        cost_estimate=pl.CostEstimate(
            flops=4 * half * width * (5 * own_ff + 2 * width),
            bytes_accessed=8 * half * (2 * width + 2 * own_ff) + 6 * width * own_ff,
            transcendentals=2 * half * own_ff,
        ),
        name="feed_forward",
    )(*hidden, *dy, w_gate_up, w_down, pick)


def one_hot_order(order, size):
    rows = lax.broadcasted_iota(jnp.int32, (size, order.shape[0]), 0)
    return (rows == order[None, :]).astype(jnp.bfloat16)


def dot32(left, right, dims=(((1,), (0,)), ((), ()))):
    return lax.dot_general(left, right, dims, preferred_element_type=jnp.float32)


def rope_columns(cols, cosine, sine):
    first, second = cols[:, 0], cols[:, 1]
    return jnp.stack([first * cosine - second * sine, second * cosine + first * sine], axis=1)


def rope_columns_back(cols, cosine, sine):
    first, second = cols[:, 0], cols[:, 1]
    return jnp.stack([first * cosine + second * sine, second * cosine - first * sine], axis=1)


def short_body(
    tokens,
    doc_lengths,
    attn_gain,
    qkv_weight,
    qkv_bias,
    out_weight,
    mlp_gain,
    gate_up_weight,
    down_weight,
    out_grad,
):
    links = Links()
    width = attn_gain.shape[0]
    qkv_width = qkv_bias.shape[0]
    query_width = QUERY_HEADS * HEAD_SIZE
    kv_width = KEY_VALUE_HEADS * HEAD_SIZE
    half = HEAD_SIZE // 2
    batches, token_count = tokens.shape[0], tokens.shape[2]
    total = batches * token_count
    devices = links.dp * links.ctx
    piece = width // devices
    own_ff = FF // links.dp
    first_row = links.me_ctx * token_count

    padded = -(-piece // 16) * 16
    key_slots = jnp.stack(
        [
            z * links.wide + (links.x - across) % links.wide
            for across in range(links.wide)
            for z in range(links.deep)
        ]
    ).astype(jnp.int32)
    row = jnp.arange(padded, dtype=jnp.int32)
    near_dp = jnp.stack(links.near_dp()).astype(jnp.int32)
    near_ctx = jnp.stack(links.near_ctx()).astype(jnp.int32)
    rows_order = near_dp.reshape(links.rows, 2).T.reshape(-1)
    owner = rows_order[:, None] * links.ctx + jnp.arange(links.ctx, dtype=jnp.int32)[None, :]
    attn_order = jnp.where(row < piece, owner[:, :, None] * piece + row, -1).reshape(-1)
    attn_pick = one_hot_order(attn_order, width)
    owner = near_dp[None, :] * links.ctx + near_ctx[:, None]
    mlp_order = (owner[:, :, None] * piece + jnp.arange(piece, dtype=jnp.int32)).reshape(-1)
    mlp_pick = one_hot_order(mlp_order, width)

    def own_rows(flat, columns):
        return jnp.pad(flat.reshape(piece, columns), ((0, padded - piece), (0, 0)))

    def rows_y(near):
        return jnp.concatenate([near] + [links.y_step(near, k) for k in range(1, links.rows)])

    def rows_core(held):
        return jnp.concatenate([held, links.core_step(held)])

    def back_core(grad):
        mine, other = jnp.split(grad, 2)
        return mine.astype(jnp.float32) + links.core_step(other).astype(jnp.float32)

    def back_y(pair):
        parts = jnp.split(pair, links.rows)
        total = parts[0]
        for step in range(1, links.rows):
            there = links.y_step(parts[step].astype(jnp.bfloat16), -step)
            total = total + there.astype(jnp.float32)
        return total.astype(jnp.bfloat16).reshape(links.ctx, padded, -1)

    w_qkv = links.broadcast(own_rows(qkv_weight, qkv_width), ("z", "x")).reshape(-1, qkv_width)
    gate_up_rows = gate_up_weight.reshape(piece, 2, links.dp, own_ff)
    gate_up_rows = gate_up_rows.transpose(2, 0, 1, 3).reshape(links.dp, piece, 2 * own_ff)
    parts = links.exchange_dp(gate_up_rows)
    all_cotangent = links.gather_y(out_grad[:, 0].reshape(total, width))
    w_qkv, all_cotangent, down_part, *parts = together(
        w_qkv, all_cotangent, down_weight.reshape(-1, width), *parts
    )

    w_qkv = rows_y(w_qkv)
    moving = (
        jnp.stack(parts).reshape(links.dp * piece, 2 * own_ff),
        down_part,
    )
    held = links.ring_x([[], []], moving)
    moving = links.ring_z(moving)
    w_out = links.broadcast(own_rows(out_weight, width), ("z", "x")).reshape(-1, width)
    w_qkv = rows_core(w_qkv)

    cotangent = out_grad[:, 0].reshape(total, width)

    inputs = tokens[:, 0].reshape(total, width).astype(jnp.float32)
    layouts = [doc_layout(doc_lengths[b, 0], first_row, token_count) for b in range(batches)]
    token_index = layouts[0][0]
    positions = jnp.concatenate([item[2] for item in layouts])
    low = jnp.stack([token_index - item[2] for item in layouts])[:, None, :]
    first = jnp.reshape(first_row, (1,)).astype(jnp.int32)
    freqs = ROPE_THETA ** (-(2.0 * jnp.arange(half, dtype=jnp.float32)) / HEAD_SIZE)
    angles = freqs[:, None] * positions.astype(jnp.float32)[None, :]
    cosine, sine = jnp.cos(angles), jnp.sin(angles)

    normed1, scale1, hidden1 = rms_forward(inputs, attn_gain)
    hidden1 = dot32(hidden1.astype(jnp.bfloat16), attn_pick).astype(jnp.bfloat16)
    qkv_cols = dot32(w_qkv, hidden1, (((0,), (1,)), ((), ()))) + qkv_bias[:, None]
    turned = rope_columns(
        qkv_cols[: query_width + kv_width].reshape(-1, 2, half, total), cosine, sine
    )
    turned = turned.reshape(query_width + kv_width, total).astype(jnp.bfloat16)
    q_cols = turned[:query_width]
    kv_cols = jnp.concatenate(
        [turned[query_width:], qkv_cols[query_width + kv_width :].astype(jnp.bfloat16)]
    )
    kv_all = links.broadcast(kv_cols, "z")
    moving, _ = together(moving, kv_cols)
    held = links.ring_x(held, moving)
    kv_all, w_out, moving = together(kv_all, w_out, moving)

    kv_all = jnp.concatenate(links.spread_x(kv_all))
    w_out = rows_y(w_out)
    for step in range(2, links.deep - 1):
        moving = links.ring_z(moving)
        if step > 2:
            held = links.ring_x(held, moving)
    moving, _ = together(moving, kv_all)
    kv_all, w_out, cotangent = together(kv_all, w_out, cotangent)

    w_out = rows_core(w_out)
    held = links.ring_x(held, moving)
    moving = links.ring_z(moving)
    att_cols, stats = attend(key_slots, first, low, q_cols, kv_all, batches)
    att_cols, w_out, all_cotangent = together(att_cols, w_out, all_cotangent)

    att_low = dot32(
        att_cols.astype(jnp.bfloat16), attn_pick, (((0,), (0,)), ((), ()))
    ).astype(jnp.bfloat16)
    residual = inputs + dot32(att_low, w_out)

    normed2, scale2, hidden2 = rms_forward(residual, mlp_gain)
    hidden2 = hidden2.astype(jnp.bfloat16)
    near_hidden2 = links.gather_y(hidden2).reshape(-1, width)
    moving, _ = together(moving, hidden2)
    w_parts, down_parts = links.ring_x(held, moving)
    w_gate_up = jnp.concatenate(w_parts)
    w_down = jnp.zeros((links.ctx, own_ff // links.ctx, width), jnp.bfloat16)
    for k, part in enumerate(down_parts):
        w_down = lax.dynamic_update_index_in_dim(w_down, part, near_ctx[k], 0)
    w_down = w_down.reshape(own_ff, width)
    near_dy = all_cotangent.reshape(-1, width)
    far_dy = links.core_step(near_dy)
    near_hidden2, far_dy, w_gate_up, w_down = together(near_hidden2, far_dy, w_gate_up, w_down)
    far_hidden2 = links.core_step(near_hidden2)
    all_hidden2, act_low, dgu, dhidden2 = feed_forward(
        (near_hidden2, far_hidden2), (near_dy, far_dy), w_gate_up, w_down, mlp_pick, total
    )
    all_cotangent = jnp.concatenate([near_dy, far_dy])
    dhidden2 = links.scatter_core(dhidden2.reshape(2, links.rows, total, width))
    dhidden2, dgu, act_low = together(dhidden2, dgu, act_low)

    grad_gate_up = dot32(all_hidden2, dgu, CONTRACT_ROWS).astype(jnp.bfloat16)
    grad_down = dot32(act_low, all_cotangent, CONTRACT_ROWS).astype(jnp.bfloat16)
    grad_gate_up, grad_down, act_low = together(grad_gate_up, grad_down, act_low)

    blocks = grad_gate_up.reshape(links.deep, links.wide, -1, 2 * own_ff)
    down_blocks = grad_down.reshape(links.ctx, own_ff // links.ctx, width)

    def across(blocks, back):
        gate_up_blocks, down_blocks = blocks
        places = [near_ctx[back * links.wide + step] for step in range(links.wide)]
        down = [lax.dynamic_index_in_dim(down_blocks, k, 0, False) for k in places]
        return links.sum_x(gate_up_blocks[back]), links.sum_x(down)

    def lowered(share):
        return [item.astype(jnp.bfloat16) for item in share]

    def plus(share, moved):
        return tuple(a + b.astype(jnp.float32) for a, b in zip(share, moved, strict=True))

    def ring(share, other):
        return plus(other, links.ring_z(lowered(share)))

    blocks = (blocks, down_blocks)
    share = across(blocks, 1)
    dhidden2 = links.scatter_y(dhidden2, jnp.bfloat16)
    out_part = dot32(act_low, w_down).astype(jnp.bfloat16)

    back_mlp, gain2_grad = rms_backward(dhidden2, normed2, scale2, mlp_gain)
    dmid = cotangent.astype(jnp.float32) + back_mlp
    dmid_low = dmid.astype(jnp.bfloat16)
    datt = dot32(dmid_low, w_out, CONTRACT_COLS).astype(jnp.bfloat16)
    datt_cols = dot32(attn_pick, datt, CONTRACT_COLS).astype(jnp.bfloat16)
    grad_out = dot32(att_low, dmid_low, CONTRACT_ROWS).astype(jnp.bfloat16)
    share, blocks, datt_cols, out_part = together(share, blocks, datt_cols, out_part)
    share = ring(share, across(blocks, 2))
    out_part = links.scatter_core(out_part.reshape(2, links.rows, total, width))
    grad_out = back_core(grad_out)
    dq_cols, dkv = attend_back(
        key_slots, first, low, q_cols, kv_all, att_cols, stats, datt_cols, batches
    )
    dq_cols, dkv, share, blocks, grad_out, out_part = together(
        dq_cols, dkv, share, blocks, grad_out, out_part
    )

    dkv = dkv.reshape(links.wide, links.deep, total, 2 * kv_width)
    dkv = links.sum_x(dkv).astype(jnp.bfloat16)
    for back in range(3, links.deep - 1):
        share = ring(share, across(blocks, back))
    share = links.ring_z(lowered(share))
    dkv, blocks, out_part = together(dkv, blocks, out_part)

    layer_out = residual + links.scatter_y(out_part, jnp.bfloat16)
    own_dkv = lax.all_to_all(dkv, "z", 0, 0)
    own_dkv, share = together(own_dkv, share)
    own_dkv = jnp.sum(own_dkv.astype(jnp.float32), axis=0).T
    share = plus(across(blocks, links.deep - 1), share)
    dq = rope_columns_back(dq_cols.reshape(-1, 2, half, total), cosine, sine)
    dq = dq.reshape(query_width, total).astype(jnp.bfloat16)
    grad_q = back_core(dot32(hidden1, dq, (((0,), (1,)), ((), ()))).astype(jnp.bfloat16))
    grad_out = back_y(grad_out)
    grad_q, grad_out = together(grad_q, grad_out)

    grad_q = jnp.concatenate([back_y(grad_q), grad_out], axis=2)
    share, blocks, grad_q = together(share, blocks, grad_q)
    share = ring(share, across(blocks, 0))
    dk = rope_columns_back(own_dkv[:kv_width].reshape(-1, 2, half, total), cosine, sine)
    dkv = jnp.concatenate([dk.reshape(kv_width, total), own_dkv[kv_width:]]).astype(jnp.bfloat16)
    grad_kv = dot32(hidden1, dkv, (((0,), (1,)), ((), ()))).astype(jnp.bfloat16)
    grad_kv = back_y(back_core(grad_kv))
    dqkv = jnp.concatenate([dq, dkv])
    bias_grad = jnp.sum(dqkv.astype(jnp.float32), axis=1)
    dhidden1 = dot32(dqkv, w_qkv, (((0,), (1,)), ((), ())))
    (top,) = together(dhidden1.astype(jnp.bfloat16))
    rest = (dhidden1 - top.astype(jnp.float32)).astype(jnp.bfloat16)
    dhidden1 = dot32(top, attn_pick, CONTRACT_COLS) + dot32(rest, attn_pick, CONTRACT_COLS)
    back_attn, gain1_grad = rms_backward(dhidden1, normed1, scale1, attn_gain)
    input_grad = dmid + back_attn
    small = links.sum_dp(jnp.concatenate([gain1_grad, bias_grad, gain2_grad]).reshape(-1, 128))
    (high,) = together(small.astype(jnp.bfloat16))
    rest = (small - high.astype(jnp.float32)).astype(jnp.bfloat16)
    sums = jnp.concatenate([high, rest]).reshape(-1)
    grads = jnp.concatenate([grad_q, grad_kv], axis=2)
    columns = grads.shape[2]
    sums = jnp.pad(sums, (0, (padded - piece) * columns - sums.size)).reshape(-1, columns)
    grads = links.scatter_near(grads + jnp.pad(sums, ((piece, 0), (0, 0))))
    share, down_share = share
    parts = share.astype(jnp.bfloat16).reshape(links.dp, piece, 2 * own_ff)
    parts = jnp.stack(links.hand_back(parts)).reshape(links.dp, piece, 2, own_ff)

    gate_up_share = parts.transpose(1, 2, 0, 3).astype(jnp.float32).reshape(-1)
    small = grads[piece:].reshape(-1)[: 2 * small.size].reshape(2, -1).sum(axis=0)
    grad_q, grad_out, grad_kv = jnp.split(grads[:piece], (query_width, query_width + width), axis=1)
    qkv_share = jnp.concatenate([grad_q, grad_kv], axis=1).reshape(-1)
    out_share = grad_out.reshape(-1)
    return (
        layer_out.astype(jnp.bfloat16).reshape(batches, 1, token_count, width),
        input_grad.reshape(batches, 1, token_count, width),
        small[:width],
        qkv_share,
        small[width : width + qkv_width],
        out_share,
        small[width + qkv_width :],
        gate_up_share,
        down_share.reshape(-1),
    )


def fits(mesh):
    dp, ctx = mesh.shape["dp"], mesh.shape["ctx"]
    devices = dp * ctx
    if dp % 2 or ctx % (dp // 2) or ctx // (dp // 2) < 3:
        return False
    piece = WIDTH // devices
    spare = (-piece % 16) * 2 * (WIDTH + KEY_VALUE_HEADS * HEAD_SIZE)
    sums = 2 * (3 * WIDTH + 2 * KEY_VALUE_HEADS * HEAD_SIZE)
    return WIDTH % devices == 0 and FF % devices == 0 and sums <= spare


def solution(mesh):
    run, dp, ctx = body, ("dp",), ("ctx",)
    if fits(mesh):
        rows = mesh.shape["dp"] // 2
        shape = (rows, 2, mesh.shape["ctx"] // rows, rows)
        run, dp, ctx = short_body, ("y", "core"), ("z", "x")
        mesh = Mesh(mesh.devices.reshape(shape), (*dp, *ctx))
    return jax.shard_map(
        run,
        mesh=mesh,
        in_specs=(
            P(None, dp, ctx, None),
            P(None, dp, None),
            P(),
            P((*dp, *ctx)),
            P(),
            P((*dp, *ctx)),
            P(),
            P((*dp, *ctx)),
            P((*dp, *ctx)),
            P(None, dp, ctx, None),
        ),
        out_specs=(
            P(None, dp, ctx, None),
            P(None, dp, ctx, None),
            P(),
            P((*dp, *ctx)),
            P(),
            P((*dp, *ctx)),
            P(),
            P((*dp, *ctx)),
            P((*dp, *ctx)),
        ),
        check_vma=False,
    )
```
